128 devices in a mesh: seg: 8 (over y, z_lo), blk: 16 (over z_hi, x, core).
Axes of the slice: x: 4, y: 4, z: 4 (z_hi: 2, z_lo: 2; z = z_hi * 2 + z_lo), core: 2. Of those that a mesh axis runs over, the one named last changes fastest.
Arguments:
- queries: bfloat16 [2048, 2048], P('blk'), may hold values from -8 to 8
- new_kv: bfloat16 [2048, 256], P('blk'), may hold values from -8 to 8
- cache_kv: bfloat16 [65536, 256], P(('seg', 'blk')), may hold values from -8 to 8
- cache_len: int32 [128], replicated, may hold values from 256 to 448
- page_owner: int32 [256, 1], replicated, may hold values from 0 to 127; in each aligned block of 256 rows (0 to 255, 256 to 511, ...) at most 8 rows name the same one
Outputs:
- attn_out: bfloat16 [2048, 2048], P('blk', 'seg')
- cache_out: bfloat16 [65536, 256], P(('seg', 'blk'))
The draws below stay inside these ranges and needn't reach their ends.
Inputs may be any that keep to these rules, and one draw needn't show every extreme that they name: `page_owner`: every device owns at least one page, no device owns more than 8 pages, and some device owns exactly 8.
All inputs are finite; a program needn't handle non-finite values.
Results may differ from the reference program's by a relative error of at most 0.018.
Values may be sent and summed in bfloat16 or wider, within the bound.
No kernel may reach another device: no remote copies, remote signals or barrier semaphores. Data moves between devices by JAX's collectives and lax.ppermute only.
A program may use at most 64 MiB of HBM per device.

```python
import math
import jax
import jax.numpy as jnp
import numpy as np
from jax import lax

HQ = 16
HD = 128
SLOTS = 512
PAGE = 8
STRETCH = 2048
PAGES = 256
MAXP = 8
CACHE_ROWS = 65536
N_SEG = 8
N_BLK = 16


def sign_pattern(key):
    sign_bits = jax.random.bernoulli(key, 0.5, (HD,))
    return jnp.where(sign_bits, 1.0, -1.0).astype(jnp.float32)


def plant_queries(drawn, signs, strengths):
    row_index = jnp.arange(STRETCH)[:, None]
    col_index = jnp.arange(HQ * HD)[None, :]
    head_index = col_index // HD
    for member in range(8):
        token_row = member * STRETCH // 8 + STRETCH // 16
        aligned = (row_index == token_row) & (head_index == 3 * member % HQ)
        drawn = jnp.where(aligned, strengths[member] * signs[col_index % HD], drawn)
    return drawn


def plant_keys(key_rows, signs, strengths, lowered):
    row_index = jnp.arange(CACHE_ROWS)[:, None]
    lane_index = jnp.arange(HD)[None, :]
    for member in range(4):
        first_row = member * CACHE_ROWS // 4 + SLOTS // 4
        strong = strengths[member] * signs[None, :]
        second = jnp.where(lane_index == 0, (strengths[member] - lowered) * signs[None, :], strong)
        key_rows = jnp.where(row_index == first_row, strong, key_rows)
        key_rows = jnp.where(row_index == first_row + 1, second, key_rows)
    return key_rows


def draw_queries(key, part):
    signs = sign_pattern(key)
    key = jax.random.fold_in(key, 11)
    drawn = jnp.clip(2.0 * jax.random.normal(key, (STRETCH, HQ * HD), jnp.float32), -8.0, 8.0)
    return plant_queries(drawn, signs, [2.5, 2.5, 2.5, 2.5, 2.5, 2.5, 2.5, 2.5]).astype(jnp.bfloat16)


def draw_cache_kv(key, part):
    signs = sign_pattern(key)
    key = jax.random.fold_in(key, 23)
    key_part, value_part, scale_part = jax.random.split(key, 3)
    value_scale = jnp.exp(jax.random.uniform(scale_part, (CACHE_ROWS, 1), jnp.float32, math.log(0.3), math.log(3.0)))
    key_rows = jnp.clip(1.5 * jax.random.normal(key_part, (CACHE_ROWS, HD), jnp.float32), -8.0, 8.0)
    value_rows = jnp.clip(jax.random.normal(value_part, (CACHE_ROWS, HD), jnp.float32), -8.0, 8.0)
    key_rows = plant_keys(key_rows, signs, [8.0, 5.0, 8.0, 6.0], 9.0)
    return jnp.concatenate([key_rows, jnp.clip(value_rows * value_scale, -8.0, 8.0)], axis=1).astype(jnp.bfloat16)


def with_ends(values, key, least, largest):
    longest = values.shape.index(max(values.shape))
    spots = []
    for shift in (0, 1):
        where = [jax.random.randint(jax.random.fold_in(key, axis), (), 0, length) for axis, length in enumerate(values.shape)]
        where[longest] = (where[longest] + shift) % values.shape[longest]
        spots.append(tuple(where))
    return values.at[spots[0]].set(least).at[spots[1]].set(largest)


def shard_levels(stream_key, extent, shards, smallest, high):
    def one(dim, shards_of):
        heights = jax.random.uniform(jax.random.fold_in(jax.random.fold_in(stream_key, 6), dim), (shards_of,), jnp.float32, smallest / len(shards), high / len(shards))
        return jnp.repeat(jnp.exp(heights), extent[dim] // shards_of).reshape((-1,) + (1,) * (len(extent) - dim - 1))

    gain = one(*shards[0])
    for cut in shards[1:]:
        gain = gain * one(*cut)
    return gain


def assign_block(own_key, own, number, rows, count, top, most, slope):
    order = jax.random.permutation(own_key, count)
    crowded, common = portions_of(count, rows * top, most, slope, True), portions_of(count, rows * top, most, slope, False)
    places = jnp.arange(count)

    def named(tallies, turn):
        used = int((tallies > 0).sum())
        fixed = max(1, used // 4)
        passed = fixed + (places - fixed + turn * (used - fixed)) % max(1, count - fixed)
        return jnp.zeros((count,), jnp.int32).at[order[jnp.where(places < fixed, places, passed)]].set(jnp.asarray(tallies, jnp.int32))

    tallies = jnp.where(number % 4 == 0, named(crowded, number // 4), named(common, number - number // 4 - 1))
    mixed = jax.random.permutation(jax.random.fold_in(own, 3), count)
    donor, taker = mixed[0:count // 2 * 2:2], mixed[1:count // 2 * 2:2]
    room = jnp.minimum(tallies[donor] - 1, most - tallies[taker]) // 2
    room = jnp.where((donor == order[0]) | (taker == order[0]) | (tallies[taker] == 0), 0, jnp.maximum(room, 0))
    passed = jax.random.randint(jax.random.fold_in(own, 4), (count // 2,), 0, 1 << 20) % (room + 1)
    tallies = tallies.at[donor].add(-passed).at[taker].add(passed)
    labels = jnp.searchsorted(jnp.cumsum(tallies), jnp.arange(rows * top), side="right").astype(jnp.int32)
    table = labels.reshape(top, rows).T
    table = table[jax.random.permutation(jax.random.fold_in(own, 1), rows)]
    turn = jax.random.randint(jax.random.fold_in(own, 2), (rows, 1), 0, top)
    return jnp.take_along_axis(table, (jnp.arange(top)[None, :] + turn) % top, axis=1)


def portions_of(count, total, most, lean, full):
    loads = [(1 << 20) // math.isqrt(rank ** lean) + 1 for rank in range(1, count + 1)]
    largest = most if full else min(most, max(-(-total // count), total * loads[0] // sum(loads)))
    least = 1 if total - largest >= count - 1 else 0
    counts, spare = [largest] + [least] * (count - 1), total - largest - least * (count - 1)
    while spare > 0:
        free = [i for i in range(1, count) if counts[i] < largest] or [i for i in range(1, count) if counts[i] < most]
        pool, remaining = sum([loads[i] for i in free]), spare
        for i in free:
            more = min(most - counts[i], max(1, remaining * loads[i] // pool), spare)
            counts[i] = counts[i] + more
            spare = spare - more
    return np.array(counts)


def centred(key, dims, spread, limit, cuts=(), kind=jnp.bfloat16):
    gain = shard_levels(key, dims, cuts, -0.22, 0.18) if cuts else 1.0
    values = jax.random.normal(key, dims, jnp.float32) * spread * gain
    return jnp.minimum(jnp.maximum(values, -limit), limit).astype(kind)


def setup_inputs(seed: int = 0) -> dict:
    keys = jax.random.split(jax.random.key(seed), 6)
    queries = draw_queries(jax.random.fold_in(keys[5], 71), 0)
    new_kv = centred(keys[1], (STRETCH, 2 * HD), 1.5, 8.0, ((0, 16),))
    cache_kv = draw_cache_kv(jax.random.fold_in(keys[5], 71), 0)
    cache_len = with_ends(jax.random.randint(keys[3], (N_SEG * N_BLK,), SLOTS // 2, SLOTS - PAGE * MAXP + 1), jax.random.fold_in(keys[3], 1), SLOTS // 2, SLOTS - PAGE * MAXP).astype(jnp.int32)
    page_owner_keys = jax.random.split(jax.random.fold_in(keys[4], 1), PAGES // PAGES)
    page_owner_turns = jax.random.permutation(jax.random.fold_in(keys[4], 3), PAGES // PAGES)
    page_owner = jax.vmap(lambda own, number: assign_block(jax.random.fold_in(keys[4], 2), own, number, PAGES, N_SEG * N_BLK, 1, MAXP, 2))(page_owner_keys, page_owner_turns).reshape((PAGES, 1))
    return dict(queries=queries, new_kv=new_kv, cache_kv=cache_kv, cache_len=cache_len, page_owner=page_owner)


neg_large = -1e+30

def slot_table(device, cache_len, page_owner, slot_count, page_rows, span_rows):
    owners = page_owner[:, 0]
    page_total = owners.shape[0]
    owned_mask = (owners == device).astype(jnp.int32)
    earlier = jnp.cumsum(owned_mask) - owned_mask
    owned_count = jnp.sum(owned_mask)
    filled = cache_len[device]
    slot_ids = jnp.arange(slot_count, dtype=jnp.int32)
    offset = slot_ids - filled
    is_new = (offset >= 0) & (offset < page_rows * owned_count)
    wanted = offset // page_rows
    page_match = (owned_mask[None, :] == 1) & (earlier[None, :] == wanted[:, None])
    page_ids = jnp.arange(page_total, dtype=jnp.int32)
    page_of = lax.optimization_barrier(jnp.sum(jnp.where(page_match, page_ids[None, :], 0), axis=1))
    source_row = jnp.where(is_new, page_of * page_rows + offset % page_rows, 0).astype(jnp.int32)
    key_pos = jnp.where(slot_ids < filled, -1, jnp.where(is_new, source_row, span_rows)).astype(jnp.int32)
    return (source_row, key_pos, is_new)

def combine_parts(left, right):
    top_max = jnp.maximum(left[1], right[1])
    left_weight = jnp.exp(left[1] - top_max)
    right_weight = jnp.exp(right[1] - top_max)
    return (left[0] * left_weight[:, None] + right[0] * right_weight[:, None], top_max, left[2] * left_weight + right[2] * right_weight)

def reference(queries, new_kv, cache_kv, cache_len, page_owner):
    device_total = N_SEG * N_BLK
    caches = cache_kv.reshape(device_total, SLOTS, 2 * HD)

    def write(item):
        device, cache = item
        source_row, key_pos, is_new = slot_table(device, cache_len, page_owner, SLOTS, PAGE, STRETCH)
        return (jnp.where(is_new[:, None], jnp.take(new_kv, source_row, axis=0), cache), key_pos)
    new_caches, positions = lax.map(write, (jnp.arange(device_total, dtype=jnp.int32), caches))
    rows_q = queries.reshape(STRETCH * HQ, HD)
    q_pos = jnp.arange(STRETCH * HQ, dtype=jnp.int32) // HQ
    score_scale = 1.0 / math.sqrt(HD)

    def visit(carried, item):
        cache, key_pos = item
        key_rows = cache[:, :HD]
        value_rows = cache[:, HD:]
        scores = jnp.dot(rows_q, key_rows.T, preferred_element_type=jnp.float32) * score_scale
        visible = key_pos[None, :] <= q_pos[:, None]
        local_max = lax.optimization_barrier(jnp.max(jnp.where(visible, scores, neg_large), axis=1))
        weights = jnp.where(visible, jnp.exp(scores - local_max[:, None]), 0.0)
        local_sum = lax.optimization_barrier(jnp.sum(weights, axis=1))
        local_out = jnp.dot(weights.astype(jnp.bfloat16), value_rows, preferred_element_type=jnp.float32)
        return (combine_parts(carried, (local_out, local_max, local_sum)), None)
    start = (jnp.zeros((STRETCH * HQ, HD), jnp.float32), jnp.full((STRETCH * HQ,), neg_large, jnp.float32), jnp.zeros((STRETCH * HQ,), jnp.float32))
    (out_acc, row_max, row_sum), _ = lax.scan(visit, start, (new_caches, positions))
    attended = (out_acc / row_sum[:, None]).reshape(STRETCH, HQ * HD).astype(jnp.bfloat16)
    return (attended, new_caches.reshape(device_total * SLOTS, 2 * HD))
```

```python
import functools

import jax
import jax.numpy as jnp
from jax import lax
from jax.experimental import pallas as pl
from jax.experimental.pallas import tpu as pltpu
from jax.sharding import PartitionSpec as P


F32 = jnp.float32
BF16 = jnp.bfloat16
HEADS = 16
HD = 128
TOK = 128
ROWS = HEADS * TOK
SLOTS = 512
FILL = 448
PAGE = 8
NSEG = 8
NBLK = 16
SHARE = TOK // NSEG
CHUNK = 2 * HD + 16
ACC = HD + 16
NEG = -1e30
SCALE = 1.4426950408889634 / HD**0.5
VMEM = pl.BlockSpec(memory_space=pltpu.VMEM)
SMEM = pl.BlockSpec(memory_space=pltpu.SMEM)
AXES = ("seg", "blk")


def neighbours(dx=0, flip_z=False, flip_core=False):
    pairs = []
    for here in range(NSEG * NBLK):
        seg, blk = divmod(here, NBLK)
        pairs.append((here, device_at(seg, blk, dx, flip_z, flip_core)))
    return pairs


def device_at(seg, blk, dx, flip_z, flip_core):
    y, z_lo = seg // 2, seg % 2
    z_hi, x, core = blk // 8, (blk // 2) % 4, blk % 2
    if flip_z:
        z_lo, z_hi = 1 - z_lo, 1 - z_hi
    if flip_core:
        core = 1 - core
    x = (x + dx) % 4
    return (y * 2 + z_lo) * NBLK + z_hi * 8 + x * 2 + core


def origin(slot):
    return device_at(lax.axis_index("seg"), lax.axis_index("blk"), *slot)


def queries_kernel(q_ref, qt_ref):
    for h in range(HEADS):
        cols = slice(h * HD, (h + 1) * HD)
        scaled = q_ref[:, cols].astype(F32).T * SCALE
        high = scaled.astype(BF16)
        qt_ref[0:HD, cols] = high
        qt_ref[HD : 2 * HD, cols] = (scaled - high.astype(F32)).astype(BF16)


def flash_kernel(slots, first, last, width, *refs):
    count = len(slots)
    len_ref, qt_ref = refs[0], refs[1]
    blocks = refs[2 : 2 + count]
    at = 2 + count
    if last:
        fresh_ref = refs[at]
        at += 1
    if not first:
        m_in, acc_in = refs[at], refs[at + 1]
        at += 2
    if last:
        part_ref = refs[at]
        at += 1
    else:
        m_ref, acc_ref = refs[at], refs[at + 1]
        at += 2
    keys, vals, vals_t = refs[at:]
    total = keys.shape[0]
    for j, slot in enumerate(slots):
        filled = len_ref[origin(slot)]
        ok = lax.broadcasted_iota(jnp.int32, (FILL, HD), 0) < filled
        key = blocks[j][0:FILL, 0:HD]
        value = blocks[j][0:FILL, HD : 2 * HD]
        key = jnp.where(ok, key, jnp.broadcast_to(key[0:1], (FILL, HD)))
        rows = slice(j * FILL, (j + 1) * FILL)
        keys[rows, 0:HD] = key
        keys[rows, HD : 2 * HD] = key
        vals[rows, 0:HD] = jnp.where(ok, value, jnp.zeros_like(value))
        vals[rows, HD : 2 * HD] = ok.astype(BF16)
    tiles = [(j * FILL, FILL) for j in range(count)]
    if last:
        rows = slice(count * FILL, total)
        tiles.append((count * FILL, total - count * FILL))
        keys[rows, 0:HD] = fresh_ref[:, 0:HD]
        keys[rows, HD : 2 * HD] = fresh_ref[:, 0:HD]
        vals[rows, 0:HD] = fresh_ref[:, HD : 2 * HD]
        vals[rows, HD : 2 * HD] = jnp.ones((total - count * FILL, HD), BF16)
        seg = lax.axis_index("seg")
        shape = (NBLK * SHARE, width)
        key_id = lax.broadcasted_iota(jnp.int32, shape, 0)
        key_pos = key_id // SHARE * TOK + seg * SHARE + key_id % SHARE
        token = lax.axis_index("blk") * TOK + lax.broadcasted_iota(jnp.int32, shape, 1) % TOK
        seen = key_pos <= token
    for c in range(total // 128):
        rows = slice(c * 128, (c + 1) * 128)
        vals_t[0:HD, rows] = vals[rows, 0:HD].T
        vals_t[HD:ACC, rows] = vals[rows, HD : 2 * HD].T[0 : ACC - HD]
    for r in range(ROWS // width):
        cols = slice(r * width, (r + 1) * width)
        query = qt_ref[:, cols]
        scores = []
        top = None if first else m_in[0:1, cols]
        for start, size in tiles:
            s = jnp.dot(keys[start : start + size, :], query, preferred_element_type=F32)
            if start == count * FILL:
                s = jnp.where(seen, s, NEG)
            scores.append(s)
            tile_top = jnp.max(s, axis=0, keepdims=True)
            top = tile_top if top is None else jnp.maximum(top, tile_top)
        out = None if first else acc_in[:, cols] * jnp.exp2(m_in[0:1, cols] - top)
        for s, (start, size) in zip(scores, tiles):
            w = jnp.exp2(s - top).astype(BF16)
            term = jnp.dot(vals_t[:, start : start + size], w, preferred_element_type=F32)
            out = term if out is None else out + term
        if not last:
            acc_ref[:, cols] = out
            m_ref[:, cols] = jnp.broadcast_to(top, (8, width))
        else:
            total_w = out[HD : HD + 1]
            normal = (out[0:HD] * (1.0 / total_w)).astype(BF16)
            log_sum = top + jnp.log2(total_w)
            a = log_sum.astype(BF16)
            rest = log_sum - a.astype(F32)
            b = rest.astype(BF16)
            c = (rest - b.astype(F32)).astype(BF16)
            for i in range(width // TOK):
                head = r * (width // TOK) + i
                lanes = slice(i * TOK, (i + 1) * TOK)
                part_ref[head // 2, head % 2 * HD : (head % 2 + 1) * HD, :] = normal[:, lanes]
                stat = 2 * HD + head % 2 * 3
                part_ref[head // 2, stat : stat + 1, :] = a[:, lanes]
                part_ref[head // 2, stat + 1 : stat + 2, :] = b[:, lanes]
                part_ref[head // 2, stat + 2 : stat + 3, :] = c[:, lanes]


def flash(slots, cache_len, qt, blocks, state, fresh=None, width=512):
    first, last = state is None, fresh is not None
    total = len(slots) * FILL + (NBLK * SHARE if last else 0)
    operands = [cache_len, qt, *blocks]
    if last:
        operands.append(fresh)
    if not first:
        operands += list(state)
    if last:
        out_shape = jax.ShapeDtypeStruct((NSEG, CHUNK, TOK), BF16)
        out_specs = VMEM
    else:
        out_shape = [jax.ShapeDtypeStruct((8, ROWS), F32), jax.ShapeDtypeStruct((ACC, ROWS), F32)]
        out_specs = [VMEM, VMEM]
    return pl.pallas_call(
        functools.partial(flash_kernel, slots, first, last, width),
        in_specs=[SMEM] + [VMEM] * (len(operands) - 1),
        out_specs=out_specs,
        out_shape=out_shape,
        scratch_shapes=[
            pltpu.VMEM((total, 2 * HD), BF16),
            pltpu.VMEM((total, 2 * HD), BF16),
            pltpu.VMEM((ACC, total), BF16),
        ],
        compiler_params=pltpu.CompilerParams(vmem_limit_bytes=32 * 1024 * 1024),
        cost_estimate=pl.CostEstimate(
            flops=4 * total * ROWS * 256, bytes_accessed=1 << 20, transcendentals=total * ROWS
        ),
        name=f"flash_{len(slots)}",
    )(*operands)


def pages_kernel(slots, len_ref, owner_ref, cache_ref, *refs):
    blocks, out_ref, rows_ref = refs[: len(slots)], refs[-2], refs[-1]
    for block, slot in zip(blocks, slots):
        blk = origin(slot) % NBLK
        rows_ref[pl.ds(pl.multiple_of(blk * TOK, TOK), TOK), :] = block[FILL : FILL + TOK, :]
    device = lax.axis_index("seg") * NBLK + lax.axis_index("blk")
    filled = len_ref[device]
    pages = owner_ref.shape[0]
    new_rows = pages * PAGE
    owned = jnp.broadcast_to((owner_ref[...] == device).astype(F32), (pages, 128)).T[0:16].astype(BF16)
    before = (
        lax.broadcasted_iota(jnp.int32, (pages, pages), 0) < lax.broadcasted_iota(jnp.int32, (pages, pages), 1)
    ).astype(BF16)
    rank = jnp.dot(owned, before, preferred_element_type=F32)
    rank = jnp.where(owned > 0, rank, -1.0).astype(BF16)
    spread = (
        lax.broadcasted_iota(jnp.int32, (pages, new_rows), 1) // PAGE
        == lax.broadcasted_iota(jnp.int32, (pages, new_rows), 0)
    ).astype(BF16)
    row_rank = jnp.dot(rank, spread, preferred_element_type=F32)[0:1].astype(jnp.int32)
    target = filled + row_rank * PAGE + lax.broadcasted_iota(jnp.int32, (1, new_rows), 1) % PAGE
    target = jnp.where(row_rank >= 0, target, -1)
    half = SLOTS // 2
    pick = (lax.broadcasted_iota(jnp.int32, (half, new_rows), 0) + half == target).astype(BF16)
    written = jnp.dot(pick, rows_ref[...], preferred_element_type=F32).astype(BF16)
    count = jnp.max(row_rank) + 1
    slot_id = lax.broadcasted_iota(jnp.int32, (half, 2 * HD), 0) + half
    is_new = (slot_id >= filled) & (slot_id < filled + count * PAGE)
    out_ref[0:half, :] = cache_ref[0:half, :]
    out_ref[half:SLOTS, :] = jnp.where(is_new, written, cache_ref[half:SLOTS, :])


def write_pages(slots, cache_len, page_owner, cache_kv, blocks):
    return pl.pallas_call(
        functools.partial(pages_kernel, slots),
        in_specs=[SMEM] + [VMEM] * (2 + len(blocks)),
        out_specs=VMEM,
        out_shape=jax.ShapeDtypeStruct(cache_kv.shape, BF16),
        scratch_shapes=[pltpu.VMEM((NBLK * TOK, 2 * HD), BF16)],
        compiler_params=pltpu.CompilerParams(vmem_limit_bytes=32 * 1024 * 1024),
        cost_estimate=pl.CostEstimate(flops=10**9, bytes_accessed=4 << 20, transcendentals=0),
        name="write_pages",
    )(cache_len, page_owner, cache_kv, *blocks)


def fresh_kernel(slots, *refs):
    blocks, out_ref = refs[:-1], refs[-1]
    start = pl.multiple_of(FILL + lax.axis_index("seg") * SHARE, SHARE)
    for block, slot in zip(blocks, slots):
        blk = origin(slot) % NBLK
        out_ref[pl.ds(pl.multiple_of(blk * SHARE, SHARE), SHARE), :] = block[pl.ds(start, SHARE), :]


def fresh_share(slots, blocks):
    return pl.pallas_call(
        functools.partial(fresh_kernel, slots),
        in_specs=[VMEM] * len(blocks),
        out_specs=VMEM,
        out_shape=jax.ShapeDtypeStruct((NBLK * SHARE, 2 * HD), BF16),
        name="fresh_share",
    )(*blocks)


def merge_kernel(parts_ref, out_ref):
    for head in range(2):
        stat = 2 * HD + head * 3
        logs = []
        for s in range(NSEG):
            three = [parts_ref[s, stat + i : stat + i + 1, :].astype(F32) for i in range(3)]
            logs.append(three[0] + three[1] + three[2])
        top = functools.reduce(jnp.maximum, logs)
        weights = [jnp.exp2(v - top) for v in logs]
        scale = 1.0 / functools.reduce(jnp.add, weights)
        out = None
        for s in range(NSEG):
            term = parts_ref[s, head * HD : (head + 1) * HD, :].astype(F32) * (weights[s] * scale)
            out = term if out is None else out + term
        out_ref[:, head * HD : (head + 1) * HD] = out.T.astype(BF16)


def merge(parts):
    return pl.pallas_call(
        merge_kernel,
        in_specs=[VMEM],
        out_specs=VMEM,
        out_shape=jax.ShapeDtypeStruct((TOK, 2 * HD), BF16),
        name="merge",
    )(parts)


def swap(block):
    return lax.ppermute(block, AXES, neighbours(flip_core=True))


def on_device(queries, new_kv, cache_kv, cache_len, page_owner):
    own = jnp.concatenate([cache_kv[:FILL], new_kv], axis=0)
    held = {}
    held[0, False] = own
    held[1, False] = lax.ppermute(own, AXES, neighbours(-1))
    held[-1, False] = lax.ppermute(own, AXES, neighbours(1))
    held[0, True] = lax.ppermute(own, AXES, neighbours(0, True))
    held[2, False] = lax.ppermute(own, AXES, neighbours(2))
    held[1, True] = lax.ppermute(held[0, True], AXES, neighbours(-1))
    held[-1, True] = lax.ppermute(held[0, True], AXES, neighbours(1))
    held[2, True] = lax.ppermute(held[0, True], AXES, neighbours(2))
    full = {}
    for (dx, flip_z), block in held.items():
        full[dx, flip_z, False] = block
        full[dx, flip_z, True] = swap(block)
    rounds = [
        [(0, False)],
        [(1, False), (-1, False), (0, True)],
        [(2, False), (1, True), (-1, True)],
        [(2, True)],
    ]
    qt = pl.pallas_call(
        queries_kernel,
        in_specs=[VMEM],
        out_specs=VMEM,
        out_shape=jax.ShapeDtypeStruct((2 * HD, ROWS), BF16),
        name="scaled_queries",
    )(queries)
    all_slots = list(full)
    fresh = fresh_share(all_slots, [full[s] for s in all_slots])
    state = None
    for number, group in enumerate(rounds):
        slots = [(dx, flip_z, core) for dx, flip_z in group for core in (False, True)]
        state = flash(
            slots, cache_len, qt, [full[s] for s in slots], state, fresh if number == len(rounds) - 1 else None
        )
    parts = lax.all_to_all(state, "seg", 0, 0)
    cache_out = write_pages(all_slots, cache_len, page_owner, cache_kv, [full[s] for s in all_slots])
    return merge(parts), cache_out


def solution(mesh):
    placed = (P("blk", None), P("blk", None), P(("seg", "blk"), None), P(), P())
    return jax.shard_map(
        on_device,
        mesh=mesh,
        in_specs=placed,
        out_specs=(P("blk", "seg"), P(("seg", "blk"), None)),
        check_vma=False,
    )
```

```python
import functools

import jax
import jax.numpy as jnp
from jax import lax
from jax.experimental import pallas as pl
from jax.experimental.pallas import tpu as pltpu
from jax.sharding import PartitionSpec as P


F32 = jnp.float32
BF16 = jnp.bfloat16
HEADS = 16
HD = 128
TOK = 128
ROWS = 2 * HEADS * TOK
PART = HEADS * TOK
SLOTS = 512
FILL = 448
PAGE = 8
NSEG = 8
NBLK = 16
SHARE = TOK // NSEG
CHUNK = 2 * HD + 32
ACC = HD + 16
NEG = -1e30
SCALE = 1.4426950408889634 / HD**0.5
VMEM = pl.BlockSpec(memory_space=pltpu.VMEM)
SMEM = pl.BlockSpec(memory_space=pltpu.SMEM)
AXES = ("seg", "blk")


def neighbours(dx=0, flip_z=False, flip_core=False):
    pairs = []
    for here in range(NSEG * NBLK):
        seg, blk = divmod(here, NBLK)
        pairs.append((here, device_at(seg, blk, dx, flip_z, flip_core)))
    return pairs


def device_at(seg, blk, dx, flip_z, flip_core):
    y, z_lo = seg // 2, seg % 2
    z_hi, x, core = blk // 8, (blk // 2) % 4, blk % 2
    if flip_z:
        z_lo, z_hi = 1 - z_lo, 1 - z_hi
    if flip_core:
        core = 1 - core
    x = (x + dx) % 4
    return (y * 2 + z_lo) * NBLK + z_hi * 8 + x * 2 + core


def origin(slot):
    return device_at(lax.axis_index("seg"), lax.axis_index("blk"), *slot)


def queries_kernel(twin_ref, own_ref, qt_ref):
    for number, q_ref in enumerate((twin_ref, own_ref)):
        for h in range(HEADS):
            scaled = q_ref[:, h * HD : (h + 1) * HD].astype(F32).T * SCALE
            high = scaled.astype(BF16)
            cols = slice(number * PART + h * TOK, number * PART + (h + 1) * TOK)
            qt_ref[0:HD, cols] = high
            qt_ref[HD : 2 * HD, cols] = (scaled - high.astype(F32)).astype(BF16)


def in_hbm(array):
    return pltpu.with_memory_space_constraint(array, pltpu.HBM)


def pack_kernel(cache_ref, new_ref, out_ref, sems):
    copies = [
        pltpu.make_async_copy(cache_ref.at[0:FILL], out_ref.at[0:FILL], sems.at[0]),
        pltpu.make_async_copy(new_ref, out_ref.at[FILL : FILL + TOK], sems.at[1]),
    ]
    for copy in copies:
        copy.start()
    for copy in copies:
        copy.wait()


def pack(cache_kv, new_kv):
    return pl.pallas_call(
        pack_kernel,
        in_specs=[pl.BlockSpec(memory_space=pltpu.HBM)] * 2,
        out_specs=VMEM,
        out_shape=jax.ShapeDtypeStruct((FILL + TOK, 2 * HD), BF16),
        scratch_shapes=[pltpu.SemaphoreType.DMA((2,))],
        compiler_params=pltpu.CompilerParams(vmem_limit_bytes=1 << 20),
        name="pack",
    )(in_hbm(cache_kv), in_hbm(new_kv))


def flash_kernel(slots, operand_count, first, last, width, *refs):
    count = len(slots)
    len_ref, qt_ref = refs[0], refs[1]
    blocks = refs[2 : 2 + operand_count]
    at = 2 + operand_count
    if last:
        fresh_ref = refs[at]
        at += 1
    if not first:
        m_in, acc_in = refs[at], refs[at + 1]
        at += 2
    if last:
        part_refs = refs[at : at + 2]
        at += 2
    else:
        m_ref, acc_ref = refs[at], refs[at + 1]
        at += 2
    keys, vals, vals_t, scores_ref = refs[at:]
    total = keys.shape[0]
    old = count * FILL
    for j, (slot, pieces) in enumerate(slots):
        filled = len_ref[origin(slot)]
        valid = blocks[pieces[0][0]][pieces[0][1] : pieces[0][1] + 1, 0:HD]
        done = 0
        for which, start, stop in pieces:
            stop = min(stop, start + FILL - done)
            size = stop - start
            ok = lax.broadcasted_iota(jnp.int32, (size, HD), 0) + done < filled
            key = blocks[which][start:stop, 0:HD]
            value = blocks[which][start:stop, HD : 2 * HD]
            key = jnp.where(ok, key, jnp.broadcast_to(valid, (size, HD)))
            rows = slice(j * FILL + done, j * FILL + done + size)
            keys[rows, 0:HD] = key
            keys[rows, HD : 2 * HD] = key
            vals[rows, 0:HD] = jnp.where(ok, value, jnp.zeros_like(value))
            vals[rows, HD : 2 * HD] = ok.astype(BF16)
            done += size
    used = old
    if last:
        used = old + fresh_ref.shape[0]
        keys[old:used, 0:HD] = fresh_ref[:, 0:HD]
        keys[old:used, HD : 2 * HD] = fresh_ref[:, 0:HD]
        vals[old:used, 0:HD] = fresh_ref[:, HD : 2 * HD]
        vals[old:used, HD : 2 * HD] = jnp.ones((used - old, HD), BF16)
    if total > used:
        keys[used:total, :] = jnp.broadcast_to(keys[0:1, :], (total - used, 2 * HD))
        vals[used:total, :] = jnp.zeros((total - used, 2 * HD), BF16)
    for c in range(total // 128):
        rows = slice(c * 128, (c + 1) * 128)
        vals_t[0:HD, rows] = vals[rows, 0:HD].T
        vals_t[HD:ACC, rows] = vals[rows, HD : 2 * HD].T[0 : ACC - HD]

    def chunk(r):
        return pl.ds(pl.multiple_of(r * width, width), width)

    def score(r):
        s = jnp.dot(keys[...], qt_ref[:, chunk(r)], preferred_element_type=F32)
        if last:
            shape = (total - old, width)
            key_id = lax.broadcasted_iota(jnp.int32, shape, 0)
            blk = lax.axis_index("blk")
            key_blk = key_id // SHARE * 2 + blk % 2
            key_pos = key_blk * TOK + lax.axis_index("seg") * SHARE + key_id % SHARE
            query_blk = jnp.where(r < PART // width, blk + 1 - blk % 2 * 2, blk)
            token = query_blk * TOK + lax.broadcasted_iota(jnp.int32, shape, 1) % TOK
            fresh = jnp.where(key_pos <= token, s[old:total], NEG)
            scores_ref[0:old] = s[0:old]
            scores_ref[old:total] = fresh
            return jnp.maximum(column_max(s[0:old]), column_max(fresh))
        scores_ref[...] = s
        return column_max(s)

    def column_max(s):
        return jnp.max(s.reshape(s.shape[0] // 8, 8, width), axis=0)

    def weigh(r, tops, more, part_ref):
        cols = chunk(r)
        top = jnp.max(tops, axis=0, keepdims=True)
        if not first:
            top = jnp.maximum(top, m_in[0:1, cols])
        w = jnp.exp2(scores_ref[...] - top).astype(BF16)
        if more:
            tops = score(r + 1)
        out = jnp.dot(vals_t[...], w, preferred_element_type=F32)
        if not first:
            out = out + acc_in[:, cols] * jnp.exp2(m_in[0:1, cols] - top)
        if not last:
            acc_ref[:, cols] = out
            m_ref[:, cols] = jnp.broadcast_to(top, (8, width))
            return tops
        total_w = out[HD : HD + 1]
        normal = (out[0:HD] * (1.0 / total_w)).astype(BF16)
        stats = three_terms(top + jnp.log2(total_w))
        for i in range(width // TOK):
            head = r % (PART // width) * (width // TOK) + i
            lanes = slice(i * TOK, (i + 1) * TOK)
            part_ref[head // 2, pl.ds(pl.multiple_of(head % 2 * HD, HD), HD), :] = normal[:, lanes]
            part_ref[head // 2, pl.ds(pl.multiple_of(2 * HD + head % 2 * 16, 16), 16), :] = stats[:, lanes]
        return tops

    tops = score(0)
    if last:
        half = PART // width
        tops = lax.fori_loop(0, half, lambda r, tops: weigh(r, tops, True, part_refs[0]), tops)
        tops = lax.fori_loop(half, 2 * half - 1, lambda r, tops: weigh(r, tops, True, part_refs[1]), tops)
        weigh(2 * half - 1, tops, False, part_refs[1])
    else:
        tops = lax.fori_loop(0, ROWS // width - 1, lambda r, tops: weigh(r, tops, True, None), tops)
        weigh(ROWS // width - 1, tops, False, None)


def three_terms(row):
    high = row.astype(BF16)
    rest = row - high.astype(F32)
    middle = rest.astype(BF16)
    low = (rest - middle.astype(F32)).astype(BF16)
    return jnp.concatenate([high, middle, low] + [high] * 13, axis=0)


def flash(held, cache_len, qt, state, fresh=None, width=512):
    first, last = state is None, fresh is not None
    slots, blocks = indexed(held)
    total = len(slots) * FILL + (fresh.shape[0] if last else 0)
    total = -(-total // 128) * 128
    operands = [cache_len, qt, *blocks]
    if last:
        operands.append(fresh)
    if not first:
        operands += list(state)
    if last:
        out_shape = [jax.ShapeDtypeStruct((NSEG, CHUNK, TOK), BF16)] * 2
    else:
        out_shape = [jax.ShapeDtypeStruct((8, ROWS), F32), jax.ShapeDtypeStruct((ACC, ROWS), F32)]
    return pl.pallas_call(
        functools.partial(flash_kernel, slots, len(blocks), first, last, width),
        in_specs=[SMEM] + [VMEM] * (len(operands) - 1),
        out_specs=[VMEM, VMEM],
        out_shape=out_shape,
        scratch_shapes=[
            pltpu.VMEM((total, 2 * HD), BF16),
            pltpu.VMEM((total, 2 * HD), BF16),
            pltpu.VMEM((ACC, total), BF16),
            pltpu.VMEM((total, width), F32),
        ],
        compiler_params=pltpu.CompilerParams(vmem_limit_bytes=24 << 20),
        cost_estimate=pl.CostEstimate(
            flops=4 * total * ROWS * 256, bytes_accessed=1 << 20, transcendentals=total * ROWS
        ),
        name=f"flash_{len(slots)}",
    )(*operands)


def indexed(held):
    arrays, slots = [], []
    for slot, pieces in held.items():
        places = []
        for array, start, stop in pieces:
            number = next((i for i, known in enumerate(arrays) if known is array), None)
            if number is None:
                number = len(arrays)
                arrays.append(array)
            places.append((number, start, stop))
        slots.append((slot, places))
    return slots, arrays


def fresh_kernel(slots, *refs):
    blocks, share_ref, rows_ref = refs[:-2], refs[-2], refs[-1]
    start = pl.multiple_of(FILL + lax.axis_index("seg") * SHARE, SHARE)
    for slot, pieces in slots:
        pair = origin(slot) % NBLK // 2
        block = blocks[pieces[0][0]]
        share_ref[pl.ds(pl.multiple_of(pair * SHARE, SHARE), SHARE), :] = block[pl.ds(start, SHARE), :]
        rows_ref[pl.ds(pl.multiple_of(pair * TOK, TOK), TOK), :] = block[FILL : FILL + TOK, :]


def fresh_rows(held):
    slots, blocks = indexed(held)
    return pl.pallas_call(
        functools.partial(fresh_kernel, slots),
        in_specs=[VMEM] * len(blocks),
        out_specs=[VMEM, VMEM],
        out_shape=[
            jax.ShapeDtypeStruct((NBLK // 2 * SHARE, 2 * HD), BF16),
            jax.ShapeDtypeStruct((NBLK // 2 * TOK, 2 * HD), BF16),
        ],
        compiler_params=pltpu.CompilerParams(vmem_limit_bytes=1 << 20),
        name="fresh_rows",
    )(*blocks)


def pages_kernel(len_ref, owner_ref, cache_ref, own_ref, twin_ref, out_ref):
    blk = lax.axis_index("blk")
    device = lax.axis_index("seg") * NBLK + blk
    filled = len_ref[device]
    pages = owner_ref.shape[1]
    owned = jnp.broadcast_to((owner_ref[...] == device).astype(F32), (16, pages)).astype(BF16)
    before = (
        lax.broadcasted_iota(jnp.int32, (pages, pages), 0) < lax.broadcasted_iota(jnp.int32, (pages, pages), 1)
    ).astype(BF16)
    rank = jnp.dot(owned, before, preferred_element_type=F32)
    rank = jnp.where(owned > 0, rank, -1.0).astype(BF16)
    half = SLOTS // 2
    written, count = None, None
    for rows_ref, core in ((own_ref, blk % 2), (twin_ref, 1 - blk % 2)):
        rows = rows_ref.shape[0]
        row = lax.broadcasted_iota(jnp.int32, (pages, rows), 1)
        page = (row // TOK * 2 + core) * (TOK // PAGE) + row % TOK // PAGE
        spread = (page == lax.broadcasted_iota(jnp.int32, (pages, rows), 0)).astype(BF16)
        row_rank = jnp.dot(rank, spread, preferred_element_type=F32)[0:1].astype(jnp.int32)
        target = filled + row_rank * PAGE + lax.broadcasted_iota(jnp.int32, (1, rows), 1) % PAGE
        target = jnp.where(row_rank >= 0, target, -1)
        pick = (lax.broadcasted_iota(jnp.int32, (half, rows), 0) + half == target).astype(BF16)
        term = jnp.dot(pick, rows_ref[...], preferred_element_type=F32)
        written = term if written is None else written + term
        most = jnp.max(row_rank) + 1
        count = most if count is None else jnp.maximum(count, most)
    slot_id = lax.broadcasted_iota(jnp.int32, (half, 2 * HD), 0) + half
    is_new = (slot_id >= filled) & (slot_id < filled + count * PAGE)
    out_ref[0:half, :] = cache_ref[0:half, :]
    out_ref[half:SLOTS, :] = jnp.where(is_new, written.astype(BF16), cache_ref[half:SLOTS, :])


def write_pages(cache_len, page_owner, cache_kv, own_rows, twin_rows):
    return pl.pallas_call(
        pages_kernel,
        in_specs=[SMEM] + [VMEM] * 4,
        out_specs=VMEM,
        out_shape=jax.ShapeDtypeStruct(cache_kv.shape, BF16),
        compiler_params=pltpu.CompilerParams(vmem_limit_bytes=16 << 20),
        cost_estimate=pl.CostEstimate(flops=10**9, bytes_accessed=2 << 20, transcendentals=0),
        name="write_pages",
    )(cache_len, page_owner.reshape(1, -1), cache_kv, own_rows, twin_rows)


def log_sum(ref, s, stat):
    three = [ref[s, stat + i : stat + i + 1, :].astype(F32) for i in range(3)]
    return three[0] + three[1] + three[2]


def pair_kernel(own_ref, twin_ref, out_ref):
    for s in range(NSEG):
        for head in range(2):
            stat = 2 * HD + head * 16
            rows = slice(head * HD, (head + 1) * HD)
            own, twin = log_sum(own_ref, s, stat), log_sum(twin_ref, s, stat)
            top = jnp.maximum(own, twin)
            own_w, twin_w = jnp.exp2(own - top), jnp.exp2(twin - top)
            total = own_w + twin_w
            scale = 1.0 / total
            out = own_ref[s, rows, :].astype(F32) * (own_w * scale) + twin_ref[s, rows, :].astype(F32) * (twin_w * scale)
            out_ref[s, rows, :] = out.astype(BF16)
            out_ref[s, stat : stat + 16, :] = three_terms(top + jnp.log2(total))


def merge_pair(own, twin):
    return pl.pallas_call(
        pair_kernel,
        in_specs=[VMEM, VMEM],
        out_specs=VMEM,
        out_shape=jax.ShapeDtypeStruct(own.shape, BF16),
        compiler_params=pltpu.CompilerParams(vmem_limit_bytes=4 << 20),
        name="merge_pair",
    )(own, twin)


def merge_kernel(parts_ref, out_ref):
    for head in range(2):
        stat = 2 * HD + head * 16
        logs = [log_sum(parts_ref, s, stat) for s in range(NSEG)]
        top = functools.reduce(jnp.maximum, logs)
        weights = [jnp.exp2(v - top) for v in logs]
        scale = 1.0 / functools.reduce(jnp.add, weights)
        out = None
        for s in range(NSEG):
            term = parts_ref[s, head * HD : (head + 1) * HD, :].astype(F32) * (weights[s] * scale)
            out = term if out is None else out + term
        out_ref[:, head * HD : (head + 1) * HD] = out.T.astype(BF16)


def merge(parts):
    return pl.pallas_call(
        merge_kernel,
        in_specs=[VMEM],
        out_specs=VMEM,
        out_shape=jax.ShapeDtypeStruct((TOK, 2 * HD), BF16),
        compiler_params=pltpu.CompilerParams(vmem_limit_bytes=4 << 20),
        name="merge",
    )(parts)


def shift(block, dx=0, flip_z=False, flip_core=False):
    return lax.ppermute(block, AXES, neighbours(-dx, flip_z, flip_core))


def after(values, other):
    return lax.optimization_barrier((values, other))


def scaled_queries(twin, own):
    return pl.pallas_call(
        queries_kernel,
        in_specs=[VMEM, VMEM],
        out_specs=VMEM,
        out_shape=jax.ShapeDtypeStruct((2 * HD, ROWS), BF16),
        compiler_params=pltpu.CompilerParams(vmem_limit_bytes=4 << 20),
        name="scaled_queries",
    )(twin, own)


def on_device(queries, new_kv, cache_kv, cache_len, page_owner):
    def placed(blocks):
        return {(*slot, False): [(block, 0, FILL + TOK)] for slot, block in blocks.items()}

    own = pack(cache_kv, new_kv)
    across = shift(own, flip_z=True)
    twin_queries = shift(queries, flip_core=True)
    beside = {(1, False): shift(own, 1), (-1, False): shift(own, -1), (2, False): shift(own, 2)}
    qt = scaled_queries(twin_queries, queries)
    held = placed({(0, False): own})
    everything = dict(held)
    state = flash(held, cache_len, qt, None)

    across, state = after(across, state)
    far = {(1, True): shift(across, 1), (-1, True): shift(across, -1)}
    beside, state = after(beside, state)
    far[2, True] = shift(beside[2, False], flip_z=True)
    held = placed({(0, True): across, **beside})
    everything.update(held)
    state = flash(held, cache_len, qt, state)

    far, state = after(far, state)
    held = placed(far)
    everything.update(held)
    fresh, rows = fresh_rows(everything)
    twin_rows = shift(rows, flip_core=True)
    twin_part, own_part = flash(held, cache_len, qt, state, fresh)
    part = merge_pair(own_part, shift(twin_part, flip_core=True))
    parts = lax.all_to_all(part, "seg", 0, 0)
    cache_out = write_pages(cache_len, page_owner, cache_kv, rows, twin_rows)
    return merge(parts), cache_out


def solution(mesh):
    placed = (P("blk", None), P("blk", None), P(("seg", "blk"), None), P(), P())
    return jax.shard_map(
        on_device,
        mesh=mesh,
        in_specs=placed,
        out_specs=(P("blk", "seg"), P(("seg", "blk"), None)),
        check_vma=False,
    )
```

```python
import functools

import jax
import jax.numpy as jnp
from jax import lax
from jax.experimental import pallas as pl
from jax.experimental.pallas import tpu as pltpu
from jax.sharding import PartitionSpec as P


F32 = jnp.float32
BF16 = jnp.bfloat16
HEADS = 16
HD = 128
TOK = 128
ROWS = 2 * HEADS * TOK
PART = HEADS * TOK
SLOTS = 512
FILL = 448
PAGE = 8
NSEG = 8
NBLK = 16
SHARE = TOK // NSEG
CHUNK = 2 * HD + 16
ACC = HD + 16
WIDTH = 512
NEG = -1e30
SCALE = 1.4426950408889634 / HD**0.5
VMEM = pl.BlockSpec(memory_space=pltpu.VMEM)
SMEM = pl.BlockSpec(memory_space=pltpu.SMEM)
AXES = ("seg", "blk")


def neighbours(dx=0, flip_z=False, flip_core=False):
    pairs = []
    for here in range(NSEG * NBLK):
        seg, blk = divmod(here, NBLK)
        pairs.append((here, device_at(seg, blk, dx, flip_z, flip_core)))
    return pairs


def device_at(seg, blk, dx, flip_z, flip_core):
    y, z_lo = seg // 2, seg % 2
    z_hi, x, core = blk // 8, (blk // 2) % 4, blk % 2
    if flip_z:
        z_lo, z_hi = 1 - z_lo, 1 - z_hi
    if flip_core:
        core = 1 - core
    x = (x + dx) % 4
    return (y * 2 + z_lo) * NBLK + z_hi * 8 + x * 2 + core


def origin(slot):
    return device_at(lax.axis_index("seg"), lax.axis_index("blk"), *slot)


def queries_kernel(twin_ref, own_ref, qt_ref):
    for number, q_ref in enumerate((twin_ref, own_ref)):
        for h in range(HEADS):
            scaled = q_ref[:, h * HD : (h + 1) * HD].astype(F32).T * SCALE
            high = scaled.astype(BF16)
            cols = slice(number * PART + h * TOK, number * PART + (h + 1) * TOK)
            qt_ref[0:HD, cols] = high
            qt_ref[HD : 2 * HD, cols] = (scaled - high.astype(F32)).astype(BF16)


def in_hbm(array):
    return pltpu.with_memory_space_constraint(array, pltpu.HBM)


def pack_kernel(cache_ref, new_ref, q_ref, out_ref, q_out, sems):
    copies = [
        pltpu.make_async_copy(cache_ref.at[0:FILL], out_ref.at[0:FILL], sems.at[0]),
        pltpu.make_async_copy(new_ref, out_ref.at[FILL : FILL + TOK], sems.at[1]),
        pltpu.make_async_copy(q_ref, q_out, sems.at[2]),
    ]
    for copy in copies:
        copy.start()
    for copy in copies:
        copy.wait()


def pack(cache_kv, new_kv, queries):
    return pl.pallas_call(
        pack_kernel,
        in_specs=[pl.BlockSpec(memory_space=pltpu.HBM)] * 3,
        out_specs=[VMEM, VMEM],
        out_shape=[
            jax.ShapeDtypeStruct((FILL + TOK, 2 * HD), BF16),
            jax.ShapeDtypeStruct(queries.shape, BF16),
        ],
        scratch_shapes=[pltpu.SemaphoreType.DMA((3,))],
        compiler_params=pltpu.CompilerParams(vmem_limit_bytes=1 << 20),
        name="pack",
    )(in_hbm(cache_kv), in_hbm(new_kv), in_hbm(queries))


def gather_keys(slots, blocks, fresh_ref, len_ref, keys, vals, vals_t):
    total = keys.shape[0]
    for j, (slot, which) in enumerate(slots):
        ok = lax.broadcasted_iota(jnp.int32, (FILL, HD), 0) < len_ref[origin(slot)]
        key = blocks[which][0:FILL, 0:HD]
        value = blocks[which][0:FILL, HD : 2 * HD]
        key = jnp.where(ok, key, jnp.broadcast_to(key[0:1], (FILL, HD)))
        rows = slice(j * FILL, (j + 1) * FILL)
        keys[rows, 0:HD] = key
        keys[rows, HD : 2 * HD] = key
        vals[rows, 0:HD] = jnp.where(ok, value, jnp.zeros_like(value))
        vals[rows, HD : 2 * HD] = ok.astype(BF16)
    old = used = len(slots) * FILL
    if fresh_ref is not None:
        used = old + fresh_ref.shape[0]
        keys[old:used, 0:HD] = fresh_ref[:, 0:HD]
        keys[old:used, HD : 2 * HD] = fresh_ref[:, 0:HD]
        vals[old:used, 0:HD] = fresh_ref[:, HD : 2 * HD]
        vals[old:used, HD : 2 * HD] = jnp.ones((used - old, HD), BF16)
    if total > used:
        keys[used:total, :] = jnp.broadcast_to(keys[0:1, :], (total - used, 2 * HD))
        vals[used:total, :] = jnp.zeros((total - used, 2 * HD), BF16)
    for c in range(total // 128):
        rows = slice(c * 128, (c + 1) * 128)
        vals_t[0:HD, rows] = vals[rows, 0:HD].T
        vals_t[HD:ACC, rows] = vals[rows, HD : 2 * HD].T[0 : ACC - HD]


def flash_columns(columns, old, keys, vals_t, qt_ref, state, even_ref, odd_ref, query_blk, emit):
    total, width = even_ref.shape
    first, last = columns[0] // width, columns[1] // width

    def column_max(s):
        return jnp.max(s.reshape(s.shape[0] // 8, 8, width), axis=0)

    def score(r, scores_ref):
        cols = pl.ds(pl.multiple_of(r * width, width), width)
        s = jnp.dot(keys[...], qt_ref[:, cols], preferred_element_type=F32)
        if query_blk is None:
            scores_ref[...] = s
            return column_max(s)
        shape = (total - old, width)
        key_id = lax.broadcasted_iota(jnp.int32, shape, 0)
        key_blk = key_id // SHARE * 2 + lax.axis_index("blk") % 2
        key_pos = key_blk * TOK + lax.axis_index("seg") * SHARE + key_id % SHARE
        token = query_blk * TOK + lax.broadcasted_iota(jnp.int32, shape, 1) % TOK
        fresh = jnp.where(key_pos <= token, s[old:total], NEG)
        scores_ref[0:old] = s[0:old]
        scores_ref[old:total] = fresh
        return jnp.maximum(column_max(s[0:old]), column_max(fresh))

    def weigh(r, tops, scores_ref, next_ref):
        cols = pl.ds(pl.multiple_of(r * width, width), width)
        top = jnp.max(tops, axis=0, keepdims=True)
        if state is not None:
            top = jnp.maximum(top, state[0][0:1, cols])
        if next_ref is not None:
            tops = score(r + 1, next_ref)
        w = jnp.exp2(scores_ref[...] - top).astype(BF16)
        out = jnp.dot(vals_t[...], w, preferred_element_type=F32)
        if state is not None:
            out = out + state[1][:, cols] * jnp.exp2(state[0][0:1, cols] - top)
        emit(r - first, cols, out, top)
        return tops

    def two(i, tops, more=True):
        tops = weigh(first + 2 * i, tops, even_ref, odd_ref)
        return weigh(first + 2 * i + 1, tops, odd_ref, even_ref if more else None)

    pairs = (last - first) // 2
    tops = lax.fori_loop(0, pairs - 1, two, score(first, even_ref))
    two(pairs - 1, tops, False)


def flash_kernel(slots, operand_count, *refs):
    len_ref, qt_ref = refs[0], refs[1]
    blocks, refs = refs[2 : 2 + operand_count], refs[2 + operand_count :]
    state, (m_ref, acc_ref, keys, vals, vals_t, even_ref, odd_ref) = refs[:-7] or None, refs[-7:]
    gather_keys(slots, blocks, None, len_ref, keys, vals, vals_t)

    def emit(r, cols, out, top):
        acc_ref[:, cols] = out
        m_ref[:, cols] = jnp.broadcast_to(top, m_ref.at[:, cols].shape)

    flash_columns((0, ROWS), keys.shape[0], keys, vals_t, qt_ref, state, even_ref, odd_ref, None, emit)


def emit_part(part_ref, width):
    def emit(r, cols, out, top):
        total = out[HD : HD + 1]
        normal = (out[0:HD] * (1.0 / total)).astype(BF16)
        stats = top + jnp.log2(total)
        for i in range(0, width // TOK, 2):
            pair = r * (width // TOK // 2) + i // 2
            for j in range(2):
                part_ref[pair, j * HD : (j + 1) * HD, :] = normal[:, (i + j) * TOK : (i + j + 1) * TOK]
            put_sums(part_ref, pair, [stats[:, (i + j) * TOK : (i + j + 1) * TOK] for j in range(2)])

    return emit


def put_sums(part_ref, pair, rows):
    terms = []
    for row in rows:
        high = row.astype(BF16)
        rest = row - high.astype(F32)
        middle = rest.astype(BF16)
        terms += [high, middle, (rest - middle.astype(F32)).astype(BF16)]
    part_ref[pair, 2 * HD : CHUNK, :] = jnp.concatenate(terms + [terms[0]] * 10, axis=0)


def get_sums(part_ref, pair, head):
    three = [part_ref[pair, 2 * HD + head * 3 + i : 2 * HD + head * 3 + i + 1, :].astype(F32) for i in range(3)]
    return three[0] + three[1] + three[2]


def twin_kernel(slots, operand_count, *refs):
    len_ref, qt_ref = refs[0], refs[1]
    blocks, refs = refs[2 : 2 + operand_count], refs[2 + operand_count :]
    fresh_ref, m_in, acc_in, part_ref, keys, vals_t, vals, even_ref, odd_ref = refs
    gather_keys(slots, blocks, fresh_ref, len_ref, keys, vals, vals_t)
    blk = lax.axis_index("blk")
    flash_columns(
        (0, PART),
        len(slots) * FILL,
        keys,
        vals_t,
        qt_ref,
        (m_in, acc_in),
        even_ref,
        odd_ref,
        blk + 1 - blk % 2 * 2,
        emit_part(part_ref, even_ref.shape[1]),
    )


def own_kernel(old, qt_ref, keys, vals_t, m_in, acc_in, part_ref, even_ref, odd_ref):
    flash_columns(
        (PART, ROWS),
        old,
        keys,
        vals_t,
        qt_ref,
        (m_in, acc_in),
        even_ref,
        odd_ref,
        lax.axis_index("blk"),
        emit_part(part_ref, even_ref.shape[1]),
    )


def flash_call(kernel, operands, first_spec, out_shape, scratch, total, rows, name, width=WIDTH):
    return pl.pallas_call(
        kernel,
        in_specs=[first_spec] + [VMEM] * (len(operands) - 1),
        out_specs=jax.tree.map(lambda _: VMEM, out_shape),
        out_shape=out_shape,
        scratch_shapes=scratch + [pltpu.VMEM((total, width), F32)] * 2,
        compiler_params=pltpu.CompilerParams(vmem_limit_bytes=24 << 20),
        cost_estimate=pl.CostEstimate(
            flops=4 * total * rows * 256, bytes_accessed=1 << 20, transcendentals=total * rows
        ),
        name=name,
    )(*operands)


def flash(held, cache_len, qt, state):
    slots, blocks = indexed(held)
    total = -(-len(slots) * FILL // 128) * 128
    return flash_call(
        functools.partial(flash_kernel, slots, len(blocks)),
        [cache_len, qt, *blocks, *(state or ())],
        SMEM,
        [jax.ShapeDtypeStruct((8, ROWS), F32), jax.ShapeDtypeStruct((ACC, ROWS), F32)],
        [
            pltpu.VMEM((total, 2 * HD), BF16),
            pltpu.VMEM((total, 2 * HD), BF16),
            pltpu.VMEM((ACC, total), BF16),
        ],
        total,
        ROWS,
        f"flash_{len(slots)}",
    )


def flash_last(held, cache_len, qt, state, fresh):
    slots, blocks = indexed(held)
    old = len(slots) * FILL
    total = -(-(old + fresh.shape[0]) // 128) * 128
    part = jax.ShapeDtypeStruct((NSEG, CHUNK, TOK), BF16)
    twin_part, keys, vals_t = flash_call(
        functools.partial(twin_kernel, slots, len(blocks)),
        [cache_len, qt, *blocks, fresh, *state],
        SMEM,
        [part, jax.ShapeDtypeStruct((total, 2 * HD), BF16), jax.ShapeDtypeStruct((ACC, total), BF16)],
        [pltpu.VMEM((total, 2 * HD), BF16)],
        total,
        PART,
        "flash_twin",
    )
    own_part = flash_call(
        functools.partial(own_kernel, old), [qt, keys, vals_t, *state], VMEM, part, [], total, PART, "flash_own"
    )
    return twin_part, own_part


def indexed(held):
    return [(slot, i) for i, slot in enumerate(held)], list(held.values())


def fresh_kernel(slots, *refs):
    blocks, share_ref, rows_ref = refs[:-2], refs[-2], refs[-1]
    start = pl.multiple_of(FILL + lax.axis_index("seg") * SHARE, SHARE)
    for slot, which in slots:
        pair = origin(slot) % NBLK // 2
        block = blocks[which]
        share_ref[pl.ds(pl.multiple_of(pair * SHARE, SHARE), SHARE), :] = block[pl.ds(start, SHARE), :]
        rows_ref[pl.ds(pl.multiple_of(pair * TOK, TOK), TOK), :] = block[FILL : FILL + TOK, :]


def fresh_rows(held):
    slots, blocks = indexed(held)
    return pl.pallas_call(
        functools.partial(fresh_kernel, slots),
        in_specs=[VMEM] * len(blocks),
        out_specs=[VMEM, VMEM],
        out_shape=[
            jax.ShapeDtypeStruct((NBLK // 2 * SHARE, 2 * HD), BF16),
            jax.ShapeDtypeStruct((NBLK // 2 * TOK, 2 * HD), BF16),
        ],
        compiler_params=pltpu.CompilerParams(vmem_limit_bytes=1 << 20),
        name="fresh_rows",
    )(*blocks)


def pages_kernel(len_ref, owner_ref, cache_ref, own_ref, twin_ref, out_ref):
    blk = lax.axis_index("blk")
    device = lax.axis_index("seg") * NBLK + blk
    filled = len_ref[device]
    pages = owner_ref.shape[1]
    owned = jnp.broadcast_to((owner_ref[...] == device).astype(F32), (16, pages)).astype(BF16)
    before = (
        lax.broadcasted_iota(jnp.int32, (pages, pages), 0) < lax.broadcasted_iota(jnp.int32, (pages, pages), 1)
    ).astype(BF16)
    rank = jnp.dot(owned, before, preferred_element_type=F32)
    rank = jnp.where(owned > 0, rank, -1.0).astype(BF16)
    half = SLOTS // 2
    written, count = None, None
    for rows_ref, core in ((own_ref, blk % 2), (twin_ref, 1 - blk % 2)):
        rows = rows_ref.shape[0]
        row = lax.broadcasted_iota(jnp.int32, (pages, rows), 1)
        page = (row // TOK * 2 + core) * (TOK // PAGE) + row % TOK // PAGE
        spread = (page == lax.broadcasted_iota(jnp.int32, (pages, rows), 0)).astype(BF16)
        row_rank = jnp.dot(rank, spread, preferred_element_type=F32)[0:1].astype(jnp.int32)
        target = filled + row_rank * PAGE + lax.broadcasted_iota(jnp.int32, (1, rows), 1) % PAGE
        target = jnp.where(row_rank >= 0, target, -1)
        pick = (lax.broadcasted_iota(jnp.int32, (half, rows), 0) + half == target).astype(BF16)
        term = jnp.dot(pick, rows_ref[...], preferred_element_type=F32)
        written = term if written is None else written + term
        most = jnp.max(row_rank) + 1
        count = most if count is None else jnp.maximum(count, most)
    slot_id = lax.broadcasted_iota(jnp.int32, (half, 2 * HD), 0) + half
    is_new = (slot_id >= filled) & (slot_id < filled + count * PAGE)
    out_ref[0:half, :] = cache_ref[0:half, :]
    out_ref[half:SLOTS, :] = jnp.where(is_new, written.astype(BF16), cache_ref[half:SLOTS, :])


def write_pages(cache_len, page_owner, cache_kv, own_rows, twin_rows):
    return pl.pallas_call(
        pages_kernel,
        in_specs=[SMEM] + [VMEM] * 4,
        out_specs=VMEM,
        out_shape=jax.ShapeDtypeStruct(cache_kv.shape, BF16),
        compiler_params=pltpu.CompilerParams(vmem_limit_bytes=16 << 20),
        cost_estimate=pl.CostEstimate(flops=10**9, bytes_accessed=2 << 20, transcendentals=0),
        name="write_pages",
    )(cache_len, page_owner.reshape(1, -1), cache_kv, own_rows, twin_rows)


def pair_kernel(own_ref, twin_ref, out_ref, held, sems):
    copies = []
    for s in range(NSEG):
        sums = []
        for head in range(2):
            rows = slice(head * HD, (head + 1) * HD)
            own, twin = get_sums(own_ref, s, head), get_sums(twin_ref, s, head)
            top = jnp.maximum(own, twin)
            own_w, twin_w = jnp.exp2(own - top), jnp.exp2(twin - top)
            total = own_w + twin_w
            scale = 1.0 / total
            out = own_ref[s, rows, :].astype(F32) * (own_w * scale) + twin_ref[s, rows, :].astype(F32) * (twin_w * scale)
            held[s, rows, :] = out.astype(BF16)
            sums.append(top + jnp.log2(total))
        put_sums(held, s, sums)
        copies.append(pltpu.make_async_copy(held.at[s], out_ref.at[s], sems.at[s]))
        copies[-1].start()
    for copy in copies:
        copy.wait()


def merge_pair(own, twin):
    return pl.pallas_call(
        pair_kernel,
        in_specs=[VMEM, VMEM],
        out_specs=pl.BlockSpec(memory_space=pltpu.HBM),
        out_shape=jax.ShapeDtypeStruct(own.shape, BF16),
        scratch_shapes=[pltpu.VMEM(own.shape, BF16), pltpu.SemaphoreType.DMA((NSEG,))],
        compiler_params=pltpu.CompilerParams(vmem_limit_bytes=4 << 20),
        name="merge_pair",
    )(own, twin)


def merge_kernel(parts_ref, out_ref):
    for head in range(2):
        logs = [get_sums(parts_ref, s, head) for s in range(NSEG)]
        top = functools.reduce(jnp.maximum, logs)
        weights = [jnp.exp2(v - top) for v in logs]
        scale = 1.0 / functools.reduce(jnp.add, weights)
        out = None
        for s in range(NSEG):
            term = parts_ref[s, head * HD : (head + 1) * HD, :].astype(F32) * (weights[s] * scale)
            out = term if out is None else out + term
        out_ref[:, head * HD : (head + 1) * HD] = out.T.astype(BF16)


def merge(parts):
    return pl.pallas_call(
        merge_kernel,
        in_specs=[VMEM],
        out_specs=VMEM,
        out_shape=jax.ShapeDtypeStruct((TOK, 2 * HD), BF16),
        compiler_params=pltpu.CompilerParams(vmem_limit_bytes=4 << 20),
        name="merge",
    )(parts)


def shift(block, dx=0, flip_z=False, flip_core=False):
    return lax.ppermute(block, AXES, neighbours(-dx, flip_z, flip_core))


def after(values, other):
    return lax.optimization_barrier((values, other))


def scaled_queries(twin, own):
    return pl.pallas_call(
        queries_kernel,
        in_specs=[VMEM, VMEM],
        out_specs=VMEM,
        out_shape=jax.ShapeDtypeStruct((2 * HD, ROWS), BF16),
        compiler_params=pltpu.CompilerParams(vmem_limit_bytes=4 << 20),
        name="scaled_queries",
    )(twin, own)


def on_device(queries, new_kv, cache_kv, cache_len, page_owner):
    own, own_queries = pack(cache_kv, new_kv, queries)
    across = shift(own, flip_z=True)
    opposite = shift(own, 2)
    beside = {(1, False, False): shift(own, 1), (-1, False, False): shift(own, -1)}
    qt = scaled_queries(shift(own_queries, flip_core=True), own_queries)
    held = {(0, False, False): own}
    everything = dict(held)
    state = flash(held, cache_len, qt, None)

    across, state = after(across, state)
    far = {(1, True, False): shift(across, 1), (-1, True, False): shift(across, -1)}
    opposite, state = after(opposite, state)
    far[2, True, False] = shift(opposite, flip_z=True)
    held = {(0, True, False): across, (2, False, False): opposite}
    everything.update(held)
    state = flash(held, cache_len, qt, state)

    beside, state = after(beside, state)
    everything.update(beside)
    state = flash(beside, cache_len, qt, state)

    far, state = after(far, state)
    everything.update(far)
    fresh, rows = fresh_rows(everything)
    twin_rows = shift(rows, flip_core=True)
    twin_part, own_part = flash_last(far, cache_len, qt, state, fresh)
    part = merge_pair(own_part, shift(twin_part, flip_core=True))
    parts = lax.all_to_all(part, "seg", 0, 0)
    cache_out = write_pages(cache_len, page_owner, cache_kv, rows, twin_rows)
    return merge(parts), cache_out


def solution(mesh):
    placed = (P("blk", None), P("blk", None), P(("seg", "blk"), None), P(), P())
    return jax.shard_map(
        on_device,
        mesh=mesh,
        in_specs=placed,
        out_specs=(P("blk", "seg"), P(("seg", "blk"), None)),
        check_vma=False,
    )
```

```python
import functools

import jax
import jax.numpy as jnp
from jax import lax
from jax.experimental import pallas as pl
from jax.experimental.pallas import tpu as pltpu
from jax.sharding import PartitionSpec as P


F32 = jnp.float32
BF16 = jnp.bfloat16
HEADS = 16
HD = 128
TOK = 128
ROWS = 2 * HEADS * TOK
PART = HEADS * TOK
SLOTS = 512
LEAST = 256
FILL = 448
PAGE = 8
NSEG = 8
NBLK = 16
SHARE = TOK // NSEG
CHUNK = 2 * HD + 16
ACC = HD + 16
WIDTH = 512
NEG = -1e30
SCALE = 1.4426950408889634 / HD**0.5
VMEM = pl.BlockSpec(memory_space=pltpu.VMEM)
SMEM = pl.BlockSpec(memory_space=pltpu.SMEM)
AXES = ("seg", "blk")
SLOT_ORDER = [(dx, flip_z, False) for flip_z in (False, True) for dx in (0, 1, -1, 2)]


def neighbours(dx=0, flip_z=False, flip_core=False):
    pairs = []
    for here in range(NSEG * NBLK):
        seg, blk = divmod(here, NBLK)
        pairs.append((here, device_at(seg, blk, dx, flip_z, flip_core)))
    return pairs


def device_at(seg, blk, dx, flip_z, flip_core):
    y, z_lo = seg // 2, seg % 2
    z_hi, x, core = blk // 8, (blk // 2) % 4, blk % 2
    if flip_z:
        z_lo, z_hi = 1 - z_lo, 1 - z_hi
    if flip_core:
        core = 1 - core
    x = (x + dx) % 4
    return (y * 2 + z_lo) * NBLK + z_hi * 8 + x * 2 + core


def origin(slot):
    return device_at(lax.axis_index("seg"), lax.axis_index("blk"), *slot)


def queries_kernel(twin_ref, own_ref, qt_ref):
    for number, q_ref in enumerate((twin_ref, own_ref)):
        for h in range(HEADS):
            scaled = q_ref[:, h * HD : (h + 1) * HD].astype(F32).T * SCALE
            high = scaled.astype(BF16)
            cols = slice(number * PART + h * TOK, number * PART + (h + 1) * TOK)
            qt_ref[0:HD, cols] = high
            qt_ref[HD : 2 * HD, cols] = (scaled - high.astype(F32)).astype(BF16)


def in_hbm(array):
    return pltpu.with_memory_space_constraint(array, pltpu.HBM)


def pack_kernel(cache_ref, new_ref, q_ref, len_ref, out_ref, q_out, filled_ref, len_copy, sems):
    copies = [
        pltpu.make_async_copy(cache_ref.at[0:FILL], out_ref.at[0:FILL], sems.at[0]),
        pltpu.make_async_copy(new_ref, out_ref.at[FILL : FILL + TOK], sems.at[1]),
        pltpu.make_async_copy(q_ref, q_out, sems.at[2]),
        pltpu.make_async_copy(len_ref, len_copy, sems.at[3]),
    ]
    for copy in copies:
        copy.start()
    for copy in reversed(copies):
        copy.wait()
    for j, slot in enumerate(SLOT_ORDER):
        filled_ref[j : j + 1, :] = jnp.full((1, 128), len_copy[origin(slot)], jnp.int32)


def pack(cache_kv, new_kv, queries, cache_len):
    return pl.pallas_call(
        pack_kernel,
        in_specs=[pl.BlockSpec(memory_space=pltpu.HBM)] * 4,
        out_specs=[VMEM] * 3,
        out_shape=[
            jax.ShapeDtypeStruct((FILL + TOK, 2 * HD), BF16),
            jax.ShapeDtypeStruct(queries.shape, BF16),
            jax.ShapeDtypeStruct((len(SLOT_ORDER), 128), jnp.int32),
        ],
        scratch_shapes=[pltpu.SMEM(cache_len.shape, jnp.int32), pltpu.SemaphoreType.DMA((4,))],
        compiler_params=pltpu.CompilerParams(vmem_limit_bytes=1 << 20),
        name="pack",
    )(*map(in_hbm, (cache_kv, new_kv, queries, cache_len)))


def gather_keys(slots, blocks, fresh_ref, filled_ref, keys, vals, vals_t):
    total = keys.shape[0]
    spans = []
    for j, (slot, which) in enumerate(slots):
        filled = filled_ref[SLOT_ORDER.index(slot) : SLOT_ORDER.index(slot) + 1, :]
        block, start = blocks[which], j * FILL
        ok = lax.broadcasted_iota(jnp.int32, (FILL - LEAST, HD), 0) < filled - LEAST
        head = block[0:LEAST, 0:HD]
        tail = block[LEAST:FILL, 0:HD]
        tail = jnp.where(ok, tail, jnp.broadcast_to(head[0:1], tail.shape))
        value = block[LEAST:FILL, HD : 2 * HD]
        for lanes in (slice(0, HD), slice(HD, 2 * HD)):
            keys[start : start + LEAST, lanes] = head
            keys[start + LEAST : start + FILL, lanes] = tail
        vals[start : start + LEAST, :] = block[0:LEAST, HD : 2 * HD]
        vals[start + LEAST : start + FILL, :] = jnp.where(ok, value, jnp.zeros_like(value))
        spans.append((start, start + LEAST, start + FILL, start + filled))
    old = used = len(slots) * FILL
    if fresh_ref is not None:
        used = old + fresh_ref.shape[0]
        keys[old:used, 0:HD] = fresh_ref[:, 0:HD]
        keys[old:used, HD : 2 * HD] = fresh_ref[:, 0:HD]
        vals[old:used, :] = fresh_ref[:, HD : 2 * HD]
        spans.append((old, used, used, used))
    if total > used:
        keys[used:total, :] = jnp.broadcast_to(keys[0:1, :], (total - used, 2 * HD))
        vals[used:total, :] = jnp.zeros((total - used, HD), BF16)
    for c in range(total // 128):
        low, high = c * 128, (c + 1) * 128
        vals_t[0:HD, low:high] = vals[low:high, :].T
        if any(start <= low and high <= sure for start, sure, _, _ in spans):
            vals_t[HD:ACC, low:high] = jnp.ones((ACC - HD, 128), BF16)
            continue
        lane = lax.broadcasted_iota(jnp.int32, (ACC - HD, 128), 1) + low
        one = None
        for start, _, stop, filled in spans:
            if start < high and stop > low:
                inside = (lane >= start) & (lane < filled)
                one = inside if one is None else one | inside
        vals_t[HD:ACC, low:high] = one.astype(F32).astype(BF16)


def flash_columns(columns, old, keys, vals_t, qt_ref, state, even_ref, odd_ref, query_blk, emit):
    total, width = even_ref.shape
    first, last = columns[0] // width, columns[1] // width

    def column_max(s):
        return jnp.max(s.reshape(s.shape[0] // 8, 8, width), axis=0)

    def score(r, scores_ref):
        cols = pl.ds(pl.multiple_of(r * width, width), width)
        s = jnp.dot(keys[...], qt_ref[:, cols], preferred_element_type=F32)
        if query_blk is None:
            scores_ref[...] = s
            return column_max(s)
        shape = (total - old, width)
        key_id = lax.broadcasted_iota(jnp.int32, shape, 0)
        key_blk = key_id // SHARE * 2 + lax.axis_index("blk") % 2
        key_pos = key_blk * TOK + lax.axis_index("seg") * SHARE + key_id % SHARE
        token = query_blk * TOK + lax.broadcasted_iota(jnp.int32, shape, 1) % TOK
        fresh = jnp.where(key_pos <= token, s[old:total], NEG)
        scores_ref[0:old] = s[0:old]
        scores_ref[old:total] = fresh
        return jnp.maximum(column_max(s[0:old]), column_max(fresh))

    def weigh(r, tops, scores_ref, next_ref):
        cols = pl.ds(pl.multiple_of(r * width, width), width)
        top = jnp.max(tops, axis=0, keepdims=True)
        if state is not None:
            top = jnp.maximum(top, state[0][0:1, cols])
        if next_ref is not None:
            tops = score(r + 1, next_ref)
        w = jnp.exp2(scores_ref[...] - top).astype(BF16)
        out = jnp.dot(vals_t[...], w, preferred_element_type=F32)
        if state is not None:
            out = out + state[1][:, cols] * jnp.exp2(state[0][0:1, cols] - top)
        emit(r - first, cols, out, top)
        return tops

    def two(i, tops, more=True):
        tops = weigh(first + 2 * i, tops, even_ref, odd_ref)
        return weigh(first + 2 * i + 1, tops, odd_ref, even_ref if more else None)

    pairs = (last - first) // 2
    trips = jnp.minimum(lax.axis_index("seg") + pairs - 1, pairs - 1)
    tops = lax.fori_loop(0, trips, two, score(first, even_ref))
    two(pairs - 1, tops, False)


def flash_kernel(slots, operand_count, *refs):
    filled_ref, qt_ref = refs[0], refs[1]
    blocks, refs = refs[2 : 2 + operand_count], refs[2 + operand_count :]
    state, (m_ref, acc_ref, keys, vals, vals_t, even_ref, odd_ref) = refs[:-7] or None, refs[-7:]
    gather_keys(slots, blocks, None, filled_ref, keys, vals, vals_t)

    def emit(r, cols, out, top):
        acc_ref[:, cols] = out
        m_ref[:, cols] = jnp.broadcast_to(top, m_ref.at[:, cols].shape)

    flash_columns((0, ROWS), keys.shape[0], keys, vals_t, qt_ref, state, even_ref, odd_ref, None, emit)


def emit_part(part_ref, width):
    def emit(r, cols, out, top):
        total = out[HD : HD + 1]
        normal = (out[0:HD] * (1.0 / total)).astype(BF16)
        stats = top + jnp.log2(total)
        for i in range(0, width // TOK, 2):
            pair = r * (width // TOK // 2) + i // 2
            for j in range(2):
                part_ref[pair, j * HD : (j + 1) * HD, :] = normal[:, (i + j) * TOK : (i + j + 1) * TOK]
            put_sums(part_ref, pair, [stats[:, (i + j) * TOK : (i + j + 1) * TOK] for j in range(2)])

    return emit


def put_sums(part_ref, pair, rows):
    terms = []
    for row in rows:
        high = row.astype(BF16)
        rest = row - high.astype(F32)
        middle = rest.astype(BF16)
        terms += [high, middle, (rest - middle.astype(F32)).astype(BF16)]
    part_ref[pair, 2 * HD : CHUNK, :] = jnp.concatenate(terms + [terms[0]] * 10, axis=0)


def get_sums(part_ref, pair, head):
    three = [part_ref[pair, 2 * HD + head * 3 + i : 2 * HD + head * 3 + i + 1, :].astype(F32) for i in range(3)]
    return three[0] + three[1] + three[2]


def twin_kernel(slots, operand_count, *refs):
    filled_ref, qt_ref = refs[0], refs[1]
    blocks, refs = refs[2 : 2 + operand_count], refs[2 + operand_count :]
    fresh_ref, m_in, acc_in, part_ref, keys, vals_t, vals, even_ref, odd_ref = refs
    gather_keys(slots, blocks, fresh_ref, filled_ref, keys, vals, vals_t)
    blk = lax.axis_index("blk")
    flash_columns(
        (0, PART),
        len(slots) * FILL,
        keys,
        vals_t,
        qt_ref,
        (m_in, acc_in),
        even_ref,
        odd_ref,
        blk + 1 - blk % 2 * 2,
        emit_part(part_ref, even_ref.shape[1]),
    )


def own_kernel(old, qt_ref, keys, vals_t, m_in, acc_in, part_ref, even_ref, odd_ref):
    flash_columns(
        (PART, ROWS),
        old,
        keys,
        vals_t,
        qt_ref,
        (m_in, acc_in),
        even_ref,
        odd_ref,
        lax.axis_index("blk"),
        emit_part(part_ref, even_ref.shape[1]),
    )


def flash_call(kernel, operands, out_shape, scratch, total, rows, name, width=WIDTH):
    return pl.pallas_call(
        kernel,
        in_specs=[VMEM] * len(operands),
        out_specs=jax.tree.map(lambda _: VMEM, out_shape),
        out_shape=out_shape,
        scratch_shapes=scratch + [pltpu.VMEM((total, width), F32)] * 2,
        compiler_params=pltpu.CompilerParams(vmem_limit_bytes=24 << 20),
        cost_estimate=pl.CostEstimate(
            flops=4 * total * rows * 256, bytes_accessed=1 << 20, transcendentals=total * rows
        ),
        name=name,
    )(*operands)


def flash(held, filled, qt, state):
    slots, blocks = indexed(held)
    total = -(-len(slots) * FILL // 128) * 128
    return flash_call(
        functools.partial(flash_kernel, slots, len(blocks)),
        [filled, qt, *blocks, *(state or ())],
        [jax.ShapeDtypeStruct((8, ROWS), F32), jax.ShapeDtypeStruct((ACC, ROWS), F32)],
        [
            pltpu.VMEM((total, 2 * HD), BF16),
            pltpu.VMEM((total, HD), BF16),
            pltpu.VMEM((ACC, total), BF16),
        ],
        total,
        ROWS,
        f"flash_{len(slots)}",
    )


def flash_last(held, filled, qt, state, fresh):
    slots, blocks = indexed(held)
    old = len(slots) * FILL
    total = -(-(old + fresh.shape[0]) // 128) * 128
    part = jax.ShapeDtypeStruct((NSEG, CHUNK, TOK), BF16)
    twin_part, keys, vals_t = flash_call(
        functools.partial(twin_kernel, slots, len(blocks)),
        [filled, qt, *blocks, fresh, *state],
        [part, jax.ShapeDtypeStruct((total, 2 * HD), BF16), jax.ShapeDtypeStruct((ACC, total), BF16)],
        [pltpu.VMEM((total, HD), BF16)],
        total,
        PART,
        "flash_twin",
    )
    own_part = flash_call(
        functools.partial(own_kernel, old), [qt, keys, vals_t, *state], part, [], total, PART, "flash_own"
    )
    return twin_part, own_part


def indexed(held):
    return [(slot, i) for i, slot in enumerate(held)], list(held.values())


def fresh_kernel(slots, *refs):
    blocks, share_ref, rows_ref = refs[:-2], refs[-2], refs[-1]
    start = pl.multiple_of(FILL + lax.axis_index("seg") * SHARE, SHARE)
    for slot, which in slots:
        pair = origin(slot) % NBLK // 2
        block = blocks[which]
        share_ref[pl.ds(pl.multiple_of(pair * SHARE, SHARE), SHARE), :] = block[pl.ds(start, SHARE), :]
        rows_ref[pl.ds(pl.multiple_of(pair * TOK, TOK), TOK), :] = block[FILL : FILL + TOK, :]


def fresh_rows(held):
    slots, blocks = indexed(held)
    return pl.pallas_call(
        functools.partial(fresh_kernel, slots),
        in_specs=[VMEM] * len(blocks),
        out_specs=[VMEM, VMEM],
        out_shape=[
            jax.ShapeDtypeStruct((NBLK // 2 * SHARE, 2 * HD), BF16),
            jax.ShapeDtypeStruct((NBLK // 2 * TOK, 2 * HD), BF16),
        ],
        compiler_params=pltpu.CompilerParams(vmem_limit_bytes=1 << 20),
        name="fresh_rows",
    )(*blocks)


def pages_kernel(len_ref, owner_ref, cache_ref, own_ref, twin_ref, out_ref):
    blk = lax.axis_index("blk")
    device = lax.axis_index("seg") * NBLK + blk
    filled = len_ref[device]
    pages = owner_ref.shape[1]
    owned = jnp.broadcast_to((owner_ref[...] == device).astype(F32), (16, pages)).astype(BF16)
    before = (
        lax.broadcasted_iota(jnp.int32, (pages, pages), 0) < lax.broadcasted_iota(jnp.int32, (pages, pages), 1)
    ).astype(BF16)
    rank = jnp.dot(owned, before, preferred_element_type=F32)
    rank = jnp.where(owned > 0, rank, -1.0).astype(BF16)
    half = SLOTS // 2
    written, count = None, None
    for rows_ref, core in ((own_ref, blk % 2), (twin_ref, 1 - blk % 2)):
        rows = rows_ref.shape[0]
        row = lax.broadcasted_iota(jnp.int32, (pages, rows), 1)
        page = (row // TOK * 2 + core) * (TOK // PAGE) + row % TOK // PAGE
        spread = (page == lax.broadcasted_iota(jnp.int32, (pages, rows), 0)).astype(BF16)
        row_rank = jnp.dot(rank, spread, preferred_element_type=F32)[0:1].astype(jnp.int32)
        target = filled + row_rank * PAGE + lax.broadcasted_iota(jnp.int32, (1, rows), 1) % PAGE
        target = jnp.where(row_rank >= 0, target, -1)
        pick = (lax.broadcasted_iota(jnp.int32, (half, rows), 0) + half == target).astype(BF16)
        term = jnp.dot(pick, rows_ref[...], preferred_element_type=F32)
        written = term if written is None else written + term
        most = jnp.max(row_rank) + 1
        count = most if count is None else jnp.maximum(count, most)
    slot_id = lax.broadcasted_iota(jnp.int32, (half, 2 * HD), 0) + half
    is_new = (slot_id >= filled) & (slot_id < filled + count * PAGE)
    out_ref[0:half, :] = cache_ref[0:half, :]
    out_ref[half:SLOTS, :] = jnp.where(is_new, written.astype(BF16), cache_ref[half:SLOTS, :])


def write_pages(cache_len, page_owner, cache_kv, own_rows, twin_rows):
    return pl.pallas_call(
        pages_kernel,
        in_specs=[SMEM] + [VMEM] * 4,
        out_specs=VMEM,
        out_shape=jax.ShapeDtypeStruct(cache_kv.shape, BF16),
        compiler_params=pltpu.CompilerParams(vmem_limit_bytes=16 << 20),
        cost_estimate=pl.CostEstimate(flops=10**9, bytes_accessed=2 << 20, transcendentals=0),
        name="write_pages",
    )(cache_len, page_owner.reshape(1, -1), cache_kv, own_rows, twin_rows)


def pair_kernel(own_ref, twin_ref, out_ref, held, sems):
    copies = []
    for s in range(NSEG):
        sums = []
        for head in range(2):
            rows = slice(head * HD, (head + 1) * HD)
            own, twin = get_sums(own_ref, s, head), get_sums(twin_ref, s, head)
            top = jnp.maximum(own, twin)
            own_w, twin_w = jnp.exp2(own - top), jnp.exp2(twin - top)
            total = own_w + twin_w
            scale = 1.0 / total
            out = own_ref[s, rows, :].astype(F32) * (own_w * scale) + twin_ref[s, rows, :].astype(F32) * (twin_w * scale)
            held[s, rows, :] = out.astype(BF16)
            sums.append(top + jnp.log2(total))
        put_sums(held, s, sums)
        copies.append(pltpu.make_async_copy(held.at[s], out_ref.at[s], sems.at[s]))
        copies[-1].start()
    for copy in copies:
        copy.wait()


def merge_pair(own, twin):
    return pl.pallas_call(
        pair_kernel,
        in_specs=[VMEM, VMEM],
        out_specs=pl.BlockSpec(memory_space=pltpu.HBM),
        out_shape=jax.ShapeDtypeStruct(own.shape, BF16),
        scratch_shapes=[pltpu.VMEM(own.shape, BF16), pltpu.SemaphoreType.DMA((NSEG,))],
        compiler_params=pltpu.CompilerParams(vmem_limit_bytes=4 << 20),
        name="merge_pair",
    )(own, twin)


def merge_kernel(parts_ref, out_ref):
    for head in range(2):
        logs = [get_sums(parts_ref, s, head) for s in range(NSEG)]
        top = functools.reduce(jnp.maximum, logs)
        weights = [jnp.exp2(v - top) for v in logs]
        scale = 1.0 / functools.reduce(jnp.add, weights)
        out = None
        for s in range(NSEG):
            term = parts_ref[s, head * HD : (head + 1) * HD, :].astype(F32) * (weights[s] * scale)
            out = term if out is None else out + term
        out_ref[:, head * HD : (head + 1) * HD] = out.T.astype(BF16)


def merge(parts):
    return pl.pallas_call(
        merge_kernel,
        in_specs=[VMEM],
        out_specs=VMEM,
        out_shape=jax.ShapeDtypeStruct((TOK, 2 * HD), BF16),
        compiler_params=pltpu.CompilerParams(vmem_limit_bytes=4 << 20),
        name="merge",
    )(parts)


def shift(block, dx=0, flip_z=False, flip_core=False):
    return lax.ppermute(block, AXES, neighbours(-dx, flip_z, flip_core))


def after(values, other):
    return lax.optimization_barrier((values, other))


def scaled_queries(twin, own):
    return pl.pallas_call(
        queries_kernel,
        in_specs=[VMEM, VMEM],
        out_specs=VMEM,
        out_shape=jax.ShapeDtypeStruct((2 * HD, ROWS), BF16),
        compiler_params=pltpu.CompilerParams(vmem_limit_bytes=4 << 20),
        name="scaled_queries",
    )(twin, own)


def on_device(queries, new_kv, cache_kv, cache_len, page_owner):
    own, own_queries, filled = pack(cache_kv, new_kv, queries, cache_len)
    across = shift(own, flip_z=True)
    opposite = shift(own, 2)
    beside = {(1, False, False): shift(own, 1), (-1, False, False): shift(own, -1)}
    qt = scaled_queries(shift(own_queries, flip_core=True), own_queries)
    held = {(0, False, False): own}
    everything = dict(held)
    state = flash(held, filled, qt, None)

    across, state = after(across, state)
    far = {(1, True, False): shift(across, 1), (-1, True, False): shift(across, -1)}
    opposite, state = after(opposite, state)
    far[2, True, False] = shift(opposite, flip_z=True)
    held = {(0, True, False): across, (2, False, False): opposite}
    everything.update(held)
    state = flash(held, filled, qt, state)

    beside, state = after(beside, state)
    everything.update(beside)
    state = flash(beside, filled, qt, state)

    far, state = after(far, state)
    everything.update(far)
    fresh, rows = fresh_rows(everything)
    twin_rows = shift(rows, flip_core=True)
    twin_part, own_part = flash_last(far, filled, qt, state, fresh)
    part = merge_pair(own_part, shift(twin_part, flip_core=True))
    parts = lax.all_to_all(part, "seg", 0, 0)
    cache_out = write_pages(cache_len, page_owner, cache_kv, rows, twin_rows)
    return merge(parts), cache_out


def solution(mesh):
    placed = (P("blk", None), P("blk", None), P(("seg", "blk"), None), P(), P())
    return jax.shard_map(
        on_device,
        mesh=mesh,
        in_specs=placed,
        out_specs=(P("blk", "seg"), P(("seg", "blk"), None)),
        check_vma=False,
    )
```

```python
import functools

import jax
import jax.numpy as jnp
from jax import lax
from jax.experimental import pallas as pl
from jax.experimental.pallas import tpu as pltpu
from jax.sharding import PartitionSpec as P


F32 = jnp.float32
BF16 = jnp.bfloat16
HEADS = 16
HD = 128
TOK = 128
ROWS = 2 * HEADS * TOK
PART = HEADS * TOK
SLOTS = 512
LEAST = 256
FILL = 448
PAGE = 8
NSEG = 8
NBLK = 16
SHARE = TOK // NSEG
CHUNK = 2 * HD + 16
ACC = HD + 16
WIDTH = 512
NEG = -1e30
SCALE = 1.4426950408889634 / HD**0.5
VMEM = pl.BlockSpec(memory_space=pltpu.VMEM)
SMEM = pl.BlockSpec(memory_space=pltpu.SMEM)
AXES = ("seg", "blk")
SLOT_ORDER = [(dx, flip_z, False) for flip_z in (False, True) for dx in (0, 1, -1, 2)]


def neighbours(dx=0, flip_z=False, flip_core=False):
    pairs = []
    for here in range(NSEG * NBLK):
        seg, blk = divmod(here, NBLK)
        pairs.append((here, device_at(seg, blk, dx, flip_z, flip_core)))
    return pairs


def device_at(seg, blk, dx, flip_z, flip_core):
    y, z_lo = seg // 2, seg % 2
    z_hi, x, core = blk // 8, (blk // 2) % 4, blk % 2
    if flip_z:
        z_lo, z_hi = 1 - z_lo, 1 - z_hi
    if flip_core:
        core = 1 - core
    x = (x + dx) % 4
    return (y * 2 + z_lo) * NBLK + z_hi * 8 + x * 2 + core


def origin(slot):
    return device_at(lax.axis_index("seg"), lax.axis_index("blk"), *slot)


def queries_kernel(twin_ref, own_ref, qt_ref):
    for number, q_ref in enumerate((twin_ref, own_ref)):
        for h in range(HEADS):
            scaled = q_ref[:, h * HD : (h + 1) * HD].astype(F32).T * SCALE
            high = scaled.astype(BF16)
            cols = slice(number * PART + h * TOK, number * PART + (h + 1) * TOK)
            qt_ref[0:HD, cols] = high
            qt_ref[HD : 2 * HD, cols] = (scaled - high.astype(F32)).astype(BF16)


def in_hbm(array):
    return pltpu.with_memory_space_constraint(array, pltpu.HBM)


def pack_kernel(cache_ref, new_ref, q_ref, len_ref, out_ref, q_out, filled_ref, len_copy, sems):
    copies = [
        pltpu.make_async_copy(cache_ref.at[0:FILL], out_ref.at[0:FILL], sems.at[0]),
        pltpu.make_async_copy(new_ref, out_ref.at[FILL : FILL + TOK], sems.at[1]),
        pltpu.make_async_copy(q_ref, q_out, sems.at[2]),
        pltpu.make_async_copy(len_ref, len_copy, sems.at[3]),
    ]
    for copy in copies:
        copy.start()
    for copy in reversed(copies):
        copy.wait()
    for j, slot in enumerate(SLOT_ORDER):
        filled_ref[j : j + 1, :] = jnp.full((1, 128), len_copy[origin(slot)], jnp.int32)


def pack(cache_kv, new_kv, queries, cache_len):
    return pl.pallas_call(
        pack_kernel,
        in_specs=[pl.BlockSpec(memory_space=pltpu.HBM)] * 4,
        out_specs=[VMEM] * 3,
        out_shape=[
            jax.ShapeDtypeStruct((FILL + TOK, 2 * HD), BF16),
            jax.ShapeDtypeStruct(queries.shape, BF16),
            jax.ShapeDtypeStruct((len(SLOT_ORDER), 128), jnp.int32),
        ],
        scratch_shapes=[pltpu.SMEM(cache_len.shape, jnp.int32), pltpu.SemaphoreType.DMA((4,))],
        compiler_params=pltpu.CompilerParams(vmem_limit_bytes=1 << 20),
        name="pack",
    )(*map(in_hbm, (cache_kv, new_kv, queries, cache_len)))


def gather_keys(slots, blocks, fresh_ref, filled_ref, keys, vals, vals_t):
    total = keys.shape[0]
    spans = []
    for j, (slot, block) in enumerate(zip(slots, blocks)):
        filled = filled_ref[SLOT_ORDER.index(slot) : SLOT_ORDER.index(slot) + 1, :]
        start = j * FILL
        ok = lax.broadcasted_iota(jnp.int32, (FILL - LEAST, HD), 0) < filled - LEAST
        head = block[0:LEAST, 0:HD]
        tail = block[LEAST:FILL, 0:HD]
        tail = jnp.where(ok, tail, jnp.broadcast_to(head[0:1], tail.shape))
        value = block[LEAST:FILL, HD : 2 * HD]
        for lanes in (slice(0, HD), slice(HD, 2 * HD)):
            keys[start : start + LEAST, lanes] = head
            keys[start + LEAST : start + FILL, lanes] = tail
        vals[start : start + LEAST, :] = block[0:LEAST, HD : 2 * HD]
        vals[start + LEAST : start + FILL, :] = jnp.where(ok, value, jnp.zeros_like(value))
        spans.append((start, start + LEAST, start + FILL, start + filled))
    old = len(slots) * FILL
    if fresh_ref is not None:
        keys[old:total, 0:HD] = fresh_ref[:, 0:HD]
        keys[old:total, HD : 2 * HD] = fresh_ref[:, 0:HD]
        vals[old:total, :] = fresh_ref[:, HD : 2 * HD]
        spans.append((old, total, total, total))
    elif total > old:
        keys[old:total, :] = jnp.broadcast_to(keys[0:1, :], (total - old, 2 * HD))
        vals[old:total, :] = jnp.zeros((total - old, HD), BF16)
    for c in range(total // 128):
        low, high = c * 128, (c + 1) * 128
        vals_t[0:HD, low:high] = vals[low:high, :].T
        if any(start <= low and high <= sure for start, sure, _, _ in spans):
            vals_t[HD:ACC, low:high] = jnp.ones((ACC - HD, 128), BF16)
            continue
        lane = lax.broadcasted_iota(jnp.int32, (ACC - HD, 128), 1) + low
        one = None
        for start, _, stop, filled in spans:
            if start < high and stop > low:
                inside = (lane >= start) & (lane < filled)
                one = inside if one is None else one | inside
        vals_t[HD:ACC, low:high] = one.astype(F32).astype(BF16)


def flash_columns(columns, old, keys, vals_t, qt_ref, state, even_ref, odd_ref, place_ref, emit):
    total, width = even_ref.shape
    first, last = columns[0] // width, columns[1] // width

    def column_max(s):
        return jnp.max(s.reshape(s.shape[0] // 8, 8, width), axis=0)

    def score(r, scores_ref):
        cols = pl.ds(pl.multiple_of(r * width, width), width)
        s = jnp.dot(keys[...], qt_ref[:, cols], preferred_element_type=F32)
        if place_ref is None:
            scores_ref[...] = s
            return column_max(s)
        blk = lax.axis_index("blk")
        query_blk = jnp.where(r < PART // width, blk + 1 - blk % 2 * 2, blk)
        token = lax.broadcasted_iota(jnp.int32, place_ref.shape, 1)
        seen = place_ref[...] - query_blk * TOK <= token
        fresh = jnp.concatenate(
            [jnp.where(seen, s[old:total, i : i + TOK], NEG) for i in range(0, width, TOK)], axis=1
        )
        scores_ref[0:old] = s[0:old]
        scores_ref[old:total] = fresh
        return jnp.maximum(column_max(s[0:old]), column_max(fresh))

    def weigh(r, tops, scores_ref, next_ref):
        cols = pl.ds(pl.multiple_of(r * width, width), width)
        top = jnp.max(tops, axis=0, keepdims=True)
        if state is not None:
            top = jnp.maximum(top, state[0][0:1, cols])
        if next_ref is not None:
            tops = score(r + 1, next_ref)
        w = jnp.exp2(scores_ref[...] - top).astype(BF16)
        out = jnp.dot(vals_t[...], w, preferred_element_type=F32)
        if state is not None:
            out = out + state[1][:, cols] * jnp.exp2(state[0][0:1, cols] - top)
        emit(r - first, cols, out, top)
        return tops

    def two(i, tops, more=True):
        tops = weigh(first + 2 * i, tops, even_ref, odd_ref)
        return weigh(first + 2 * i + 1, tops, odd_ref, even_ref if more else None)

    pairs = (last - first) // 2
    trips = jnp.minimum(lax.axis_index("seg") + pairs - 1, pairs - 1)
    tops = lax.fori_loop(0, trips, two, score(first, even_ref))
    two(pairs - 1, tops, False)


def flash_kernel(slots, has_fresh, *refs):
    filled_ref, qt_ref = refs[0], refs[1]
    blocks, refs = refs[2 : 2 + len(slots)], refs[2 + len(slots) :]
    fresh_ref = place_ref = None
    if has_fresh:
        fresh_ref, place_ref, refs = refs[0], refs[1], refs[2:]
    state, (m_ref, acc_ref, keys, vals, vals_t, even_ref, odd_ref) = refs[:-7] or None, refs[-7:]
    gather_keys(slots, blocks, fresh_ref, filled_ref, keys, vals, vals_t)

    def emit(r, cols, out, top):
        acc_ref[:, cols] = out
        m_ref[:, cols] = jnp.broadcast_to(top, m_ref.at[:, cols].shape)

    old = len(slots) * FILL
    flash_columns((0, ROWS), old, keys, vals_t, qt_ref, state, even_ref, odd_ref, place_ref, emit)


def emit_part(part_ref, width):
    def emit(r, cols, out, top):
        total = out[HD : HD + 1]
        normal = (out[0:HD] * (1.0 / total)).astype(BF16)
        stats = top + jnp.log2(total)
        for i in range(0, width // TOK, 2):
            pair = r * (width // TOK // 2) + i // 2
            for j in range(2):
                part_ref[pair, j * HD : (j + 1) * HD, :] = normal[:, (i + j) * TOK : (i + j + 1) * TOK]
            put_sums(part_ref, pair, [stats[:, (i + j) * TOK : (i + j + 1) * TOK] for j in range(2)])

    return emit


def put_sums(part_ref, pair, rows):
    terms = []
    for row in rows:
        high = row.astype(BF16)
        rest = row - high.astype(F32)
        middle = rest.astype(BF16)
        terms += [high, middle, (rest - middle.astype(F32)).astype(BF16)]
    part_ref[pair, 2 * HD : CHUNK, :] = jnp.concatenate(terms + [terms[0]] * 10, axis=0)


def get_sums(part_ref, pair, head):
    three = [part_ref[pair, 2 * HD + head * 3 + i : 2 * HD + head * 3 + i + 1, :].astype(F32) for i in range(3)]
    return three[0] + three[1] + three[2]


def twin_kernel(slots, *refs):
    filled_ref, qt_ref = refs[0], refs[1]
    blocks, refs = refs[2 : 2 + len(slots)], refs[2 + len(slots) :]
    fresh_ref, place_ref, m_in, acc_in, part_ref, keys, vals_t, vals, even_ref, odd_ref = refs
    gather_keys(slots, blocks, fresh_ref, filled_ref, keys, vals, vals_t)
    emit = emit_part(part_ref, even_ref.shape[1])
    state, old = (m_in, acc_in), len(slots) * FILL
    flash_columns((0, PART), old, keys, vals_t, qt_ref, state, even_ref, odd_ref, place_ref, emit)


def own_kernel(old, qt_ref, keys, vals_t, place_ref, m_in, acc_in, part_ref, even_ref, odd_ref):
    emit = emit_part(part_ref, even_ref.shape[1])
    flash_columns((PART, ROWS), old, keys, vals_t, qt_ref, (m_in, acc_in), even_ref, odd_ref, place_ref, emit)


def flash_call(kernel, operands, out_shape, scratch, total, rows, name, width=WIDTH):
    return pl.pallas_call(
        kernel,
        in_specs=[VMEM] * len(operands),
        out_specs=jax.tree.map(lambda _: VMEM, out_shape),
        out_shape=out_shape,
        scratch_shapes=scratch + [pltpu.VMEM((total, width), F32)] * 2,
        compiler_params=pltpu.CompilerParams(vmem_limit_bytes=24 << 20),
        cost_estimate=pl.CostEstimate(
            flops=4 * total * rows * 256, bytes_accessed=1 << 20, transcendentals=total * rows
        ),
        name=name,
    )(*operands)


def flash(held, filled, qt, state, fresh=()):
    total = -(-len(held) * FILL // 128) * 128
    if fresh:
        total = len(held) * FILL + fresh[0].shape[0]
    return flash_call(
        functools.partial(flash_kernel, list(held), bool(fresh)),
        [filled, qt, *held.values(), *fresh, *(state or ())],
        [jax.ShapeDtypeStruct((8, ROWS), F32), jax.ShapeDtypeStruct((ACC, ROWS), F32)],
        [
            pltpu.VMEM((total, 2 * HD), BF16),
            pltpu.VMEM((total, HD), BF16),
            pltpu.VMEM((ACC, total), BF16),
        ],
        total,
        ROWS,
        f"flash_{len(held)}",
    )


def flash_last(held, filled, qt, state, fresh):
    old = len(held) * FILL
    total = old + fresh[0].shape[0]
    part = jax.ShapeDtypeStruct((NSEG, CHUNK, TOK), BF16)
    twin_part, keys, vals_t = flash_call(
        functools.partial(twin_kernel, list(held)),
        [filled, qt, *held.values(), *fresh, *state],
        [part, jax.ShapeDtypeStruct((total, 2 * HD), BF16), jax.ShapeDtypeStruct((ACC, total), BF16)],
        [pltpu.VMEM((total, HD), BF16)],
        total,
        PART,
        "flash_twin",
    )
    own_part = flash_call(
        functools.partial(own_kernel, old), [qt, keys, vals_t, fresh[1], *state], part, [], total, PART, "flash_own"
    )
    return twin_part, own_part


def fresh_kernel(slots, *refs):
    blocks, share_ref, place_ref = refs[: len(slots)], refs[-2], refs[-1]
    first = lax.axis_index("seg") * SHARE
    for j, (slot, block) in enumerate(zip(slots, blocks)):
        rows = slice(j * SHARE, (j + 1) * SHARE)
        share_ref[rows, :] = block[pl.ds(pl.multiple_of(FILL + first, SHARE), SHARE), :]
        place = origin(slot) % NBLK * TOK + first
        place_ref[rows, :] = lax.broadcasted_iota(jnp.int32, (SHARE, TOK), 0) + place
    rest = share_ref.shape[0] - len(slots) * SHARE
    share_ref[len(slots) * SHARE :, :] = jnp.zeros((rest, 2 * HD), BF16)
    place_ref[len(slots) * SHARE :, :] = jnp.full((rest, TOK), NBLK * TOK, jnp.int32)


def fresh_rows(held, after_slots):
    old = after_slots * FILL
    size = -(-(old + len(held) * SHARE) // 128) * 128 - old
    return pl.pallas_call(
        functools.partial(fresh_kernel, list(held)),
        in_specs=[VMEM] * len(held),
        out_specs=[VMEM, VMEM],
        out_shape=[jax.ShapeDtypeStruct((size, 2 * HD), BF16), jax.ShapeDtypeStruct((size, TOK), jnp.int32)],
        compiler_params=pltpu.CompilerParams(vmem_limit_bytes=1 << 20),
        name="fresh_rows",
    )(*held.values())


def rows_kernel(slots, *refs):
    for slot, block in zip(slots, refs):
        pair = origin(slot) % NBLK // 2
        refs[-1][pl.ds(pl.multiple_of(pair * TOK, TOK), TOK), :] = block[FILL : FILL + TOK, :]


def new_rows(held):
    return pl.pallas_call(
        functools.partial(rows_kernel, list(held)),
        in_specs=[VMEM] * len(held),
        out_specs=VMEM,
        out_shape=jax.ShapeDtypeStruct((NBLK // 2 * TOK, 2 * HD), BF16),
        compiler_params=pltpu.CompilerParams(vmem_limit_bytes=1 << 20),
        name="new_rows",
    )(*held.values())


def pages_kernel(len_ref, owner_ref, cache_ref, own_ref, twin_ref, out_ref):
    blk = lax.axis_index("blk")
    device = lax.axis_index("seg") * NBLK + blk
    filled = len_ref[device]
    pages = owner_ref.shape[1]
    owned = jnp.broadcast_to((owner_ref[...] == device).astype(F32), (16, pages)).astype(BF16)
    before = (
        lax.broadcasted_iota(jnp.int32, (pages, pages), 0) < lax.broadcasted_iota(jnp.int32, (pages, pages), 1)
    ).astype(BF16)
    rank = jnp.dot(owned, before, preferred_element_type=F32)
    rank = jnp.where(owned > 0, rank, -1.0).astype(BF16)
    half = SLOTS // 2
    written, count = None, None
    for rows_ref, core in ((own_ref, blk % 2), (twin_ref, 1 - blk % 2)):
        rows = rows_ref.shape[0]
        row = lax.broadcasted_iota(jnp.int32, (pages, rows), 1)
        page = (row // TOK * 2 + core) * (TOK // PAGE) + row % TOK // PAGE
        spread = (page == lax.broadcasted_iota(jnp.int32, (pages, rows), 0)).astype(BF16)
        row_rank = jnp.dot(rank, spread, preferred_element_type=F32)[0:1].astype(jnp.int32)
        target = filled + row_rank * PAGE + lax.broadcasted_iota(jnp.int32, (1, rows), 1) % PAGE
        target = jnp.where(row_rank >= 0, target, -1)
        pick = (lax.broadcasted_iota(jnp.int32, (half, rows), 0) + half == target).astype(BF16)
        term = jnp.dot(pick, rows_ref[...], preferred_element_type=F32)
        written = term if written is None else written + term
        most = jnp.max(row_rank) + 1
        count = most if count is None else jnp.maximum(count, most)
    slot_id = lax.broadcasted_iota(jnp.int32, (half, 2 * HD), 0) + half
    is_new = (slot_id >= filled) & (slot_id < filled + count * PAGE)
    out_ref[0:half, :] = cache_ref[0:half, :]
    out_ref[half:SLOTS, :] = jnp.where(is_new, written.astype(BF16), cache_ref[half:SLOTS, :])


def write_pages(cache_len, page_owner, cache_kv, own_rows, twin_rows):
    return pl.pallas_call(
        pages_kernel,
        in_specs=[SMEM] + [VMEM] * 4,
        out_specs=VMEM,
        out_shape=jax.ShapeDtypeStruct(cache_kv.shape, BF16),
        compiler_params=pltpu.CompilerParams(vmem_limit_bytes=16 << 20),
        cost_estimate=pl.CostEstimate(flops=10**9, bytes_accessed=2 << 20, transcendentals=0),
        name="write_pages",
    )(cache_len, page_owner.reshape(1, -1), cache_kv, own_rows, twin_rows)


def pair_kernel(own_ref, twin_ref, out_ref, held, sems):
    copies = []
    for s in range(NSEG):
        sums = []
        for head in range(2):
            rows = slice(head * HD, (head + 1) * HD)
            own, twin = get_sums(own_ref, s, head), get_sums(twin_ref, s, head)
            top = jnp.maximum(own, twin)
            own_w, twin_w = jnp.exp2(own - top), jnp.exp2(twin - top)
            total = own_w + twin_w
            scale = 1.0 / total
            out = own_ref[s, rows, :].astype(F32) * (own_w * scale) + twin_ref[s, rows, :].astype(F32) * (twin_w * scale)
            held[s, rows, :] = out.astype(BF16)
            sums.append(top + jnp.log2(total))
        put_sums(held, s, sums)
        copies.append(pltpu.make_async_copy(held.at[s], out_ref.at[s], sems.at[s]))
        copies[-1].start()
    for copy in copies:
        copy.wait()


def merge_pair(own, twin):
    return pl.pallas_call(
        pair_kernel,
        in_specs=[VMEM, VMEM],
        out_specs=pl.BlockSpec(memory_space=pltpu.HBM),
        out_shape=jax.ShapeDtypeStruct(own.shape, BF16),
        scratch_shapes=[pltpu.VMEM(own.shape, BF16), pltpu.SemaphoreType.DMA((NSEG,))],
        compiler_params=pltpu.CompilerParams(vmem_limit_bytes=4 << 20),
        name="merge_pair",
    )(own, twin)


def merge_kernel(parts_ref, out_ref):
    for head in range(2):
        logs = [get_sums(parts_ref, s, head) for s in range(NSEG)]
        top = functools.reduce(jnp.maximum, logs)
        weights = [jnp.exp2(v - top) for v in logs]
        scale = 1.0 / functools.reduce(jnp.add, weights)
        out = None
        for s in range(NSEG):
            term = parts_ref[s, head * HD : (head + 1) * HD, :].astype(F32) * (weights[s] * scale)
            out = term if out is None else out + term
        out_ref[:, head * HD : (head + 1) * HD] = out.T.astype(BF16)


def merge(parts):
    return pl.pallas_call(
        merge_kernel,
        in_specs=[VMEM],
        out_specs=VMEM,
        out_shape=jax.ShapeDtypeStruct((TOK, 2 * HD), BF16),
        compiler_params=pltpu.CompilerParams(vmem_limit_bytes=4 << 20),
        name="merge",
    )(parts)


def shift(block, dx=0, flip_z=False, flip_core=False):
    return lax.ppermute(block, AXES, neighbours(-dx, flip_z, flip_core))


def after(values, other):
    return lax.optimization_barrier((values, other))


def scaled_queries(twin, own):
    return pl.pallas_call(
        queries_kernel,
        in_specs=[VMEM, VMEM],
        out_specs=VMEM,
        out_shape=jax.ShapeDtypeStruct((2 * HD, ROWS), BF16),
        compiler_params=pltpu.CompilerParams(vmem_limit_bytes=4 << 20),
        name="scaled_queries",
    )(twin, own)


def on_device(queries, new_kv, cache_kv, cache_len, page_owner):
    own, own_queries, filled = pack(cache_kv, new_kv, queries, cache_len)
    across = shift(own, flip_z=True)
    opposite = shift(own, 2)
    beside = {(1, False, False): shift(own, 1), (-1, False, False): shift(own, -1)}
    qt = scaled_queries(shift(own_queries, flip_core=True), own_queries)
    held = {(0, False, False): own}
    everything = dict(held)
    state = flash(held, filled, qt, None)

    across, state = after(across, state)
    far = {(1, True, False): shift(across, 1), (-1, True, False): shift(across, -1)}
    opposite, state = after(opposite, state)
    far[2, True, False] = shift(opposite, flip_z=True)
    held = {(0, True, False): across, (2, False, False): opposite}
    everything.update(held)
    state = flash(held, filled, qt, state)

    beside, state = after(beside, state)
    everything.update(beside)
    state = flash(beside, filled, qt, state, fresh_rows(everything, len(beside)))

    far, state = after(far, state)
    everything.update(far)
    rows = new_rows(everything)
    twin_rows = shift(rows, flip_core=True)
    twin_part, own_part = flash_last(far, filled, qt, state, fresh_rows(far, len(far)))
    part = merge_pair(own_part, shift(twin_part, flip_core=True))
    parts = lax.all_to_all(part, "seg", 0, 0)
    cache_out = write_pages(cache_len, page_owner, cache_kv, rows, twin_rows)
    return merge(parts), cache_out


def solution(mesh):
    placed = (P("blk", None), P("blk", None), P(("seg", "blk"), None), P(), P())
    return jax.shard_map(
        on_device,
        mesh=mesh,
        in_specs=placed,
        out_specs=(P("blk", "seg"), P(("seg", "blk"), None)),
        check_vma=False,
    )
```

```python
import functools

import jax
import jax.numpy as jnp
from jax import lax
from jax.experimental import pallas as pl
from jax.experimental.pallas import tpu as pltpu
from jax.sharding import PartitionSpec as P


F32 = jnp.float32
BF16 = jnp.bfloat16
HEADS = 16
HD = 128
TOK = 128
ROWS = 2 * HEADS * TOK
PART = HEADS * TOK
SLOTS = 512
LEAST = 256
FILL = 448
PAGE = 8
NSEG = 8
NBLK = 16
SHARE = TOK // NSEG
CHUNK = 2 * HD + 16
ACC = HD + 16
WIDTH = 512
NEG = -1e30
SCALE = 1.4426950408889634 / HD**0.5
VMEM = pl.BlockSpec(memory_space=pltpu.VMEM)
SMEM = pl.BlockSpec(memory_space=pltpu.SMEM)
AXES = ("seg", "blk")
SLOT_ORDER = [(dx, flip_z, False) for flip_z in (False, True) for dx in (0, 1, -1, 2)]


def neighbours(dx=0, flip_z=False, flip_core=False):
    pairs = []
    for here in range(NSEG * NBLK):
        seg, blk = divmod(here, NBLK)
        pairs.append((here, device_at(seg, blk, dx, flip_z, flip_core)))
    return pairs


def device_at(seg, blk, dx, flip_z, flip_core):
    y, z_lo = seg // 2, seg % 2
    z_hi, x, core = blk // 8, (blk // 2) % 4, blk % 2
    if flip_z:
        z_lo, z_hi = 1 - z_lo, 1 - z_hi
    if flip_core:
        core = 1 - core
    x = (x + dx) % 4
    return (y * 2 + z_lo) * NBLK + z_hi * 8 + x * 2 + core


def origin(slot):
    return device_at(lax.axis_index("seg"), lax.axis_index("blk"), *slot)


def queries_kernel(twin_ref, own_hbm, len_hbm, qt_ref, filled_ref, own_ref, len_ref, sems):
    own_copy = pltpu.make_async_copy(own_hbm, own_ref, sems.at[0])
    len_copy = pltpu.make_async_copy(len_hbm, len_ref, sems.at[1])
    own_copy.start()
    len_copy.start()
    for number, q_ref in enumerate((twin_ref, own_ref)):
        if number == 1:
            own_copy.wait()
        for h in range(HEADS):
            scaled = q_ref[:, h * HD : (h + 1) * HD].astype(F32).T * SCALE
            high = scaled.astype(BF16)
            cols = slice(number * PART + h * TOK, number * PART + (h + 1) * TOK)
            qt_ref[0:HD, cols] = high
            qt_ref[HD : 2 * HD, cols] = (scaled - high.astype(F32)).astype(BF16)
    len_copy.wait()
    for j, slot in enumerate(SLOT_ORDER):
        filled_ref[j : j + 1, :] = jnp.full((1, 128), len_ref[origin(slot)], jnp.int32)


def in_hbm(array):
    return pltpu.with_memory_space_constraint(array, pltpu.HBM)


def pack_kernel(cache_ref, new_ref, out_ref, sems):
    copies = [
        pltpu.make_async_copy(cache_ref.at[0:FILL], out_ref.at[0:FILL], sems.at[0]),
        pltpu.make_async_copy(new_ref, out_ref.at[FILL : FILL + TOK], sems.at[1]),
    ]
    for copy in copies:
        copy.start()
    for copy in copies:
        copy.wait()


def pack(cache_kv, new_kv):
    return pl.pallas_call(
        pack_kernel,
        in_specs=[pl.BlockSpec(memory_space=pltpu.HBM)] * 2,
        out_specs=VMEM,
        out_shape=jax.ShapeDtypeStruct((FILL + TOK, 2 * HD), BF16),
        scratch_shapes=[pltpu.SemaphoreType.DMA((2,))],
        compiler_params=pltpu.CompilerParams(vmem_limit_bytes=1 << 20),
        name="pack",
    )(in_hbm(cache_kv), in_hbm(new_kv))


def gather_keys(slots, blocks, fresh_ref, filled_ref, keys, vals, vals_t):
    total = keys.shape[0]
    spans = []
    for j, (slot, block) in enumerate(zip(slots, blocks)):
        filled = filled_ref[SLOT_ORDER.index(slot) : SLOT_ORDER.index(slot) + 1, :]
        start = j * FILL
        ok = lax.broadcasted_iota(jnp.int32, (FILL - LEAST, HD), 0) < filled - LEAST
        head = block[0:LEAST, 0:HD]
        tail = block[LEAST:FILL, 0:HD]
        tail = jnp.where(ok, tail, jnp.broadcast_to(head[0:1], tail.shape))
        value = block[LEAST:FILL, HD : 2 * HD]
        for lanes in (slice(0, HD), slice(HD, 2 * HD)):
            keys[start : start + LEAST, lanes] = head
            keys[start + LEAST : start + FILL, lanes] = tail
        vals[start : start + LEAST, :] = block[0:LEAST, HD : 2 * HD]
        vals[start + LEAST : start + FILL, :] = jnp.where(ok, value, jnp.zeros_like(value))
        spans.append((start, start + LEAST, start + FILL, start + filled))
    old = len(slots) * FILL
    if fresh_ref is not None:
        keys[old:total, 0:HD] = fresh_ref[:, 0:HD]
        keys[old:total, HD : 2 * HD] = fresh_ref[:, 0:HD]
        vals[old:total, :] = fresh_ref[:, HD : 2 * HD]
        spans.append((old, total, total, total))
    elif total > old:
        keys[old:total, :] = jnp.broadcast_to(keys[0:1, :], (total - old, 2 * HD))
        vals[old:total, :] = jnp.zeros((total - old, HD), BF16)
    for c in range(total // 128):
        low, high = c * 128, (c + 1) * 128
        vals_t[0:HD, low:high] = vals[low:high, :].T
        if any(start <= low and high <= sure for start, sure, _, _ in spans):
            vals_t[HD:ACC, low:high] = jnp.ones((ACC - HD, 128), BF16)
            continue
        lane = lax.broadcasted_iota(jnp.int32, (ACC - HD, 128), 1) + low
        one = None
        for start, _, stop, filled in spans:
            if start < high and stop > low:
                inside = (lane >= start) & (lane < filled)
                one = inside if one is None else one | inside
        vals_t[HD:ACC, low:high] = one.astype(F32).astype(BF16)


def flash_columns(columns, old, keys, vals_t, qt_ref, state, even_ref, odd_ref, place_ref, emit):
    total, width = even_ref.shape
    first, last = columns[0] // width, columns[1] // width

    def column_max(s):
        return jnp.max(s.reshape(s.shape[0] // 8, 8, width), axis=0)

    def score(r, scores_ref):
        cols = pl.ds(pl.multiple_of(r * width, width), width)
        s = jnp.dot(keys[...], qt_ref[:, cols], preferred_element_type=F32)
        if place_ref is None:
            scores_ref[...] = s
            return column_max(s)
        blk = lax.axis_index("blk")
        query_blk = jnp.where(r < PART // width, blk + 1 - blk % 2 * 2, blk)
        token = lax.broadcasted_iota(jnp.int32, place_ref.shape, 1)
        seen = place_ref[...] - query_blk * TOK <= token
        fresh = jnp.concatenate(
            [jnp.where(seen, s[old:total, i : i + TOK], NEG) for i in range(0, width, TOK)], axis=1
        )
        scores_ref[0:old] = s[0:old]
        scores_ref[old:total] = fresh
        return jnp.maximum(column_max(s[0:old]), column_max(fresh))

    def weigh(r, tops, scores_ref, next_ref):
        cols = pl.ds(pl.multiple_of(r * width, width), width)
        top = jnp.max(tops, axis=0, keepdims=True)
        if state is not None:
            top = jnp.maximum(top, state[0][0:1, cols])
        if next_ref is not None:
            tops = score(r + 1, next_ref)
        w = jnp.exp2(scores_ref[...] - top).astype(BF16)
        out = jnp.dot(vals_t[...], w, preferred_element_type=F32)
        if state is not None:
            out = out + state[1][:, cols] * jnp.exp2(state[0][0:1, cols] - top)
        emit(r - first, cols, out, top)
        return tops

    def two(i, tops, more=True):
        tops = weigh(first + 2 * i, tops, even_ref, odd_ref)
        return weigh(first + 2 * i + 1, tops, odd_ref, even_ref if more else None)

    pairs = (last - first) // 2
    trips = jnp.minimum(lax.axis_index("seg") + pairs - 1, pairs - 1)
    tops = lax.fori_loop(0, trips, two, score(first, even_ref))
    two(pairs - 1, tops, False)


def flash_kernel(slots, has_fresh, *refs):
    filled_ref, qt_ref = refs[0], refs[1]
    blocks, refs = refs[2 : 2 + len(slots)], refs[2 + len(slots) :]
    fresh_ref = place_ref = None
    if has_fresh:
        fresh_ref, place_ref, refs = refs[0], refs[1], refs[2:]
    state, (m_ref, acc_ref, keys, vals, vals_t, even_ref, odd_ref) = refs[:-7] or None, refs[-7:]
    gather_keys(slots, blocks, fresh_ref, filled_ref, keys, vals, vals_t)

    def emit(r, cols, out, top):
        acc_ref[:, cols] = out
        m_ref[:, cols] = jnp.broadcast_to(top, m_ref.at[:, cols].shape)

    old = len(slots) * FILL
    flash_columns((0, ROWS), old, keys, vals_t, qt_ref, state, even_ref, odd_ref, place_ref, emit)


def emit_part(part_ref, width):
    def emit(r, cols, out, top):
        total = out[HD : HD + 1]
        normal = (out[0:HD] * (1.0 / total)).astype(BF16)
        stats = top + jnp.log2(total)
        for i in range(0, width // TOK, 2):
            pair = r * (width // TOK // 2) + i // 2
            for j in range(2):
                part_ref[pair, j * HD : (j + 1) * HD, :] = normal[:, (i + j) * TOK : (i + j + 1) * TOK]
            put_sums(part_ref, pair, [stats[:, (i + j) * TOK : (i + j + 1) * TOK] for j in range(2)])

    return emit


def put_sums(part_ref, pair, rows):
    terms = []
    for row in rows:
        high = row.astype(BF16)
        rest = row - high.astype(F32)
        middle = rest.astype(BF16)
        terms += [high, middle, (rest - middle.astype(F32)).astype(BF16)]
    part_ref[pair, 2 * HD : CHUNK, :] = jnp.concatenate(terms + [terms[0]] * 10, axis=0)


def get_sums(part_ref, pair, head):
    three = [part_ref[pair, 2 * HD + head * 3 + i : 2 * HD + head * 3 + i + 1, :].astype(F32) for i in range(3)]
    return three[0] + three[1] + three[2]


def twin_kernel(slots, *refs):
    filled_ref, qt_ref = refs[0], refs[1]
    blocks, refs = refs[2 : 2 + len(slots)], refs[2 + len(slots) :]
    fresh_ref, place_ref, m_in, acc_in, part_ref, keys, vals_t, vals, even_ref, odd_ref = refs
    gather_keys(slots, blocks, fresh_ref, filled_ref, keys, vals, vals_t)
    emit = emit_part(part_ref, even_ref.shape[1])
    state, old = (m_in, acc_in), len(slots) * FILL
    flash_columns((0, PART), old, keys, vals_t, qt_ref, state, even_ref, odd_ref, place_ref, emit)


def own_kernel(old, qt_ref, keys, vals_t, place_ref, m_in, acc_in, part_ref, even_ref, odd_ref):
    emit = emit_part(part_ref, even_ref.shape[1])
    flash_columns((PART, ROWS), old, keys, vals_t, qt_ref, (m_in, acc_in), even_ref, odd_ref, place_ref, emit)


def flash_call(kernel, operands, out_shape, scratch, total, rows, name, width=WIDTH):
    return pl.pallas_call(
        kernel,
        in_specs=[VMEM] * len(operands),
        out_specs=jax.tree.map(lambda _: VMEM, out_shape),
        out_shape=out_shape,
        scratch_shapes=scratch + [pltpu.VMEM((total, width), F32)] * 2,
        compiler_params=pltpu.CompilerParams(vmem_limit_bytes=24 << 20),
        cost_estimate=pl.CostEstimate(
            flops=4 * total * rows * 256, bytes_accessed=1 << 20, transcendentals=total * rows
        ),
        name=name,
    )(*operands)


def flash(held, filled, qt, state, fresh=()):
    total = -(-len(held) * FILL // 128) * 128
    if fresh:
        total = len(held) * FILL + fresh[0].shape[0]
    return flash_call(
        functools.partial(flash_kernel, list(held), bool(fresh)),
        [filled, qt, *held.values(), *fresh, *(state or ())],
        [jax.ShapeDtypeStruct((8, ROWS), F32), jax.ShapeDtypeStruct((ACC, ROWS), F32)],
        [
            pltpu.VMEM((total, 2 * HD), BF16),
            pltpu.VMEM((total, HD), BF16),
            pltpu.VMEM((ACC, total), BF16),
        ],
        total,
        ROWS,
        f"flash_{len(held)}",
    )


def flash_last(held, filled, qt, state, fresh):
    old = len(held) * FILL
    total = old + fresh[0].shape[0]
    part = jax.ShapeDtypeStruct((NSEG, CHUNK, TOK), BF16)
    twin_part, keys, vals_t = flash_call(
        functools.partial(twin_kernel, list(held)),
        [filled, qt, *held.values(), *fresh, *state],
        [part, jax.ShapeDtypeStruct((total, 2 * HD), BF16), jax.ShapeDtypeStruct((ACC, total), BF16)],
        [pltpu.VMEM((total, HD), BF16)],
        total,
        PART,
        "flash_twin",
    )
    own_part = flash_call(
        functools.partial(own_kernel, old), [qt, keys, vals_t, fresh[1], *state], part, [], total, PART, "flash_own"
    )
    return twin_part, own_part


def fresh_kernel(slots, *refs):
    blocks, share_ref, place_ref = refs[: len(slots)], refs[-2], refs[-1]
    first = lax.axis_index("seg") * SHARE
    for j, (slot, block) in enumerate(zip(slots, blocks)):
        rows = slice(j * SHARE, (j + 1) * SHARE)
        share_ref[rows, :] = block[pl.ds(pl.multiple_of(FILL + first, SHARE), SHARE), :]
        place = origin(slot) % NBLK * TOK + first
        place_ref[rows, :] = lax.broadcasted_iota(jnp.int32, (SHARE, TOK), 0) + place
    rest = share_ref.shape[0] - len(slots) * SHARE
    share_ref[len(slots) * SHARE :, :] = jnp.zeros((rest, 2 * HD), BF16)
    place_ref[len(slots) * SHARE :, :] = jnp.full((rest, TOK), NBLK * TOK, jnp.int32)


def fresh_rows(held, after_slots):
    old = after_slots * FILL
    size = -(-(old + len(held) * SHARE) // 128) * 128 - old
    return pl.pallas_call(
        functools.partial(fresh_kernel, list(held)),
        in_specs=[VMEM] * len(held),
        out_specs=[VMEM, VMEM],
        out_shape=[jax.ShapeDtypeStruct((size, 2 * HD), BF16), jax.ShapeDtypeStruct((size, TOK), jnp.int32)],
        compiler_params=pltpu.CompilerParams(vmem_limit_bytes=1 << 20),
        name="fresh_rows",
    )(*held.values())


def rows_kernel(slots, *refs):
    for slot, block in zip(slots, refs):
        pair = origin(slot) % NBLK // 2
        refs[-1][pl.ds(pl.multiple_of(pair * TOK, TOK), TOK), :] = block[FILL : FILL + TOK, :]


def new_rows(held):
    return pl.pallas_call(
        functools.partial(rows_kernel, list(held)),
        in_specs=[VMEM] * len(held),
        out_specs=VMEM,
        out_shape=jax.ShapeDtypeStruct((NBLK // 2 * TOK, 2 * HD), BF16),
        compiler_params=pltpu.CompilerParams(vmem_limit_bytes=1 << 20),
        name="new_rows",
    )(*held.values())


def pages_kernel(len_ref, owner_ref, cache_ref, own_ref, twin_ref, out_ref):
    blk = lax.axis_index("blk")
    device = lax.axis_index("seg") * NBLK + blk
    filled = len_ref[device]
    pages = owner_ref.shape[1]
    owned = jnp.broadcast_to((owner_ref[...] == device).astype(F32), (16, pages)).astype(BF16)
    before = (
        lax.broadcasted_iota(jnp.int32, (pages, pages), 0) < lax.broadcasted_iota(jnp.int32, (pages, pages), 1)
    ).astype(BF16)
    rank = jnp.dot(owned, before, preferred_element_type=F32)
    rank = jnp.where(owned > 0, rank, -1.0).astype(BF16)
    half = SLOTS // 2
    written, count = None, None
    for rows_ref, core in ((own_ref, blk % 2), (twin_ref, 1 - blk % 2)):
        rows = rows_ref.shape[0]
        row = lax.broadcasted_iota(jnp.int32, (pages, rows), 1)
        page = (row // TOK * 2 + core) * (TOK // PAGE) + row % TOK // PAGE
        spread = (page == lax.broadcasted_iota(jnp.int32, (pages, rows), 0)).astype(BF16)
        row_rank = jnp.dot(rank, spread, preferred_element_type=F32)[0:1].astype(jnp.int32)
        target = filled + row_rank * PAGE + lax.broadcasted_iota(jnp.int32, (1, rows), 1) % PAGE
        target = jnp.where(row_rank >= 0, target, -1)
        pick = (lax.broadcasted_iota(jnp.int32, (half, rows), 0) + half == target).astype(BF16)
        term = jnp.dot(pick, rows_ref[...], preferred_element_type=F32)
        written = term if written is None else written + term
        most = jnp.max(row_rank) + 1
        count = most if count is None else jnp.maximum(count, most)
    slot_id = lax.broadcasted_iota(jnp.int32, (half, 2 * HD), 0) + half
    is_new = (slot_id >= filled) & (slot_id < filled + count * PAGE)
    out_ref[0:half, :] = cache_ref[0:half, :]
    out_ref[half:SLOTS, :] = jnp.where(is_new, written.astype(BF16), cache_ref[half:SLOTS, :])


def write_pages(cache_len, page_owner, cache_kv, own_rows, twin_rows):
    return pl.pallas_call(
        pages_kernel,
        in_specs=[SMEM] + [VMEM] * 4,
        out_specs=VMEM,
        out_shape=jax.ShapeDtypeStruct(cache_kv.shape, BF16),
        compiler_params=pltpu.CompilerParams(vmem_limit_bytes=16 << 20),
        cost_estimate=pl.CostEstimate(flops=10**9, bytes_accessed=2 << 20, transcendentals=0),
        name="write_pages",
    )(cache_len, page_owner.reshape(1, -1), cache_kv, own_rows, twin_rows)


def pair_kernel(own_ref, twin_ref, out_ref, held, sems):
    copies = []
    for s in range(NSEG):
        sums = []
        for head in range(2):
            rows = slice(head * HD, (head + 1) * HD)
            own, twin = get_sums(own_ref, s, head), get_sums(twin_ref, s, head)
            top = jnp.maximum(own, twin)
            own_w, twin_w = jnp.exp2(own - top), jnp.exp2(twin - top)
            total = own_w + twin_w
            scale = 1.0 / total
            out = own_ref[s, rows, :].astype(F32) * (own_w * scale) + twin_ref[s, rows, :].astype(F32) * (twin_w * scale)
            held[s, rows, :] = out.astype(BF16)
            sums.append(top + jnp.log2(total))
        put_sums(held, s, sums)
        copies.append(pltpu.make_async_copy(held.at[s], out_ref.at[s], sems.at[s]))
        copies[-1].start()
    for copy in copies:
        copy.wait()


def merge_pair(own, twin):
    return pl.pallas_call(
        pair_kernel,
        in_specs=[VMEM, VMEM],
        out_specs=pl.BlockSpec(memory_space=pltpu.HBM),
        out_shape=jax.ShapeDtypeStruct(own.shape, BF16),
        scratch_shapes=[pltpu.VMEM(own.shape, BF16), pltpu.SemaphoreType.DMA((NSEG,))],
        compiler_params=pltpu.CompilerParams(vmem_limit_bytes=4 << 20),
        name="merge_pair",
    )(own, twin)


def merge_kernel(parts_ref, out_ref):
    for head in range(2):
        logs = [get_sums(parts_ref, s, head) for s in range(NSEG)]
        top = functools.reduce(jnp.maximum, logs)
        weights = [jnp.exp2(v - top) for v in logs]
        scale = 1.0 / functools.reduce(jnp.add, weights)
        out = None
        for s in range(NSEG):
            term = parts_ref[s, head * HD : (head + 1) * HD, :].astype(F32) * (weights[s] * scale)
            out = term if out is None else out + term
        out_ref[:, head * HD : (head + 1) * HD] = out.T.astype(BF16)


def merge(parts):
    return pl.pallas_call(
        merge_kernel,
        in_specs=[VMEM],
        out_specs=VMEM,
        out_shape=jax.ShapeDtypeStruct((TOK, 2 * HD), BF16),
        compiler_params=pltpu.CompilerParams(vmem_limit_bytes=4 << 20),
        name="merge",
    )(parts)


def shift(block, dx=0, flip_z=False, flip_core=False):
    return lax.ppermute(block, AXES, neighbours(-dx, flip_z, flip_core))


def after(values, other):
    return lax.optimization_barrier((values, other))


def scaled_queries(twin, own, cache_len):
    return pl.pallas_call(
        queries_kernel,
        in_specs=[VMEM] + [pl.BlockSpec(memory_space=pltpu.HBM)] * 2,
        out_specs=[VMEM, VMEM],
        out_shape=[
            jax.ShapeDtypeStruct((2 * HD, ROWS), BF16),
            jax.ShapeDtypeStruct((len(SLOT_ORDER), 128), jnp.int32),
        ],
        scratch_shapes=[
            pltpu.VMEM(own.shape, BF16),
            pltpu.SMEM(cache_len.shape, jnp.int32),
            pltpu.SemaphoreType.DMA((2,)),
        ],
        compiler_params=pltpu.CompilerParams(vmem_limit_bytes=4 << 20),
        name="scaled_queries",
    )(twin, in_hbm(own), in_hbm(cache_len))


def on_device(queries, new_kv, cache_kv, cache_len, page_owner):
    own = pack(cache_kv, new_kv)
    across = shift(own, flip_z=True)
    opposite = shift(own, 2)
    beside = {(1, False, False): shift(own, 1), (-1, False, False): shift(own, -1)}
    twin_queries = shift(after(queries, own)[0], flip_core=True)
    qt, filled = scaled_queries(twin_queries, queries, cache_len)
    held = {(0, False, False): own}
    everything = dict(held)
    state = flash(held, filled, qt, None)

    across, state = after(across, state)
    far = {(1, True, False): shift(across, 1), (-1, True, False): shift(across, -1)}
    opposite, state = after(opposite, state)
    far[2, True, False] = shift(opposite, flip_z=True)
    held = {(0, True, False): across, (2, False, False): opposite}
    everything.update(held)
    state = flash(held, filled, qt, state)

    beside, state = after(beside, state)
    everything.update(beside)
    state = flash(beside, filled, qt, state, fresh_rows(everything, len(beside)))

    far, state = after(far, state)
    everything.update(far)
    rows = new_rows(everything)
    twin_rows = shift(rows, flip_core=True)
    twin_part, own_part = flash_last(far, filled, qt, state, fresh_rows(far, len(far)))
    part = merge_pair(own_part, shift(twin_part, flip_core=True))
    parts = lax.all_to_all(part, "seg", 0, 0)
    cache_out = write_pages(cache_len, page_owner, cache_kv, rows, twin_rows)
    return merge(parts), cache_out


def solution(mesh):
    placed = (P("blk", None), P("blk", None), P(("seg", "blk"), None), P(), P())
    return jax.shard_map(
        on_device,
        mesh=mesh,
        in_specs=placed,
        out_specs=(P("blk", "seg"), P(("seg", "blk"), None)),
        check_vma=False,
    )
```

```python
import functools

import jax
import jax.numpy as jnp
from jax import lax
from jax.experimental import pallas as pl
from jax.experimental.pallas import tpu as pltpu
from jax.sharding import PartitionSpec as P


F32 = jnp.float32
BF16 = jnp.bfloat16
HEADS = 16
HD = 128
TOK = 128
ROWS = 2 * HEADS * TOK
PART = HEADS * TOK
SLOTS = 512
LEAST = 256
FILL = 448
PAGE = 8
NSEG = 8
NBLK = 16
SHARE = TOK // NSEG
CHUNK = 2 * HD + 16
ACC = HD + 16
WIDTH = 512
NEG = -1e30
SCALE = 1.4426950408889634 / HD**0.5
VMEM = pl.BlockSpec(memory_space=pltpu.VMEM)
SMEM = pl.BlockSpec(memory_space=pltpu.SMEM)
AXES = ("seg", "blk")
SLOT_ORDER = [(dx, flip_z, False) for flip_z in (False, True) for dx in (0, 1, 3, 2)]


def neighbours(dx=0, flip_z=False, flip_core=False):
    pairs = []
    for here in range(NSEG * NBLK):
        seg, blk = divmod(here, NBLK)
        pairs.append((here, device_at(seg, blk, dx, flip_z, flip_core)))
    return pairs


def device_at(seg, blk, dx, flip_z, flip_core):
    y, z_lo = seg // 2, seg % 2
    z_hi, x, core = blk // 8, (blk // 2) % 4, blk % 2
    if flip_z:
        z_lo, z_hi = 1 - z_lo, 1 - z_hi
    if flip_core:
        core = 1 - core
    x = x ^ dx
    return (y * 2 + z_lo) * NBLK + z_hi * 8 + x * 2 + core


def origin(slot):
    return device_at(lax.axis_index("seg"), lax.axis_index("blk"), *slot)


def queries_kernel(twin_ref, own_hbm, len_hbm, qt_ref, filled_ref, own_ref, len_ref, sems):
    own_copy = pltpu.make_async_copy(own_hbm, own_ref, sems.at[0])
    len_copy = pltpu.make_async_copy(len_hbm, len_ref, sems.at[1])
    own_copy.start()
    len_copy.start()
    for number, q_ref in enumerate((twin_ref, own_ref)):
        if number == 1:
            own_copy.wait()
        for h in range(HEADS):
            scaled = q_ref[:, h * HD : (h + 1) * HD].astype(F32).T * SCALE
            high = scaled.astype(BF16)
            cols = slice(number * PART + h * TOK, number * PART + (h + 1) * TOK)
            qt_ref[0:HD, cols] = high
            qt_ref[HD : 2 * HD, cols] = (scaled - high.astype(F32)).astype(BF16)
    len_copy.wait()
    for j, slot in enumerate(SLOT_ORDER):
        filled_ref[j : j + 1, :] = jnp.full((1, 128), len_ref[origin(slot)], jnp.int32)


def in_hbm(array):
    return pltpu.with_memory_space_constraint(array, pltpu.HBM)


def pack_kernel(cache_ref, new_ref, out_ref, sems):
    copies = [
        pltpu.make_async_copy(cache_ref.at[0:FILL], out_ref.at[0:FILL], sems.at[0]),
        pltpu.make_async_copy(new_ref, out_ref.at[FILL : FILL + TOK], sems.at[1]),
    ]
    for copy in copies:
        copy.start()
    for copy in copies:
        copy.wait()


def pack(cache_kv, new_kv):
    return pl.pallas_call(
        pack_kernel,
        in_specs=[pl.BlockSpec(memory_space=pltpu.HBM)] * 2,
        out_specs=VMEM,
        out_shape=jax.ShapeDtypeStruct((FILL + TOK, 2 * HD), BF16),
        scratch_shapes=[pltpu.SemaphoreType.DMA((2,))],
        compiler_params=pltpu.CompilerParams(vmem_limit_bytes=1 << 20),
        name="pack",
    )(in_hbm(cache_kv), in_hbm(new_kv))


def gather_keys(slots, blocks, fresh_ref, filled_ref, keys, vals, vals_t):
    total = keys.shape[0]
    spans = []
    for j, (slot, block) in enumerate(zip(slots, blocks)):
        filled = filled_ref[SLOT_ORDER.index(slot) : SLOT_ORDER.index(slot) + 1, :]
        start = j * FILL
        ok = lax.broadcasted_iota(jnp.int32, (FILL - LEAST, HD), 0) < filled - LEAST
        head = block[0:LEAST, 0:HD]
        tail = block[LEAST:FILL, 0:HD]
        tail = jnp.where(ok, tail, jnp.broadcast_to(head[0:1], tail.shape))
        value = block[LEAST:FILL, HD : 2 * HD]
        for lanes in (slice(0, HD), slice(HD, 2 * HD)):
            keys[start : start + LEAST, lanes] = head
            keys[start + LEAST : start + FILL, lanes] = tail
        vals[start : start + LEAST, :] = block[0:LEAST, HD : 2 * HD]
        vals[start + LEAST : start + FILL, :] = jnp.where(ok, value, jnp.zeros_like(value))
        spans.append((start, start + LEAST, start + FILL, start + filled))
    old = len(slots) * FILL
    if fresh_ref is not None:
        keys[old:total, 0:HD] = fresh_ref[:, 0:HD]
        keys[old:total, HD : 2 * HD] = fresh_ref[:, 0:HD]
        vals[old:total, :] = fresh_ref[:, HD : 2 * HD]
        spans.append((old, total, total, total))
    elif total > old:
        keys[old:total, :] = jnp.broadcast_to(keys[0:1, :], (total - old, 2 * HD))
        vals[old:total, :] = jnp.zeros((total - old, HD), BF16)
    for c in range(total // 128):
        low, high = c * 128, (c + 1) * 128
        vals_t[0:HD, low:high] = vals[low:high, :].T
        if any(start <= low and high <= sure for start, sure, _, _ in spans):
            vals_t[HD:ACC, low:high] = jnp.ones((ACC - HD, 128), BF16)
            continue
        lane = lax.broadcasted_iota(jnp.int32, (ACC - HD, 128), 1) + low
        one = None
        for start, _, stop, filled in spans:
            if start < high and stop > low:
                inside = (lane >= start) & (lane < filled)
                one = inside if one is None else one | inside
        vals_t[HD:ACC, low:high] = one.astype(F32).astype(BF16)


def flash_columns(
    columns, old, keys, vals_t, qt_ref, state, even_ref, odd_ref, place_ref, emit, given=None, handed=None
):
    total, width = even_ref.shape
    first, last = columns[0] // width, columns[1] // width

    def column_max(s):
        return jnp.max(s.reshape(s.shape[0] // 8, 8, width), axis=0)

    def score(r, scores_ref):
        cols = pl.ds(pl.multiple_of(r * width, width), width)
        s = jnp.dot(keys[...], qt_ref[:, cols], preferred_element_type=F32)
        if place_ref is None:
            scores_ref[...] = s
            return column_max(s)
        blk = lax.axis_index("blk")
        query_blk = jnp.where(r < PART // width, blk + 1 - blk % 2 * 2, blk)
        token = lax.broadcasted_iota(jnp.int32, place_ref.shape, 1)
        seen = place_ref[...] - query_blk * TOK <= token
        fresh = jnp.concatenate(
            [jnp.where(seen, s[old:total, i : i + TOK], NEG) for i in range(0, width, TOK)], axis=1
        )
        scores_ref[0:old] = s[0:old]
        scores_ref[old:total] = fresh
        return jnp.maximum(column_max(s[0:old]), column_max(fresh))

    def weigh(r, tops, scores_ref, next_ref):
        cols = pl.ds(pl.multiple_of(r * width, width), width)
        top = jnp.max(tops, axis=0, keepdims=True)
        if state is not None:
            top = jnp.maximum(top, state[0][0:1, cols])
        if next_ref is not None:
            tops = score(r + 1, next_ref)
        w = jnp.exp2(scores_ref[...] - top).astype(BF16)
        out = jnp.dot(vals_t[...], w, preferred_element_type=F32)
        if state is not None:
            out = out + state[1][:, cols] * jnp.exp2(state[0][0:1, cols] - top)
        emit(r - first, cols, out, top)
        return tops

    def two(i, tops, here_ref, next_ref):
        tops = weigh(first + 2 * i, tops, here_ref, odd_ref)
        return weigh(first + 2 * i + 1, tops, odd_ref, next_ref)

    pairs = (last - first) // 2
    here_ref, tops = (even_ref, score(first, even_ref)) if given is None else (given[0], given[1][...])
    trips = jnp.minimum(lax.axis_index("seg") + pairs - 1, pairs - 1)
    tops = lax.fori_loop(0, trips, lambda i, tops: two(i, tops, here_ref, even_ref), tops)
    tops = two(pairs - 1, tops, even_ref, None if handed is None else handed[0])
    if handed is not None:
        handed[1][...] = tops


def flash_kernel(slots, has_fresh, *refs):
    filled_ref, qt_ref = refs[0], refs[1]
    blocks, refs = refs[2 : 2 + len(slots)], refs[2 + len(slots) :]
    fresh_ref = place_ref = None
    if has_fresh:
        fresh_ref, place_ref, refs = refs[0], refs[1], refs[2:]
    state, (m_ref, acc_ref, keys, vals, vals_t, even_ref, odd_ref) = refs[:-7] or None, refs[-7:]
    gather_keys(slots, blocks, fresh_ref, filled_ref, keys, vals, vals_t)

    def emit(r, cols, out, top):
        acc_ref[:, cols] = out
        m_ref[:, cols] = jnp.broadcast_to(top, m_ref.at[:, cols].shape)

    old = len(slots) * FILL
    flash_columns((0, ROWS), old, keys, vals_t, qt_ref, state, even_ref, odd_ref, place_ref, emit)


def emit_part(part_ref, width):
    def emit(r, cols, out, top):
        total = out[HD : HD + 1]
        normal = (out[0:HD] * (1.0 / total)).astype(BF16)
        stats = top + jnp.log2(total)
        for i in range(0, width // TOK, 2):
            pair = r * (width // TOK // 2) + i // 2
            for j in range(2):
                part_ref[pair, j * HD : (j + 1) * HD, :] = normal[:, (i + j) * TOK : (i + j + 1) * TOK]
            put_sums(part_ref, pair, [stats[:, (i + j) * TOK : (i + j + 1) * TOK] for j in range(2)])

    return emit


def put_sums(part_ref, pair, rows):
    terms = []
    for row in rows:
        high = row.astype(BF16)
        rest = row - high.astype(F32)
        middle = rest.astype(BF16)
        terms += [high, middle, (rest - middle.astype(F32)).astype(BF16)]
    part_ref[pair, 2 * HD : CHUNK, :] = jnp.concatenate(terms + [terms[0]] * 10, axis=0)


def get_sums(part_ref, pair, head):
    three = [part_ref[pair, 2 * HD + head * 3 + i : 2 * HD + head * 3 + i + 1, :].astype(F32) for i in range(3)]
    return three[0] + three[1] + three[2]


def twin_kernel(slots, *refs):
    filled_ref, qt_ref = refs[0], refs[1]
    blocks, refs = refs[2 : 2 + len(slots)], refs[2 + len(slots) :]
    fresh_ref, place_ref, m_in, acc_in, part_ref, keys, vals_t, scores_ref, tops_ref, vals, even_ref, odd_ref = refs
    gather_keys(slots, blocks, fresh_ref, filled_ref, keys, vals, vals_t)
    emit = emit_part(part_ref, even_ref.shape[1])
    flash_columns(
        (0, PART),
        len(slots) * FILL,
        keys,
        vals_t,
        qt_ref,
        (m_in, acc_in),
        even_ref,
        odd_ref,
        place_ref,
        emit,
        handed=(scores_ref, tops_ref),
    )


def own_kernel(old, qt_ref, keys, vals_t, scores_ref, tops_ref, place_ref, m_in, acc_in, part_ref, even_ref, odd_ref):
    emit = emit_part(part_ref, even_ref.shape[1])
    flash_columns(
        (PART, ROWS),
        old,
        keys,
        vals_t,
        qt_ref,
        (m_in, acc_in),
        even_ref,
        odd_ref,
        place_ref,
        emit,
        given=(scores_ref, tops_ref),
    )


def flash_call(kernel, operands, out_shape, scratch, total, rows, name, width=WIDTH):
    return pl.pallas_call(
        kernel,
        in_specs=[VMEM] * len(operands),
        out_specs=jax.tree.map(lambda _: VMEM, out_shape),
        out_shape=out_shape,
        scratch_shapes=scratch + [pltpu.VMEM((total, width), F32)] * 2,
        compiler_params=pltpu.CompilerParams(vmem_limit_bytes=24 << 20),
        cost_estimate=pl.CostEstimate(
            flops=4 * total * rows * 256, bytes_accessed=1 << 20, transcendentals=total * rows
        ),
        name=name,
    )(*operands)


def flash(held, filled, qt, state, fresh=()):
    total = -(-len(held) * FILL // 128) * 128
    if fresh:
        total = len(held) * FILL + fresh[0].shape[0]
    return flash_call(
        functools.partial(flash_kernel, list(held), bool(fresh)),
        [filled, qt, *held.values(), *fresh, *(state or ())],
        [jax.ShapeDtypeStruct((8, ROWS), F32), jax.ShapeDtypeStruct((ACC, ROWS), F32)],
        [
            pltpu.VMEM((total, 2 * HD), BF16),
            pltpu.VMEM((total, HD), BF16),
            pltpu.VMEM((ACC, total), BF16),
        ],
        total,
        ROWS,
        f"flash_{len(held)}",
    )


def flash_last(held, filled, qt, state, fresh):
    old = len(held) * FILL
    total = old + fresh[0].shape[0]
    part = jax.ShapeDtypeStruct((NSEG, CHUNK, TOK), BF16)
    twin_part, *handed = flash_call(
        functools.partial(twin_kernel, list(held)),
        [filled, qt, *held.values(), *fresh, *state],
        [
            part,
            jax.ShapeDtypeStruct((total, 2 * HD), BF16),
            jax.ShapeDtypeStruct((ACC, total), BF16),
            jax.ShapeDtypeStruct((total, WIDTH), F32),
            jax.ShapeDtypeStruct((8, WIDTH), F32),
        ],
        [pltpu.VMEM((total, HD), BF16)],
        total,
        PART,
        "flash_twin",
    )
    own_part = flash_call(
        functools.partial(own_kernel, old), [qt, *handed, fresh[1], *state], part, [], total, PART, "flash_own"
    )
    return twin_part, own_part


def fresh_kernel(slots, *refs):
    blocks, share_ref, place_ref = refs[: len(slots)], refs[-2], refs[-1]
    first = lax.axis_index("seg") * SHARE
    for j, (slot, block) in enumerate(zip(slots, blocks)):
        rows = slice(j * SHARE, (j + 1) * SHARE)
        share_ref[rows, :] = block[pl.ds(pl.multiple_of(FILL + first, SHARE), SHARE), :]
        place = origin(slot) % NBLK * TOK + first
        place_ref[rows, :] = lax.broadcasted_iota(jnp.int32, (SHARE, TOK), 0) + place
    rest = share_ref.shape[0] - len(slots) * SHARE
    share_ref[len(slots) * SHARE :, :] = jnp.zeros((rest, 2 * HD), BF16)
    place_ref[len(slots) * SHARE :, :] = jnp.full((rest, TOK), NBLK * TOK, jnp.int32)


def fresh_rows(held, after_slots):
    old = after_slots * FILL
    size = -(-(old + len(held) * SHARE) // 128) * 128 - old
    return pl.pallas_call(
        functools.partial(fresh_kernel, list(held)),
        in_specs=[VMEM] * len(held),
        out_specs=[VMEM, VMEM],
        out_shape=[jax.ShapeDtypeStruct((size, 2 * HD), BF16), jax.ShapeDtypeStruct((size, TOK), jnp.int32)],
        compiler_params=pltpu.CompilerParams(vmem_limit_bytes=1 << 20),
        name="fresh_rows",
    )(*held.values())


def rows_kernel(slots, *refs):
    for slot, block in zip(slots, refs):
        pair = origin(slot) % NBLK // 2
        refs[-1][pl.ds(pl.multiple_of(pair * TOK, TOK), TOK), :] = block[FILL : FILL + TOK, :]


def new_rows(held):
    return pl.pallas_call(
        functools.partial(rows_kernel, list(held)),
        in_specs=[VMEM] * len(held),
        out_specs=VMEM,
        out_shape=jax.ShapeDtypeStruct((NBLK // 2 * TOK, 2 * HD), BF16),
        compiler_params=pltpu.CompilerParams(vmem_limit_bytes=1 << 20),
        name="new_rows",
    )(*held.values())


def pages_kernel(len_ref, owner_ref, cache_ref, own_ref, twin_ref, out_ref):
    blk = lax.axis_index("blk")
    device = lax.axis_index("seg") * NBLK + blk
    filled = len_ref[device]
    pages = owner_ref.shape[1]
    owned = jnp.broadcast_to((owner_ref[...] == device).astype(F32), (16, pages)).astype(BF16)
    before = (
        lax.broadcasted_iota(jnp.int32, (pages, pages), 0) < lax.broadcasted_iota(jnp.int32, (pages, pages), 1)
    ).astype(BF16)
    rank = jnp.dot(owned, before, preferred_element_type=F32)
    rank = jnp.where(owned > 0, rank, -1.0).astype(BF16)
    half = SLOTS // 2
    written, count = None, None
    for rows_ref, core in ((own_ref, blk % 2), (twin_ref, 1 - blk % 2)):
        rows = rows_ref.shape[0]
        row = lax.broadcasted_iota(jnp.int32, (pages, rows), 1)
        page = (row // TOK * 2 + core) * (TOK // PAGE) + row % TOK // PAGE
        spread = (page == lax.broadcasted_iota(jnp.int32, (pages, rows), 0)).astype(BF16)
        row_rank = jnp.dot(rank, spread, preferred_element_type=F32)[0:1].astype(jnp.int32)
        target = filled + row_rank * PAGE + lax.broadcasted_iota(jnp.int32, (1, rows), 1) % PAGE
        target = jnp.where(row_rank >= 0, target, -1)
        pick = (lax.broadcasted_iota(jnp.int32, (half, rows), 0) + half == target).astype(BF16)
        term = jnp.dot(pick, rows_ref[...], preferred_element_type=F32)
        written = term if written is None else written + term
        most = jnp.max(row_rank) + 1
        count = most if count is None else jnp.maximum(count, most)
    slot_id = lax.broadcasted_iota(jnp.int32, (half, 2 * HD), 0) + half
    is_new = (slot_id >= filled) & (slot_id < filled + count * PAGE)
    out_ref[0:half, :] = cache_ref[0:half, :]
    out_ref[half:SLOTS, :] = jnp.where(is_new, written.astype(BF16), cache_ref[half:SLOTS, :])


def write_pages(cache_len, page_owner, cache_kv, own_rows, twin_rows):
    return pl.pallas_call(
        pages_kernel,
        in_specs=[SMEM] + [VMEM] * 4,
        out_specs=VMEM,
        out_shape=jax.ShapeDtypeStruct(cache_kv.shape, BF16),
        compiler_params=pltpu.CompilerParams(vmem_limit_bytes=16 << 20),
        cost_estimate=pl.CostEstimate(flops=10**9, bytes_accessed=2 << 20, transcendentals=0),
        name="write_pages",
    )(cache_len, page_owner.reshape(1, -1), cache_kv, own_rows, twin_rows)


def pair_kernel(own_ref, twin_ref, out_ref, held, sems):
    copies = []
    for s in range(NSEG):
        sums = []
        for head in range(2):
            rows = slice(head * HD, (head + 1) * HD)
            own, twin = get_sums(own_ref, s, head), get_sums(twin_ref, s, head)
            top = jnp.maximum(own, twin)
            own_w, twin_w = jnp.exp2(own - top), jnp.exp2(twin - top)
            total = own_w + twin_w
            scale = 1.0 / total
            out = own_ref[s, rows, :].astype(F32) * (own_w * scale) + twin_ref[s, rows, :].astype(F32) * (twin_w * scale)
            held[s, rows, :] = out.astype(BF16)
            sums.append(top + jnp.log2(total))
        put_sums(held, s, sums)
        copies.append(pltpu.make_async_copy(held.at[s], out_ref.at[s], sems.at[s]))
        copies[-1].start()
    for copy in copies:
        copy.wait()


def merge_pair(own, twin):
    return pl.pallas_call(
        pair_kernel,
        in_specs=[VMEM, VMEM],
        out_specs=pl.BlockSpec(memory_space=pltpu.HBM),
        out_shape=jax.ShapeDtypeStruct(own.shape, BF16),
        scratch_shapes=[pltpu.VMEM(own.shape, BF16), pltpu.SemaphoreType.DMA((NSEG,))],
        compiler_params=pltpu.CompilerParams(vmem_limit_bytes=4 << 20),
        name="merge_pair",
    )(own, twin)


def merge_kernel(parts_ref, out_ref):
    for head in range(2):
        logs = [get_sums(parts_ref, s, head) for s in range(NSEG)]
        top = functools.reduce(jnp.maximum, logs)
        weights = [jnp.exp2(v - top) for v in logs]
        scale = 1.0 / functools.reduce(jnp.add, weights)
        out = None
        for s in range(NSEG):
            term = parts_ref[s, head * HD : (head + 1) * HD, :].astype(F32) * (weights[s] * scale)
            out = term if out is None else out + term
        out_ref[:, head * HD : (head + 1) * HD] = out.T.astype(BF16)


def merge(parts):
    return pl.pallas_call(
        merge_kernel,
        in_specs=[VMEM],
        out_specs=VMEM,
        out_shape=jax.ShapeDtypeStruct((TOK, 2 * HD), BF16),
        compiler_params=pltpu.CompilerParams(vmem_limit_bytes=4 << 20),
        name="merge",
    )(parts)


def shift(block, dx=0, flip_z=False, flip_core=False):
    return lax.ppermute(block, AXES, neighbours(dx, flip_z, flip_core))


def after(values, other):
    return lax.optimization_barrier((values, other))


def scaled_queries(twin, own, cache_len):
    return pl.pallas_call(
        queries_kernel,
        in_specs=[VMEM] + [pl.BlockSpec(memory_space=pltpu.HBM)] * 2,
        out_specs=[VMEM, VMEM],
        out_shape=[
            jax.ShapeDtypeStruct((2 * HD, ROWS), BF16),
            jax.ShapeDtypeStruct((len(SLOT_ORDER), 128), jnp.int32),
        ],
        scratch_shapes=[
            pltpu.VMEM(own.shape, BF16),
            pltpu.SMEM(cache_len.shape, jnp.int32),
            pltpu.SemaphoreType.DMA((2,)),
        ],
        compiler_params=pltpu.CompilerParams(vmem_limit_bytes=4 << 20),
        name="scaled_queries",
    )(twin, in_hbm(own), in_hbm(cache_len))


def on_device(queries, new_kv, cache_kv, cache_len, page_owner):
    own = pack(cache_kv, new_kv)
    across = shift(own, flip_z=True)
    opposite = shift(own, 2)
    beside = {(1, False, False): shift(own, 1), (3, False, False): shift(own, 3)}
    twin_queries = shift(after(queries, own)[0], flip_core=True)
    qt, filled = scaled_queries(twin_queries, queries, cache_len)
    held = {(0, False, False): own}
    everything = dict(held)
    state = flash(held, filled, qt, None)

    across, state = after(across, state)
    far = {(1, True, False): shift(across, 1), (3, True, False): shift(across, 3)}
    opposite, state = after(opposite, state)
    far[2, True, False] = shift(opposite, flip_z=True)
    held = {(0, True, False): across, (2, False, False): opposite}
    everything.update(held)
    state = flash(held, filled, qt, state)

    beside, state = after(beside, state)
    everything.update(beside)
    state = flash(beside, filled, qt, state, fresh_rows(everything, len(beside)))

    far, state = after(far, state)
    everything.update(far)
    rows = new_rows(everything)
    twin_rows = shift(rows, flip_core=True)
    twin_part, own_part = flash_last(far, filled, qt, state, fresh_rows(far, len(far)))
    part = merge_pair(own_part, shift(twin_part, flip_core=True))
    parts = lax.all_to_all(part, "seg", 0, 0)
    cache_out = write_pages(cache_len, page_owner, cache_kv, rows, twin_rows)
    return merge(parts), cache_out


def solution(mesh):
    placed = (P("blk", None), P("blk", None), P(("seg", "blk"), None), P(), P())
    return jax.shard_map(
        on_device,
        mesh=mesh,
        in_specs=placed,
        out_specs=(P("blk", "seg"), P(("seg", "blk"), None)),
        check_vma=False,
    )
```

```python
import functools

import jax
import jax.numpy as jnp
from jax import lax
from jax.experimental import pallas as pl
from jax.experimental.pallas import tpu as pltpu
from jax.sharding import PartitionSpec as P


F32 = jnp.float32
BF16 = jnp.bfloat16
HEADS = 16
HD = 128
TOK = 128
ROWS = 2 * HEADS * TOK
PART = HEADS * TOK
SLOTS = 512
LEAST = 256
FILL = 448
PAGE = 8
NSEG = 8
NBLK = 16
SHARE = TOK // NSEG
CHUNK = 2 * HD + 16
ACC = HD + 16
WIDTH = 512
NEG = -1e30
SCALE = 1.4426950408889634 / HD**0.5
VMEM = pl.BlockSpec(memory_space=pltpu.VMEM)
SMEM = pl.BlockSpec(memory_space=pltpu.SMEM)
AXES = ("seg", "blk")
SLOT_ORDER = [(dx, flip_z, False) for flip_z in (False, True) for dx in (0, 1, 3, 2)]


def neighbours(dx=0, flip_z=False, flip_core=False):
    pairs = []
    for here in range(NSEG * NBLK):
        seg, blk = divmod(here, NBLK)
        pairs.append((here, device_at(seg, blk, dx, flip_z, flip_core)))
    return pairs


def device_at(seg, blk, dx, flip_z, flip_core):
    y, z_lo = seg // 2, seg % 2
    z_hi, x, core = blk // 8, (blk // 2) % 4, blk % 2
    if flip_z:
        z_lo, z_hi = 1 - z_lo, 1 - z_hi
    if flip_core:
        core = 1 - core
    x = x ^ dx
    return (y * 2 + z_lo) * NBLK + z_hi * 8 + x * 2 + core


def origin(slot):
    return device_at(lax.axis_index("seg"), lax.axis_index("blk"), *slot)


def queries_kernel(twin_ref, own_hbm, len_hbm, qt_ref, filled_ref, own_ref, len_ref, sems):
    own_copy = pltpu.make_async_copy(own_hbm, own_ref, sems.at[0])
    len_copy = pltpu.make_async_copy(len_hbm, len_ref, sems.at[1])
    own_copy.start()
    len_copy.start()
    for number, q_ref in enumerate((twin_ref, own_ref)):
        if number == 1:
            own_copy.wait()
        for h in range(HEADS):
            scaled = q_ref[:, h * HD : (h + 1) * HD].astype(F32).T * SCALE
            high = scaled.astype(BF16)
            cols = slice(number * PART + h * TOK, number * PART + (h + 1) * TOK)
            qt_ref[0:HD, cols] = high
            qt_ref[HD : 2 * HD, cols] = (scaled - high.astype(F32)).astype(BF16)
    len_copy.wait()
    for j, slot in enumerate(SLOT_ORDER):
        filled_ref[j : j + 1, :] = jnp.full((1, 128), len_ref[origin(slot)], jnp.int32)


def in_hbm(array):
    return pltpu.with_memory_space_constraint(array, pltpu.HBM)


def pack_kernel(cache_ref, new_ref, out_ref, sems):
    copies = [
        pltpu.make_async_copy(cache_ref.at[0:FILL], out_ref.at[0:FILL], sems.at[0]),
        pltpu.make_async_copy(new_ref, out_ref.at[FILL : FILL + TOK], sems.at[1]),
    ]
    for copy in copies:
        copy.start()
    for copy in copies:
        copy.wait()


def pack(cache_kv, new_kv):
    return pl.pallas_call(
        pack_kernel,
        in_specs=[pl.BlockSpec(memory_space=pltpu.HBM)] * 2,
        out_specs=VMEM,
        out_shape=jax.ShapeDtypeStruct((FILL + TOK, 2 * HD), BF16),
        scratch_shapes=[pltpu.SemaphoreType.DMA((2,))],
        compiler_params=pltpu.CompilerParams(vmem_limit_bytes=1 << 20),
        name="pack",
    )(in_hbm(cache_kv), in_hbm(new_kv))


def gather_keys(slots, blocks, fresh_ref, filled_ref, keys, vals, vals_t):
    total = keys.shape[0]
    spans = []
    for j, (slot, block) in enumerate(zip(slots, blocks)):
        filled = filled_ref[SLOT_ORDER.index(slot) : SLOT_ORDER.index(slot) + 1, :]
        start = j * FILL
        ok = lax.broadcasted_iota(jnp.int32, (FILL - LEAST, HD), 0) < filled - LEAST
        head = block[0:LEAST, 0:HD]
        tail = block[LEAST:FILL, 0:HD]
        tail = jnp.where(ok, tail, jnp.broadcast_to(head[0:1], tail.shape))
        value = block[LEAST:FILL, HD : 2 * HD]
        for lanes in (slice(0, HD), slice(HD, 2 * HD)):
            keys[start : start + LEAST, lanes] = head
            keys[start + LEAST : start + FILL, lanes] = tail
        vals[start : start + LEAST, :] = block[0:LEAST, HD : 2 * HD]
        vals[start + LEAST : start + FILL, :] = jnp.where(ok, value, jnp.zeros_like(value))
        spans.append((start, start + LEAST, start + FILL, start + filled))
    old = len(slots) * FILL
    if fresh_ref is not None:
        keys[old:total, 0:HD] = fresh_ref[:, 0:HD]
        keys[old:total, HD : 2 * HD] = fresh_ref[:, 0:HD]
        vals[old:total, :] = fresh_ref[:, HD : 2 * HD]
        spans.append((old, total, total, total))
    elif total > old:
        keys[old:total, :] = jnp.broadcast_to(keys[0:1, :], (total - old, 2 * HD))
        vals[old:total, :] = jnp.zeros((total - old, HD), BF16)
    for c in range(total // 128):
        low, high = c * 128, (c + 1) * 128
        vals_t[0:HD, low:high] = vals[low:high, :].T
        if any(start <= low and high <= sure for start, sure, _, _ in spans):
            vals_t[HD:ACC, low:high] = jnp.ones((ACC - HD, 128), BF16)
            continue
        lane = lax.broadcasted_iota(jnp.int32, (ACC - HD, 128), 1) + low
        one = None
        for start, _, stop, filled in spans:
            if start < high and stop > low:
                inside = (lane >= start) & (lane < filled)
                one = inside if one is None else one | inside
        vals_t[HD:ACC, low:high] = one.astype(F32).astype(BF16)


def flash_columns(
    columns, old, keys, vals_t, qt_ref, state, even_ref, odd_ref, place_ref, emit, given=None, handed=None
):
    total, width = even_ref.shape
    first, last = columns[0] // width, columns[1] // width

    def column_max(s):
        return jnp.max(s.reshape(s.shape[0] // 8, 8, width), axis=0)

    def score(r, scores_ref):
        cols = pl.ds(pl.multiple_of(r * width, width), width)
        s = jnp.dot(keys[...], qt_ref[:, cols], preferred_element_type=F32)
        if place_ref is None:
            scores_ref[...] = s
            return column_max(s)
        blk = lax.axis_index("blk")
        query_blk = jnp.where(r < PART // width, blk + 1 - blk % 2 * 2, blk)
        token = lax.broadcasted_iota(jnp.int32, place_ref.shape, 1)
        seen = place_ref[...] - query_blk * TOK <= token
        fresh = jnp.concatenate(
            [jnp.where(seen, s[old:total, i : i + TOK], NEG) for i in range(0, width, TOK)], axis=1
        )
        scores_ref[0:old] = s[0:old]
        scores_ref[old:total] = fresh
        return jnp.maximum(column_max(s[0:old]), column_max(fresh))

    def weigh(r, tops, scores_ref, next_ref):
        cols = pl.ds(pl.multiple_of(r * width, width), width)
        top = jnp.max(tops, axis=0, keepdims=True)
        if state is not None:
            top = jnp.maximum(top, state[0][0:1, cols])
        if next_ref is not None:
            tops = score(r + 1, next_ref)
        w = jnp.exp2(scores_ref[...] - top).astype(BF16)
        out = jnp.dot(vals_t[...], w, preferred_element_type=F32)
        if state is not None:
            out = out + state[1][:, cols] * jnp.exp2(state[0][0:1, cols] - top)
        emit(r - first, cols, out, top)
        return tops

    def two(i, tops, here_ref, next_ref):
        tops = weigh(first + 2 * i, tops, here_ref, odd_ref)
        return weigh(first + 2 * i + 1, tops, odd_ref, next_ref)

    pairs = (last - first) // 2
    here_ref, tops = (even_ref, score(first, even_ref)) if given is None else (given[0], given[1][...])
    trips = jnp.minimum(lax.axis_index("seg") + pairs - 1, pairs - 1)
    tops = lax.fori_loop(0, trips, lambda i, tops: two(i, tops, here_ref, even_ref), tops)
    tops = two(pairs - 1, tops, even_ref, None if handed is None else handed[0])
    if handed is not None:
        handed[1][...] = tops


def flash_kernel(slots, has_fresh, *refs):
    filled_ref, qt_ref = refs[0], refs[1]
    blocks, refs = refs[2 : 2 + len(slots)], refs[2 + len(slots) :]
    fresh_ref = place_ref = None
    if has_fresh:
        fresh_ref, place_ref, refs = refs[0], refs[1], refs[2:]
    state, (m_ref, acc_ref, keys, vals, vals_t, even_ref, odd_ref) = refs[:-7] or None, refs[-7:]
    gather_keys(slots, blocks, fresh_ref, filled_ref, keys, vals, vals_t)

    def emit(r, cols, out, top):
        acc_ref[:, cols] = out
        m_ref[:, cols] = jnp.broadcast_to(top, m_ref.at[:, cols].shape)

    old = len(slots) * FILL
    flash_columns((0, ROWS), old, keys, vals_t, qt_ref, state, even_ref, odd_ref, place_ref, emit)


def emit_part(part_ref, width):
    def emit(r, cols, out, top):
        total = out[HD : HD + 1]
        normal = (out[0:HD] * (1.0 / total)).astype(BF16)
        stats = top + jnp.log2(total)
        for i in range(0, width // TOK, 2):
            pair = r * (width // TOK // 2) + i // 2
            for j in range(2):
                part_ref[pair, j * HD : (j + 1) * HD, :] = normal[:, (i + j) * TOK : (i + j + 1) * TOK]
            put_sums(part_ref, pair, [stats[:, (i + j) * TOK : (i + j + 1) * TOK] for j in range(2)])

    return emit


def put_sums(part_ref, pair, rows):
    terms = []
    for row in rows:
        high = row.astype(BF16)
        rest = row - high.astype(F32)
        middle = rest.astype(BF16)
        terms += [high, middle, (rest - middle.astype(F32)).astype(BF16)]
    part_ref[pair, 2 * HD : CHUNK, :] = jnp.concatenate(terms + [terms[0]] * 10, axis=0)


def get_sums(part_ref, pair, head):
    three = [part_ref[pair, 2 * HD + head * 3 + i : 2 * HD + head * 3 + i + 1, :].astype(F32) for i in range(3)]
    return three[0] + three[1] + three[2]


def twin_kernel(slots, *refs):
    filled_ref, qt_ref = refs[0], refs[1]
    blocks, refs = refs[2 : 2 + len(slots)], refs[2 + len(slots) :]
    fresh_ref, place_ref, m_in, acc_in, part_ref, keys, vals_t, scores_ref, tops_ref, vals, even_ref, odd_ref = refs
    gather_keys(slots, blocks, fresh_ref, filled_ref, keys, vals, vals_t)
    emit = emit_part(part_ref, even_ref.shape[1])
    flash_columns(
        (0, PART),
        len(slots) * FILL,
        keys,
        vals_t,
        qt_ref,
        (m_in, acc_in),
        even_ref,
        odd_ref,
        place_ref,
        emit,
        handed=(scores_ref, tops_ref),
    )


def own_kernel(old, qt_ref, keys, vals_t, scores_ref, tops_ref, place_ref, m_in, acc_in, part_ref, even_ref, odd_ref):
    emit = emit_part(part_ref, even_ref.shape[1])
    flash_columns(
        (PART, ROWS),
        old,
        keys,
        vals_t,
        qt_ref,
        (m_in, acc_in),
        even_ref,
        odd_ref,
        place_ref,
        emit,
        given=(scores_ref, tops_ref),
    )


def flash_call(kernel, operands, out_shape, scratch, total, rows, name, width=WIDTH):
    return pl.pallas_call(
        kernel,
        in_specs=[VMEM] * len(operands),
        out_specs=jax.tree.map(lambda _: VMEM, out_shape),
        out_shape=out_shape,
        scratch_shapes=scratch + [pltpu.VMEM((total, width), F32)] * 2,
        compiler_params=pltpu.CompilerParams(vmem_limit_bytes=24 << 20),
        cost_estimate=pl.CostEstimate(
            flops=4 * total * rows * 256, bytes_accessed=1 << 20, transcendentals=total * rows
        ),
        name=name,
    )(*operands)


def flash(held, filled, qt, state, fresh=()):
    total = -(-len(held) * FILL // 128) * 128
    if fresh:
        total = len(held) * FILL + fresh[0].shape[0]
    return flash_call(
        functools.partial(flash_kernel, list(held), bool(fresh)),
        [filled, qt, *held.values(), *fresh, *(state or ())],
        [jax.ShapeDtypeStruct((8, ROWS), F32), jax.ShapeDtypeStruct((ACC, ROWS), F32)],
        [
            pltpu.VMEM((total, 2 * HD), BF16),
            pltpu.VMEM((total, HD), BF16),
            pltpu.VMEM((ACC, total), BF16),
        ],
        total,
        ROWS,
        f"flash_{len(held)}",
        WIDTH if state else 2 * WIDTH,
    )


def flash_last(held, filled, qt, state, fresh):
    old = len(held) * FILL
    total = old + fresh[0].shape[0]
    part = jax.ShapeDtypeStruct((NSEG, CHUNK, TOK), BF16)
    twin_part, *handed = flash_call(
        functools.partial(twin_kernel, list(held)),
        [filled, qt, *held.values(), *fresh, *state],
        [
            part,
            jax.ShapeDtypeStruct((total, 2 * HD), BF16),
            jax.ShapeDtypeStruct((ACC, total), BF16),
            jax.ShapeDtypeStruct((total, WIDTH), F32),
            jax.ShapeDtypeStruct((8, WIDTH), F32),
        ],
        [pltpu.VMEM((total, HD), BF16)],
        total,
        PART,
        "flash_twin",
    )
    own_part = flash_call(
        functools.partial(own_kernel, old), [qt, *handed, fresh[1], *state], part, [], total, PART, "flash_own"
    )
    return twin_part, own_part


def fresh_kernel(slots, *refs):
    blocks, share_ref, place_ref = refs[: len(slots)], refs[-2], refs[-1]
    first = lax.axis_index("seg") * SHARE
    for j, (slot, block) in enumerate(zip(slots, blocks)):
        rows = slice(j * SHARE, (j + 1) * SHARE)
        share_ref[rows, :] = block[pl.ds(pl.multiple_of(FILL + first, SHARE), SHARE), :]
        place = origin(slot) % NBLK * TOK + first
        place_ref[rows, :] = lax.broadcasted_iota(jnp.int32, (SHARE, TOK), 0) + place
    rest = share_ref.shape[0] - len(slots) * SHARE
    share_ref[len(slots) * SHARE :, :] = jnp.zeros((rest, 2 * HD), BF16)
    place_ref[len(slots) * SHARE :, :] = jnp.full((rest, TOK), NBLK * TOK, jnp.int32)


def fresh_rows(held, after_slots):
    old = after_slots * FILL
    size = -(-(old + len(held) * SHARE) // 128) * 128 - old
    return pl.pallas_call(
        functools.partial(fresh_kernel, list(held)),
        in_specs=[VMEM] * len(held),
        out_specs=[VMEM, VMEM],
        out_shape=[jax.ShapeDtypeStruct((size, 2 * HD), BF16), jax.ShapeDtypeStruct((size, TOK), jnp.int32)],
        compiler_params=pltpu.CompilerParams(vmem_limit_bytes=1 << 20),
        name="fresh_rows",
    )(*held.values())


def rows_kernel(slots, *refs):
    for slot, block in zip(slots, refs):
        pair = origin(slot) % NBLK // 2
        refs[-1][pl.ds(pl.multiple_of(pair * TOK, TOK), TOK), :] = block[FILL : FILL + TOK, :]


def new_rows(held):
    return pl.pallas_call(
        functools.partial(rows_kernel, list(held)),
        in_specs=[VMEM] * len(held),
        out_specs=VMEM,
        out_shape=jax.ShapeDtypeStruct((NBLK // 2 * TOK, 2 * HD), BF16),
        compiler_params=pltpu.CompilerParams(vmem_limit_bytes=1 << 20),
        name="new_rows",
    )(*held.values())


def pages_kernel(len_ref, owner_ref, cache_ref, own_ref, twin_ref, out_ref):
    blk = lax.axis_index("blk")
    device = lax.axis_index("seg") * NBLK + blk
    filled = len_ref[device]
    pages = owner_ref.shape[1]
    owned = jnp.broadcast_to((owner_ref[...] == device).astype(F32), (16, pages)).astype(BF16)
    before = (
        lax.broadcasted_iota(jnp.int32, (pages, pages), 0) < lax.broadcasted_iota(jnp.int32, (pages, pages), 1)
    ).astype(BF16)
    rank = jnp.dot(owned, before, preferred_element_type=F32)
    rank = jnp.where(owned > 0, rank, -1.0).astype(BF16)
    half = SLOTS // 2
    written, count = None, None
    for rows_ref, core in ((own_ref, blk % 2), (twin_ref, 1 - blk % 2)):
        rows = rows_ref.shape[0]
        row = lax.broadcasted_iota(jnp.int32, (pages, rows), 1)
        page = (row // TOK * 2 + core) * (TOK // PAGE) + row % TOK // PAGE
        spread = (page == lax.broadcasted_iota(jnp.int32, (pages, rows), 0)).astype(BF16)
        row_rank = jnp.dot(rank, spread, preferred_element_type=F32)[0:1].astype(jnp.int32)
        target = filled + row_rank * PAGE + lax.broadcasted_iota(jnp.int32, (1, rows), 1) % PAGE
        target = jnp.where(row_rank >= 0, target, -1)
        pick = (lax.broadcasted_iota(jnp.int32, (half, rows), 0) + half == target).astype(BF16)
        term = jnp.dot(pick, rows_ref[...], preferred_element_type=F32)
        written = term if written is None else written + term
        most = jnp.max(row_rank) + 1
        count = most if count is None else jnp.maximum(count, most)
    slot_id = lax.broadcasted_iota(jnp.int32, (half, 2 * HD), 0) + half
    is_new = (slot_id >= filled) & (slot_id < filled + count * PAGE)
    out_ref[0:half, :] = cache_ref[0:half, :]
    out_ref[half:SLOTS, :] = jnp.where(is_new, written.astype(BF16), cache_ref[half:SLOTS, :])


def write_pages(cache_len, page_owner, cache_kv, own_rows, twin_rows):
    return pl.pallas_call(
        pages_kernel,
        in_specs=[SMEM] + [VMEM] * 4,
        out_specs=VMEM,
        out_shape=jax.ShapeDtypeStruct(cache_kv.shape, BF16),
        compiler_params=pltpu.CompilerParams(vmem_limit_bytes=16 << 20),
        cost_estimate=pl.CostEstimate(flops=10**9, bytes_accessed=2 << 20, transcendentals=0),
        name="write_pages",
    )(cache_len, page_owner.reshape(1, -1), cache_kv, own_rows, twin_rows)


def pair_kernel(own_ref, twin_ref, out_ref, held, sems):
    copies = []
    for s in range(NSEG):
        sums = []
        for head in range(2):
            rows = slice(head * HD, (head + 1) * HD)
            own, twin = get_sums(own_ref, s, head), get_sums(twin_ref, s, head)
            top = jnp.maximum(own, twin)
            own_w, twin_w = jnp.exp2(own - top), jnp.exp2(twin - top)
            total = own_w + twin_w
            scale = 1.0 / total
            out = own_ref[s, rows, :].astype(F32) * (own_w * scale) + twin_ref[s, rows, :].astype(F32) * (twin_w * scale)
            held[s, rows, :] = out.astype(BF16)
            sums.append(top + jnp.log2(total))
        put_sums(held, s, sums)
        copies.append(pltpu.make_async_copy(held.at[s], out_ref.at[s], sems.at[s]))
        copies[-1].start()
    for copy in copies:
        copy.wait()


def merge_pair(own, twin):
    return pl.pallas_call(
        pair_kernel,
        in_specs=[VMEM, VMEM],
        out_specs=pl.BlockSpec(memory_space=pltpu.HBM),
        out_shape=jax.ShapeDtypeStruct(own.shape, BF16),
        scratch_shapes=[pltpu.VMEM(own.shape, BF16), pltpu.SemaphoreType.DMA((NSEG,))],
        compiler_params=pltpu.CompilerParams(vmem_limit_bytes=4 << 20),
        name="merge_pair",
    )(own, twin)


def merge_kernel(parts_ref, out_ref):
    for head in range(2):
        logs = [get_sums(parts_ref, s, head) for s in range(NSEG)]
        top = functools.reduce(jnp.maximum, logs)
        weights = [jnp.exp2(v - top) for v in logs]
        scale = 1.0 / functools.reduce(jnp.add, weights)
        out = None
        for s in range(NSEG):
            term = parts_ref[s, head * HD : (head + 1) * HD, :].astype(F32) * (weights[s] * scale)
            out = term if out is None else out + term
        out_ref[:, head * HD : (head + 1) * HD] = out.T.astype(BF16)


def merge(parts):
    return pl.pallas_call(
        merge_kernel,
        in_specs=[VMEM],
        out_specs=VMEM,
        out_shape=jax.ShapeDtypeStruct((TOK, 2 * HD), BF16),
        compiler_params=pltpu.CompilerParams(vmem_limit_bytes=4 << 20),
        name="merge",
    )(parts)


def shift(block, dx=0, flip_z=False, flip_core=False):
    return lax.ppermute(block, AXES, neighbours(dx, flip_z, flip_core))


def after(values, other):
    return lax.optimization_barrier((values, other))


def scaled_queries(twin, own, cache_len):
    return pl.pallas_call(
        queries_kernel,
        in_specs=[VMEM] + [pl.BlockSpec(memory_space=pltpu.HBM)] * 2,
        out_specs=[VMEM, VMEM],
        out_shape=[
            jax.ShapeDtypeStruct((2 * HD, ROWS), BF16),
            jax.ShapeDtypeStruct((len(SLOT_ORDER), 128), jnp.int32),
        ],
        scratch_shapes=[
            pltpu.VMEM(own.shape, BF16),
            pltpu.SMEM(cache_len.shape, jnp.int32),
            pltpu.SemaphoreType.DMA((2,)),
        ],
        compiler_params=pltpu.CompilerParams(vmem_limit_bytes=4 << 20),
        name="scaled_queries",
    )(twin, in_hbm(own), in_hbm(cache_len))


def on_device(queries, new_kv, cache_kv, cache_len, page_owner):
    own = pack(cache_kv, new_kv)
    across = shift(own, flip_z=True)
    opposite = shift(own, 2)
    beside = {(1, False, False): shift(own, 1), (3, False, False): shift(own, 3)}
    twin_queries = shift(after(queries, own)[0], flip_core=True)
    qt, filled = scaled_queries(twin_queries, queries, cache_len)
    held = {(0, False, False): own}
    everything = dict(held)
    state = flash(held, filled, qt, None)

    across, state = after(across, state)
    far = {(1, True, False): shift(across, 1), (3, True, False): shift(across, 3)}
    opposite, state = after(opposite, state)
    far[2, True, False] = shift(opposite, flip_z=True)
    held = {(0, True, False): across, (2, False, False): opposite}
    everything.update(held)
    state = flash(held, filled, qt, state)

    beside, state = after(beside, state)
    everything.update(beside)
    state = flash(beside, filled, qt, state, fresh_rows(everything, len(beside)))

    far, state = after(far, state)
    everything.update(far)
    rows = new_rows(everything)
    twin_rows = shift(rows, flip_core=True)
    twin_part, own_part = flash_last(far, filled, qt, state, fresh_rows(far, len(far)))
    part = merge_pair(own_part, shift(twin_part, flip_core=True))
    parts = lax.all_to_all(part, "seg", 0, 0)
    cache_out = write_pages(cache_len, page_owner, cache_kv, rows, twin_rows)
    return merge(parts), cache_out


def solution(mesh):
    placed = (P("blk", None), P("blk", None), P(("seg", "blk"), None), P(), P())
    return jax.shard_map(
        on_device,
        mesh=mesh,
        in_specs=placed,
        out_specs=(P("blk", "seg"), P(("seg", "blk"), None)),
        check_vma=False,
    )
```

```python
import functools

import jax
import jax.numpy as jnp
from jax import lax
from jax.experimental import pallas as pl
from jax.experimental.pallas import tpu as pltpu
from jax.sharding import PartitionSpec as P


F32 = jnp.float32
BF16 = jnp.bfloat16
HEADS = 16
HD = 128
TOK = 128
ROWS = 2 * HEADS * TOK
PART = HEADS * TOK
SLOTS = 512
LEAST = 256
FILL = 448
PAGE = 8
NSEG = 8
NBLK = 16
SHARE = TOK // NSEG
CHUNK = 2 * HD + 16
ACC = HD + 16
WIDTH = 512
NEG = -1e30
SCALE = 1.4426950408889634 / HD**0.5
VMEM = pl.BlockSpec(memory_space=pltpu.VMEM)
SMEM = pl.BlockSpec(memory_space=pltpu.SMEM)
AXES = ("seg", "blk")
SLOT_ORDER = [(dx, flip_z, False) for flip_z in (False, True) for dx in (0, 1, 3, 2)]


def neighbours(dx=0, flip_z=False, flip_core=False):
    pairs = []
    for here in range(NSEG * NBLK):
        seg, blk = divmod(here, NBLK)
        pairs.append((here, device_at(seg, blk, dx, flip_z, flip_core)))
    return pairs


def device_at(seg, blk, dx, flip_z, flip_core):
    y, z_lo = seg // 2, seg % 2
    z_hi, x, core = blk // 8, (blk // 2) % 4, blk % 2
    if flip_z:
        z_lo, z_hi = 1 - z_lo, 1 - z_hi
    if flip_core:
        core = 1 - core
    x = x ^ dx
    return (y * 2 + z_lo) * NBLK + z_hi * 8 + x * 2 + core


def origin(slot):
    return device_at(lax.axis_index("seg"), lax.axis_index("blk"), *slot)


def queries_kernel(twin_ref, own_hbm, len_hbm, qt_ref, filled_ref, own_ref, len_ref, sems):
    own_copy = pltpu.make_async_copy(own_hbm, own_ref, sems.at[0])
    len_copy = pltpu.make_async_copy(len_hbm, len_ref, sems.at[1])
    own_copy.start()
    len_copy.start()
    for number, q_ref in enumerate((twin_ref, own_ref)):
        if number == 1:
            own_copy.wait()
        for h in range(HEADS):
            scaled = q_ref[:, h * HD : (h + 1) * HD].astype(F32).T * SCALE
            high = scaled.astype(BF16)
            cols = slice(number * PART + h * TOK, number * PART + (h + 1) * TOK)
            qt_ref[0:HD, cols] = high
            qt_ref[HD : 2 * HD, cols] = (scaled - high.astype(F32)).astype(BF16)
    len_copy.wait()
    for j, slot in enumerate(SLOT_ORDER):
        here = lax.broadcasted_iota(jnp.int32, len_ref.shape, 1) == origin(slot)
        filled = jnp.sum(jnp.where(here, len_ref[...], 0).astype(F32), axis=1, keepdims=True)
        filled_ref[j : j + 1, :] = jnp.broadcast_to(filled.astype(jnp.int32), (1, 128))


def in_hbm(array):
    return pltpu.with_memory_space_constraint(array, pltpu.HBM)


def pack_kernel(cache_ref, new_ref, out_ref, sems):
    copies = [
        pltpu.make_async_copy(cache_ref.at[0:FILL], out_ref.at[0:FILL], sems.at[0]),
        pltpu.make_async_copy(new_ref, out_ref.at[FILL : FILL + TOK], sems.at[1]),
    ]
    for copy in copies:
        copy.start()
    for copy in copies:
        copy.wait()


def pack(cache_kv, new_kv):
    return pl.pallas_call(
        pack_kernel,
        in_specs=[pl.BlockSpec(memory_space=pltpu.HBM)] * 2,
        out_specs=VMEM,
        out_shape=jax.ShapeDtypeStruct((FILL + TOK, 2 * HD), BF16),
        scratch_shapes=[pltpu.SemaphoreType.DMA((2,))],
        compiler_params=pltpu.CompilerParams(vmem_limit_bytes=1 << 20),
        name="pack",
    )(in_hbm(cache_kv), in_hbm(new_kv))


def gather_keys(slots, blocks, fresh_ref, filled_ref, keys, vals, vals_t):
    total = keys.shape[0]
    spans = []
    for j, (slot, block) in enumerate(zip(slots, blocks)):
        filled = filled_ref[SLOT_ORDER.index(slot) : SLOT_ORDER.index(slot) + 1, :]
        start = j * FILL
        ok = lax.broadcasted_iota(jnp.int32, (FILL - LEAST, HD), 0) < filled - LEAST
        head = block[0:LEAST, 0:HD]
        tail = block[LEAST:FILL, 0:HD]
        tail = jnp.where(ok, tail, jnp.broadcast_to(head[0:1], tail.shape))
        value = block[LEAST:FILL, HD : 2 * HD]
        for lanes in (slice(0, HD), slice(HD, 2 * HD)):
            keys[start : start + LEAST, lanes] = head
            keys[start + LEAST : start + FILL, lanes] = tail
        vals[start : start + LEAST, :] = block[0:LEAST, HD : 2 * HD]
        vals[start + LEAST : start + FILL, :] = jnp.where(ok, value, jnp.zeros_like(value))
        spans.append((start, start + LEAST, start + FILL, start + filled))
    old = len(slots) * FILL
    if fresh_ref is not None:
        keys[old:total, 0:HD] = fresh_ref[:, 0:HD]
        keys[old:total, HD : 2 * HD] = fresh_ref[:, 0:HD]
        vals[old:total, :] = fresh_ref[:, HD : 2 * HD]
        spans.append((old, total, total, total))
    elif total > old:
        keys[old:total, :] = jnp.broadcast_to(keys[0:1, :], (total - old, 2 * HD))
        vals[old:total, :] = jnp.zeros((total - old, HD), BF16)
    for c in range(total // 128):
        low, high = c * 128, (c + 1) * 128
        vals_t[0:HD, low:high] = vals[low:high, :].T
        if any(start <= low and high <= sure for start, sure, _, _ in spans):
            vals_t[HD:ACC, low:high] = jnp.ones((ACC - HD, 128), BF16)
            continue
        lane = lax.broadcasted_iota(jnp.int32, (ACC - HD, 128), 1) + low
        one = None
        for start, _, stop, filled in spans:
            if start < high and stop > low:
                inside = (lane >= start) & (lane < filled)
                one = inside if one is None else one | inside
        vals_t[HD:ACC, low:high] = one.astype(F32).astype(BF16)


def flash_columns(
    columns, old, keys, vals_t, qt_ref, state, even_ref, odd_ref, place_ref, emit, given=None, handed=None
):
    total, width = even_ref.shape
    first, last = columns[0] // width, columns[1] // width

    def column_max(s):
        return jnp.max(s.reshape(s.shape[0] // 8, 8, width), axis=0)

    def score(r, scores_ref):
        cols = pl.ds(pl.multiple_of(r * width, width), width)
        s = jnp.dot(keys[...], qt_ref[:, cols], preferred_element_type=F32)
        if place_ref is None:
            scores_ref[...] = s
            return column_max(s)
        blk = lax.axis_index("blk")
        query_blk = jnp.where(r < PART // width, blk + 1 - blk % 2 * 2, blk)
        token = lax.broadcasted_iota(jnp.int32, place_ref.shape, 1)
        seen = place_ref[...] - query_blk * TOK <= token
        fresh = jnp.concatenate(
            [jnp.where(seen, s[old:total, i : i + TOK], NEG) for i in range(0, width, TOK)], axis=1
        )
        scores_ref[0:old] = s[0:old]
        scores_ref[old:total] = fresh
        return jnp.maximum(column_max(s[0:old]), column_max(fresh))

    def weigh(r, tops, scores_ref, next_ref):
        cols = pl.ds(pl.multiple_of(r * width, width), width)
        top = jnp.max(tops, axis=0, keepdims=True)
        if state is not None:
            top = jnp.maximum(top, state[0][0:1, cols])
        if next_ref is not None:
            tops = score(r + 1, next_ref)
        w = jnp.exp2(scores_ref[...] - top).astype(BF16)
        out = jnp.dot(vals_t[...], w, preferred_element_type=F32)
        if state is not None:
            out = out + state[1][:, cols] * jnp.exp2(state[0][0:1, cols] - top)
        emit(r - first, cols, out, top)
        return tops

    def two(i, tops, here_ref, next_ref):
        tops = weigh(first + 2 * i, tops, here_ref, odd_ref)
        return weigh(first + 2 * i + 1, tops, odd_ref, next_ref)

    pairs = (last - first) // 2
    here_ref, tops = (even_ref, score(first, even_ref)) if given is None else (given[0], given[1][...])
    trips = jnp.minimum(lax.axis_index("seg") + pairs - 1, pairs - 1)
    tops = lax.fori_loop(0, trips, lambda i, tops: two(i, tops, here_ref, even_ref), tops)
    tops = two(pairs - 1, tops, even_ref, None if handed is None else handed[0])
    if handed is not None:
        handed[1][...] = tops


def flash_kernel(slots, has_fresh, *refs):
    filled_ref, qt_ref = refs[0], refs[1]
    blocks, refs = refs[2 : 2 + len(slots)], refs[2 + len(slots) :]
    fresh_ref = place_ref = None
    if has_fresh:
        fresh_ref, place_ref, refs = refs[0], refs[1], refs[2:]
    state, (m_ref, acc_ref, keys, vals, vals_t, even_ref, odd_ref) = refs[:-7] or None, refs[-7:]
    gather_keys(slots, blocks, fresh_ref, filled_ref, keys, vals, vals_t)

    def emit(r, cols, out, top):
        acc_ref[:, cols] = out
        m_ref[:, cols] = jnp.broadcast_to(top, m_ref.at[:, cols].shape)

    old = len(slots) * FILL
    flash_columns((0, ROWS), old, keys, vals_t, qt_ref, state, even_ref, odd_ref, place_ref, emit)


def emit_part(part_ref, width):
    def emit(r, cols, out, top):
        total = out[HD : HD + 1]
        normal = (out[0:HD] * (1.0 / total)).astype(BF16)
        stats = top + jnp.log2(total)
        for i in range(0, width // TOK, 2):
            pair = r * (width // TOK // 2) + i // 2
            for j in range(2):
                part_ref[pair, j * HD : (j + 1) * HD, :] = normal[:, (i + j) * TOK : (i + j + 1) * TOK]
            put_sums(part_ref, pair, [stats[:, (i + j) * TOK : (i + j + 1) * TOK] for j in range(2)])

    return emit


def put_sums(part_ref, pair, rows):
    terms = []
    for row in rows:
        high = row.astype(BF16)
        rest = row - high.astype(F32)
        middle = rest.astype(BF16)
        terms += [high, middle, (rest - middle.astype(F32)).astype(BF16)]
    part_ref[pair, 2 * HD : CHUNK, :] = jnp.concatenate(terms + [terms[0]] * 10, axis=0)


def get_sums(part_ref, pair, head):
    three = [part_ref[pair, 2 * HD + head * 3 + i : 2 * HD + head * 3 + i + 1, :].astype(F32) for i in range(3)]
    return three[0] + three[1] + three[2]


def twin_kernel(slots, *refs):
    filled_ref, qt_ref = refs[0], refs[1]
    blocks, refs = refs[2 : 2 + len(slots)], refs[2 + len(slots) :]
    fresh_ref, place_ref, m_in, acc_in, part_ref, keys, vals_t, scores_ref, tops_ref, vals, even_ref, odd_ref = refs
    gather_keys(slots, blocks, fresh_ref, filled_ref, keys, vals, vals_t)
    emit = emit_part(part_ref, even_ref.shape[1])
    flash_columns(
        (0, PART),
        len(slots) * FILL,
        keys,
        vals_t,
        qt_ref,
        (m_in, acc_in),
        even_ref,
        odd_ref,
        place_ref,
        emit,
        handed=(scores_ref, tops_ref),
    )


def own_kernel(old, qt_ref, keys, vals_t, scores_ref, tops_ref, place_ref, m_in, acc_in, part_ref, even_ref, odd_ref):
    emit = emit_part(part_ref, even_ref.shape[1])
    flash_columns(
        (PART, ROWS),
        old,
        keys,
        vals_t,
        qt_ref,
        (m_in, acc_in),
        even_ref,
        odd_ref,
        place_ref,
        emit,
        given=(scores_ref, tops_ref),
    )


def flash_call(kernel, operands, out_shape, scratch, total, rows, name, width=WIDTH):
    return pl.pallas_call(
        kernel,
        in_specs=[VMEM] * len(operands),
        out_specs=jax.tree.map(lambda _: VMEM, out_shape),
        out_shape=out_shape,
        scratch_shapes=scratch + [pltpu.VMEM((total, width), F32)] * 2,
        compiler_params=pltpu.CompilerParams(vmem_limit_bytes=24 << 20),
        cost_estimate=pl.CostEstimate(
            flops=4 * total * rows * 256, bytes_accessed=1 << 20, transcendentals=total * rows
        ),
        name=name,
    )(*operands)


def flash(held, filled, qt, state, fresh=()):
    total = -(-len(held) * FILL // 128) * 128
    if fresh:
        total = len(held) * FILL + fresh[0].shape[0]
    return flash_call(
        functools.partial(flash_kernel, list(held), bool(fresh)),
        [filled, qt, *held.values(), *fresh, *(state or ())],
        [jax.ShapeDtypeStruct((8, ROWS), F32), jax.ShapeDtypeStruct((ACC, ROWS), F32)],
        [
            pltpu.VMEM((total, 2 * HD), BF16),
            pltpu.VMEM((total, HD), BF16),
            pltpu.VMEM((ACC, total), BF16),
        ],
        total,
        ROWS,
        f"flash_{len(held)}",
        WIDTH if state else 2 * WIDTH,
    )


def flash_last(held, filled, qt, state, fresh):
    old = len(held) * FILL
    total = old + fresh[0].shape[0]
    part = jax.ShapeDtypeStruct((NSEG, CHUNK, TOK), BF16)
    twin_part, *handed = flash_call(
        functools.partial(twin_kernel, list(held)),
        [filled, qt, *held.values(), *fresh, *state],
        [
            part,
            jax.ShapeDtypeStruct((total, 2 * HD), BF16),
            jax.ShapeDtypeStruct((ACC, total), BF16),
            jax.ShapeDtypeStruct((total, WIDTH), F32),
            jax.ShapeDtypeStruct((8, WIDTH), F32),
        ],
        [pltpu.VMEM((total, HD), BF16)],
        total,
        PART,
        "flash_twin",
    )
    own_part = flash_call(
        functools.partial(own_kernel, old), [qt, *handed, fresh[1], *state], part, [], total, PART, "flash_own"
    )
    return twin_part, own_part


def fresh_kernel(slots, *refs):
    blocks, share_ref, place_ref = refs[: len(slots)], refs[-2], refs[-1]
    first = lax.axis_index("seg") * SHARE
    for j, (slot, block) in enumerate(zip(slots, blocks)):
        rows = slice(j * SHARE, (j + 1) * SHARE)
        share_ref[rows, :] = block[pl.ds(pl.multiple_of(FILL + first, SHARE), SHARE), :]
        place = origin(slot) % NBLK * TOK + first
        place_ref[rows, :] = lax.broadcasted_iota(jnp.int32, (SHARE, TOK), 0) + place
    rest = share_ref.shape[0] - len(slots) * SHARE
    share_ref[len(slots) * SHARE :, :] = jnp.zeros((rest, 2 * HD), BF16)
    place_ref[len(slots) * SHARE :, :] = jnp.full((rest, TOK), NBLK * TOK, jnp.int32)


def fresh_rows(held, after_slots):
    old = after_slots * FILL
    size = -(-(old + len(held) * SHARE) // 128) * 128 - old
    return pl.pallas_call(
        functools.partial(fresh_kernel, list(held)),
        in_specs=[VMEM] * len(held),
        out_specs=[VMEM, VMEM],
        out_shape=[jax.ShapeDtypeStruct((size, 2 * HD), BF16), jax.ShapeDtypeStruct((size, TOK), jnp.int32)],
        compiler_params=pltpu.CompilerParams(vmem_limit_bytes=1 << 20),
        name="fresh_rows",
    )(*held.values())


def rows_kernel(slots, *refs):
    for slot, block in zip(slots, refs):
        pair = origin(slot) % NBLK // 2
        refs[-1][pl.ds(pl.multiple_of(pair * TOK, TOK), TOK), :] = block[FILL : FILL + TOK, :]


def new_rows(held):
    return pl.pallas_call(
        functools.partial(rows_kernel, list(held)),
        in_specs=[VMEM] * len(held),
        out_specs=VMEM,
        out_shape=jax.ShapeDtypeStruct((NBLK // 2 * TOK, 2 * HD), BF16),
        compiler_params=pltpu.CompilerParams(vmem_limit_bytes=1 << 20),
        name="new_rows",
    )(*held.values())


def pages_kernel(len_ref, owner_ref, cache_ref, own_ref, twin_ref, out_ref):
    blk = lax.axis_index("blk")
    device = lax.axis_index("seg") * NBLK + blk
    filled = len_ref[device]
    pages = owner_ref.shape[1]
    owned = jnp.broadcast_to((owner_ref[...] == device).astype(F32), (16, pages)).astype(BF16)
    before = (
        lax.broadcasted_iota(jnp.int32, (pages, pages), 0) < lax.broadcasted_iota(jnp.int32, (pages, pages), 1)
    ).astype(BF16)
    rank = jnp.dot(owned, before, preferred_element_type=F32)
    rank = jnp.where(owned > 0, rank, -1.0).astype(BF16)
    half = SLOTS // 2
    written, count = None, None
    for rows_ref, core in ((own_ref, blk % 2), (twin_ref, 1 - blk % 2)):
        rows = rows_ref.shape[0]
        row = lax.broadcasted_iota(jnp.int32, (pages, rows), 1)
        page = (row // TOK * 2 + core) * (TOK // PAGE) + row % TOK // PAGE
        spread = (page == lax.broadcasted_iota(jnp.int32, (pages, rows), 0)).astype(BF16)
        row_rank = jnp.dot(rank, spread, preferred_element_type=F32)[0:1].astype(jnp.int32)
        target = filled + row_rank * PAGE + lax.broadcasted_iota(jnp.int32, (1, rows), 1) % PAGE
        target = jnp.where(row_rank >= 0, target, -1)
        pick = (lax.broadcasted_iota(jnp.int32, (half, rows), 0) + half == target).astype(BF16)
        term = jnp.dot(pick, rows_ref[...], preferred_element_type=F32)
        written = term if written is None else written + term
        most = jnp.max(row_rank) + 1
        count = most if count is None else jnp.maximum(count, most)
    slot_id = lax.broadcasted_iota(jnp.int32, (half, 2 * HD), 0) + half
    is_new = (slot_id >= filled) & (slot_id < filled + count * PAGE)
    out_ref[0:half, :] = cache_ref[0:half, :]
    out_ref[half:SLOTS, :] = jnp.where(is_new, written.astype(BF16), cache_ref[half:SLOTS, :])


def write_pages(cache_len, page_owner, cache_kv, own_rows, twin_rows):
    return pl.pallas_call(
        pages_kernel,
        in_specs=[SMEM] + [VMEM] * 4,
        out_specs=VMEM,
        out_shape=jax.ShapeDtypeStruct(cache_kv.shape, BF16),
        compiler_params=pltpu.CompilerParams(vmem_limit_bytes=16 << 20),
        cost_estimate=pl.CostEstimate(flops=10**9, bytes_accessed=2 << 20, transcendentals=0),
        name="write_pages",
    )(cache_len, page_owner.reshape(1, -1), cache_kv, own_rows, twin_rows)


def pair_kernel(own_ref, twin_ref, out_ref, held, sems):
    copies = []
    for s in range(NSEG):
        sums = []
        for head in range(2):
            rows = slice(head * HD, (head + 1) * HD)
            own, twin = get_sums(own_ref, s, head), get_sums(twin_ref, s, head)
            top = jnp.maximum(own, twin)
            own_w, twin_w = jnp.exp2(own - top), jnp.exp2(twin - top)
            total = own_w + twin_w
            scale = 1.0 / total
            out = own_ref[s, rows, :].astype(F32) * (own_w * scale) + twin_ref[s, rows, :].astype(F32) * (twin_w * scale)
            held[s, rows, :] = out.astype(BF16)
            sums.append(top + jnp.log2(total))
        put_sums(held, s, sums)
        copies.append(pltpu.make_async_copy(held.at[s], out_ref.at[s], sems.at[s]))
        copies[-1].start()
    for copy in copies:
        copy.wait()


def merge_pair(own, twin):
    return pl.pallas_call(
        pair_kernel,
        in_specs=[VMEM, VMEM],
        out_specs=pl.BlockSpec(memory_space=pltpu.HBM),
        out_shape=jax.ShapeDtypeStruct(own.shape, BF16),
        scratch_shapes=[pltpu.VMEM(own.shape, BF16), pltpu.SemaphoreType.DMA((NSEG,))],
        compiler_params=pltpu.CompilerParams(vmem_limit_bytes=4 << 20),
        name="merge_pair",
    )(own, twin)


def merge_kernel(parts_ref, out_ref):
    for head in range(2):
        logs = [get_sums(parts_ref, s, head) for s in range(NSEG)]
        top = functools.reduce(jnp.maximum, logs)
        weights = [jnp.exp2(v - top) for v in logs]
        scale = 1.0 / functools.reduce(jnp.add, weights)
        out = None
        for s in range(NSEG):
            term = parts_ref[s, head * HD : (head + 1) * HD, :].astype(F32) * (weights[s] * scale)
            out = term if out is None else out + term
        out_ref[:, head * HD : (head + 1) * HD] = out.T.astype(BF16)


def merge(parts):
    return pl.pallas_call(
        merge_kernel,
        in_specs=[VMEM],
        out_specs=VMEM,
        out_shape=jax.ShapeDtypeStruct((TOK, 2 * HD), BF16),
        compiler_params=pltpu.CompilerParams(vmem_limit_bytes=4 << 20),
        name="merge",
    )(parts)


def shift(block, dx=0, flip_z=False, flip_core=False):
    return lax.ppermute(block, AXES, neighbours(dx, flip_z, flip_core))


def after(values, other):
    return lax.optimization_barrier((values, other))


def scaled_queries(twin, own, cache_len):
    return pl.pallas_call(
        queries_kernel,
        in_specs=[VMEM] + [pl.BlockSpec(memory_space=pltpu.HBM)] * 2,
        out_specs=[VMEM, VMEM],
        out_shape=[
            jax.ShapeDtypeStruct((2 * HD, ROWS), BF16),
            jax.ShapeDtypeStruct((len(SLOT_ORDER), 128), jnp.int32),
        ],
        scratch_shapes=[
            pltpu.VMEM(own.shape, BF16),
            pltpu.VMEM((1, cache_len.shape[0]), jnp.int32),
            pltpu.SemaphoreType.DMA((2,)),
        ],
        compiler_params=pltpu.CompilerParams(vmem_limit_bytes=4 << 20),
        name="scaled_queries",
    )(twin, in_hbm(own), in_hbm(cache_len.reshape(1, -1)))


def on_device(queries, new_kv, cache_kv, cache_len, page_owner):
    own = pack(cache_kv, new_kv)
    across = shift(own, flip_z=True)
    opposite = shift(own, 2)
    beside = {(1, False, False): shift(own, 1), (3, False, False): shift(own, 3)}
    twin_queries = shift(after(queries, own)[0], flip_core=True)
    qt, filled = scaled_queries(twin_queries, queries, cache_len)
    held = {(0, False, False): own}
    everything = dict(held)
    state = flash(held, filled, qt, None)

    across, state = after(across, state)
    far = {(1, True, False): shift(across, 1), (3, True, False): shift(across, 3)}
    opposite, state = after(opposite, state)
    far[2, True, False] = shift(opposite, flip_z=True)
    held = {(0, True, False): across, (2, False, False): opposite}
    everything.update(held)
    state = flash(held, filled, qt, state)

    beside, state = after(beside, state)
    everything.update(beside)
    state = flash(beside, filled, qt, state, fresh_rows(everything, len(beside)))

    far, state = after(far, state)
    everything.update(far)
    rows = new_rows(everything)
    twin_rows = shift(rows, flip_core=True)
    twin_part, own_part = flash_last(far, filled, qt, state, fresh_rows(far, len(far)))
    part = merge_pair(own_part, shift(twin_part, flip_core=True))
    parts = lax.all_to_all(part, "seg", 0, 0)
    cache_out = write_pages(cache_len, page_owner, cache_kv, rows, twin_rows)
    return merge(parts), cache_out


def solution(mesh):
    placed = (P("blk", None), P("blk", None), P(("seg", "blk"), None), P(), P())
    return jax.shard_map(
        on_device,
        mesh=mesh,
        in_specs=placed,
        out_specs=(P("blk", "seg"), P(("seg", "blk"), None)),
        check_vma=False,
    )
```
